32 devices in a mesh: dp: 8 (over z, x), fsdp: 4 (over y, core).
Axes of the slice: x: 2, y: 2, z: 4, core: 2. Of those that a mesh axis runs over, the one named last changes fastest.
Arguments:
- tokens: bfloat16 [32768, 768], P(('dp', 'fsdp')), may hold values from -6 to 6
- layout_cells: int32 [2, 32768], P(None, ('dp', 'fsdp')), may hold values from 0 to 31
- pad_mask: int32 [32768], P(('dp', 'fsdp')), may hold values from 0 to 1, as said below
- query_weight: bfloat16 [768, 768], P('fsdp'), may hold values from -0.21875 to 0.21875
- key_weight: bfloat16 [768, 768], P('fsdp'), may hold values from -0.21875 to 0.21875
- value_weight: bfloat16 [768, 768], P('fsdp'), may hold values from -0.21875 to 0.21875
- out_weight: bfloat16 [768, 768], P('fsdp'), may hold values from -0.875 to 0.875
- query_bias: bfloat16 [768], P('fsdp'), may hold values from -4 to 4
- value_bias: bfloat16 [768], P('fsdp'), may hold values from -4 to 4
- out_bias: bfloat16 [768], P('fsdp'), may hold values from -4 to 4
- bias_table: bfloat16 [12, 96], P('fsdp'), may hold values from -4 to 4
- first_gain: bfloat16 [768], P('fsdp'), may hold values from 0.25 to 1.75
- first_shift: bfloat16 [768], P('fsdp'), may hold values from -4 to 4
- up_weight: bfloat16 [768, 3072], P('fsdp'), may hold values from -0.21875 to 0.21875
- up_bias: bfloat16 [3072], P('fsdp'), may hold values from -4 to 4
- down_weight: bfloat16 [3072, 768], P('fsdp'), may hold values from -0.109375 to 0.109375
- down_bias: bfloat16 [768], P('fsdp'), may hold values from -4 to 4
- second_gain: bfloat16 [768], P('fsdp'), may hold values from 0.25 to 1.75
- second_shift: bfloat16 [768], P('fsdp'), may hold values from -4 to 4
- cotangent: bfloat16 [32768, 768], P(('dp', 'fsdp')), may hold values from -6 to 6
Outputs:
- output: bfloat16 [32768, 768], P(('dp', 'fsdp'))
- input_grad: bfloat16 [32768, 768], P(('dp', 'fsdp'))
- grad_query: float32 [768, 768], P('fsdp')
- grad_key: float32 [768, 768], P('fsdp')
- grad_value: float32 [768, 768], P('fsdp')
- grad_out: float32 [768, 768], P('fsdp')
- grad_query_bias: float32 [768], P('fsdp')
- grad_value_bias: float32 [768], P('fsdp')
- grad_out_bias: float32 [768], P('fsdp')
- grad_table: float32 [12, 96], P('fsdp')
- grad_first_gain: float32 [768], P('fsdp')
- grad_first_shift: float32 [768], P('fsdp')
- grad_up: float32 [768, 3072], P('fsdp')
- grad_up_bias: float32 [3072], P('fsdp')
- grad_down: float32 [3072, 768], P('fsdp')
- grad_down_bias: float32 [768], P('fsdp')
- grad_second_gain: float32 [768], P('fsdp')
- grad_second_shift: float32 [768], P('fsdp')
The draws below stay inside these ranges and needn't reach their ends.
Inputs may be any that keep to these rules, and one draw needn't show every extreme that they name: `pad_mask`: within each window of 512 consecutive tokens the ones form a prefix of one token or more; some windows are all ones.
All inputs are finite; a program needn't handle non-finite values.
Results may differ from the reference program's by a relative error of at most 0.017.
Values may be sent and summed in bfloat16 or wider, within the bound.
No kernel may reach another device: no remote copies, remote signals or barrier semaphores. Data moves between devices by JAX's collectives and lax.ppermute only.
A program may use at most 256 MiB of HBM per device.

```python
import math
from functools import partial
import jax
import jax.numpy as jnp
from jax import lax

D = 768
HEADS = 12
HD = 64
FF = 3072
WIN = 512
BUCKETS = 32
TOKENS = 32768


def draw_pad_mask(key, part):
    key = jax.random.fold_in(key, 11)
    first, second = jax.random.split(key)
    windows = TOKENS // WIN
    whole = jax.random.randint(first, (windows,), 0, 5) < 3
    short_len = jax.random.randint(second, (windows,), 1, WIN)
    length = jnp.where(whole, WIN, short_len)
    places = jnp.arange(WIN, dtype=jnp.int32)
    return (places[None, :] < length[:, None]).astype(jnp.int32).reshape(TOKENS)


def with_ends(drawn, key, least, largest):
    place = [jax.random.randint(jax.random.fold_in(key, axis), (), 0, length) for axis, length in enumerate(drawn.shape)]
    longest = drawn.shape.index(max(drawn.shape))
    beside = place[:longest] + [(place[longest] + 1) % drawn.shape[longest]] + place[longest + 1:]
    return drawn.at[tuple(place)].set(least).at[tuple(beside)].set(largest)


def level_of(rng, dims, cuts, least, largest):
    def one(axis_at, parts):
        steps = jax.random.uniform(jax.random.fold_in(jax.random.fold_in(rng, 6), axis_at), (parts,), jnp.float32, least / len(cuts), largest / len(cuts))
        return jnp.repeat(jnp.exp(steps), dims[axis_at] // parts).reshape((-1,) + (1,) * (len(dims) - axis_at - 1))

    factor_of = one(*cuts[0])
    for cut in cuts[1:]:
        factor_of = factor_of * one(*cut)
    return factor_of


def bell_draw(stream_key, extent, scale, reach, shards=(), held_as=jnp.bfloat16):
    drawn = jax.random.normal(stream_key, extent, jnp.float32) * scale
    if len(shards) > 0:
        drawn = level_of(stream_key, extent, shards, -0.22, 0.18) * drawn
    return jnp.clip(drawn, min=-reach, max=reach).astype(held_as)


def setup_inputs(seed: int = 0) -> dict:
    keys = jax.random.split(jax.random.key(seed), 21)
    return {
        "tokens": bell_draw(keys[0], (TOKENS, D), 1.0, 6.0, ((0, 32),)),
        "layout_cells": with_ends(jax.random.randint(keys[1], (2, TOKENS), 0, BUCKETS), jax.random.fold_in(keys[1], 1), 0, BUCKETS - 1).astype(jnp.int32),
        "pad_mask": draw_pad_mask(jax.random.fold_in(keys[20], 71), 0),
        "query_weight": bell_draw(keys[3], (D, D), D ** -0.5, 0.21875, ((0, 4),)),
        "key_weight": bell_draw(keys[4], (D, D), D ** -0.5, 0.21875, ((0, 4),)),
        "value_weight": bell_draw(keys[5], (D, D), D ** -0.5, 0.21875, ((0, 4),)),
        "out_weight": bell_draw(keys[6], (D, D), (D // 16) ** -0.5, 0.875, ((0, 4),)),
        "query_bias": bell_draw(keys[7], (D,), 0.3, 4.0, ((0, 4),)),
        "value_bias": bell_draw(keys[8], (D,), 0.3, 4.0, ((0, 4),)),
        "out_bias": bell_draw(keys[9], (D,), 0.3, 4.0, ((0, 4),)),
        "bias_table": bell_draw(keys[10], (HEADS, 3 * BUCKETS), 0.7, 4.0, ((0, 4),)),
        "first_gain": jnp.clip(1.0 + 0.15 * jax.random.normal(keys[11], (D,), jnp.float32), 0.25, 1.75).astype(jnp.bfloat16),
        "first_shift": bell_draw(keys[12], (D,), 0.3, 4.0, ((0, 4),)),
        "up_weight": bell_draw(keys[13], (D, FF), D ** -0.5, 0.21875, ((0, 4),)),
        "up_bias": bell_draw(keys[14], (FF,), 0.3, 4.0, ((0, 4),)),
        "down_weight": bell_draw(keys[15], (FF, D), FF ** -0.5, 0.109375, ((0, 4),)),
        "down_bias": bell_draw(keys[16], (D,), 0.3, 4.0, ((0, 4),)),
        "second_gain": jnp.clip(1.0 + 0.15 * jax.random.normal(keys[17], (D,), jnp.float32), 0.25, 1.75).astype(jnp.bfloat16),
        "second_shift": bell_draw(keys[18], (D,), 0.3, 4.0, ((0, 4),)),
        "cotangent": bell_draw(keys[19], (TOKENS, D), 1.0, 6.0, ((0, 32),)),
    }


@jax.custom_vjp
def low(v):
    return lax.optimization_barrier(v.astype(jnp.bfloat16)).astype(jnp.float32)

@jax.custom_vjp
def low_back(v):
    return v

def low_keep(v):
    return (low(v), None)

def low_pass(kept, grad):
    return (grad,)

def back_keep(v):
    return (v, None)

def back_low(kept, grad):
    return (low(grad),)
low.defvjp(low_keep, low_pass)
low_back.defvjp(back_keep, back_low)

def matmul(left, right):
    return jnp.dot(left, right, precision=lax.Precision.HIGHEST)

def layer_norm(hidden, gain, shift):
    centre = hidden - lax.optimization_barrier(jnp.mean(hidden, axis=-1, keepdims=True))
    spread = lax.optimization_barrier(jnp.mean(centre * centre, axis=-1, keepdims=True))
    return centre * lax.rsqrt(spread + 1e-05) * gain + shift

def gelu_exact(values):
    return jax.nn.gelu(values, approximate=False)

def bucket_onehot(cell_x, cell_y):
    places = jnp.arange(WIN, dtype=jnp.int32)
    half_span = BUCKETS // 2
    labels = jnp.arange(BUCKETS, dtype=jnp.int32)
    tables = []
    for coords in (places, cell_x, cell_y):
        relative = jnp.clip(coords[None, :] - coords[:, None], -half_span, half_span - 1) + half_span
        tables.append(relative.reshape(1, -1) == labels[:, None])
    return jnp.concatenate(tables, axis=0)

def window_mix(table, pieces):
    query_win, key_win, value_win, cell_x, cell_y, valid_win = pieces
    onehot = bucket_onehot(cell_x, cell_y).astype(jnp.float32)
    rel_bias = matmul(table, onehot).reshape(HEADS, WIN, WIN)
    raw_scores = jnp.einsum('qhd,khd->hqk', query_win, key_win, precision=lax.Precision.HIGHEST) * HD ** (-0.5) + rel_bias
    scores = jnp.where(valid_win[None, None, :], low_back(raw_scores), -1e+30)
    probability = jax.nn.softmax(scores, axis=-1)
    mixed = jnp.einsum('hqk,khd->qhd', low(probability), value_win, precision=lax.Precision.HIGHEST)
    return low(low_back(mixed))

def layer(x_rows, cell_rows, mask_rows, query_weight, key_weight, value_weight, out_weight, query_bias, value_bias, out_bias, bias_table, first_gain, first_shift, up_weight, up_bias, down_weight, down_bias, second_gain, second_shift):
    windows = x_rows.shape[0] // WIN
    queries = low(low_back(matmul(x_rows, query_weight) + query_bias))
    key_rows = low(low_back(matmul(x_rows, key_weight)))
    value_rows = low(low_back(matmul(x_rows, value_weight) + value_bias))

    def to_windows(array):
        return array.reshape(windows, WIN, HEADS, HD)
    cells_x = cell_rows[0].reshape(windows, WIN)
    cells_y = cell_rows[1].reshape(windows, WIN)
    valid_keys = mask_rows.reshape(windows, WIN) > 0
    mixed = lax.map(jax.checkpoint(partial(window_mix, bias_table)), (to_windows(queries), to_windows(key_rows), to_windows(value_rows), cells_x, cells_y, valid_keys))
    mixed = mixed.reshape(x_rows.shape[0], D)
    attended = low_back(matmul(mixed, out_weight) + out_bias)
    normed = layer_norm(x_rows + attended, first_gain, first_shift)
    hidden = low_back(matmul(low(normed), up_weight) + up_bias)
    active = low(gelu_exact(hidden))
    branch = low_back(matmul(active, down_weight) + down_bias)
    return layer_norm(normed + branch, second_gain, second_shift)

def reference(tokens, layout_cells, pad_mask, query_weight, key_weight, value_weight, out_weight, query_bias, value_bias, out_bias, bias_table, first_gain, first_shift, up_weight, up_bias, down_weight, down_bias, second_gain, second_shift, cotangent):
    params = tuple((weight.astype(jnp.float32) for weight in (query_weight, key_weight, value_weight, out_weight, query_bias, value_bias, out_bias, bias_table, first_gain, first_shift, up_weight, up_bias, down_weight, down_bias, second_gain, second_shift)))
    windows = TOKENS // WIN
    group = 8 if windows % 8 == 0 else 1
    steps = windows // group
    row_count = group * WIN
    inputs = tokens.astype(jnp.float32).reshape(steps, row_count, D)
    cells = jnp.transpose(layout_cells.reshape(2, steps, row_count), (1, 0, 2))
    masks = pad_mask.reshape(steps, row_count)
    cotangents = cotangent.astype(jnp.float32).reshape(steps, row_count, D)

    def one_group(carry, pieces):
        x_rows, cell_rows, mask_rows, cot_rows = pieces

        def forward(inner_rows, *weights):
            return layer(inner_rows, cell_rows, mask_rows, *weights)
        result, pull = jax.vjp(forward, x_rows, *params)
        grads = pull(cot_rows)
        updated = tuple((total + gradient for total, gradient in zip(carry, grads[1:])))
        return (updated, (result.astype(jnp.bfloat16), grads[0].astype(jnp.bfloat16)))
    start = tuple((jnp.zeros_like(weight) for weight in params))
    totals, (results, input_grads) = lax.scan(one_group, start, (inputs, cells, masks, cotangents))
    factor = 1.0 / math.sqrt(TOKENS)
    return (results.reshape(TOKENS, D), input_grads.reshape(TOKENS, D), totals[0] * factor, totals[1] * factor, totals[2] * factor, totals[3] * factor, totals[4] * factor, totals[5] * factor, totals[6] * factor, totals[7] * factor, totals[8] * factor, totals[9] * factor, totals[10] * factor, totals[11] * factor, totals[12] * factor, totals[13] * factor, totals[14] * factor, totals[15] * factor)
```

```python
import functools
import math

import jax
import jax.numpy as jnp
import numpy as np
from jax import lax
from jax.experimental import pallas as pl
from jax.experimental.pallas import tpu as pltpu
from jax.sharding import PartitionSpec as P

HEADS = 12
HD = 64
WIN = 512
BUCKETS = 32
PAIRS = HEADS // 2
SCALE = HD ** (-0.5)
EPS = 1e-05
BF = jnp.bfloat16
F32 = jnp.float32
VMEM_LIMIT = 60 * 1024 * 1024
GROUPS = ((0, 2), (2, 2), (4, 2))


def params():
    return pltpu.CompilerParams(vmem_limit_bytes=VMEM_LIMIT)


def cost(flops, nbytes, transcendentals=0):
    return pl.CostEstimate(
        flops=int(flops), bytes_accessed=int(nbytes), transcendentals=int(transcendentals)
    )


def struct(shape, dtype):
    return jax.ShapeDtypeStruct(shape, dtype)


def dot(left, right):
    return lax.dot_general(left, right, (((1,), (0,)), ((), ())), preferred_element_type=F32)


def dot_t(left, right):
    return lax.dot_general(left, right, (((1,), (1,)), ((), ())), preferred_element_type=F32)


def tdot(left, right):
    return lax.dot_general(left, right, (((0,), (0,)), ((), ())), preferred_element_type=F32)


def split3(values):
    high = values.astype(BF)
    rest = values - high.astype(F32)
    middle = rest.astype(BF)
    return high, middle, (rest - middle.astype(F32)).astype(BF)


def swap(array, axis, bit):
    return lax.ppermute(array, axis, [(i, i ^ bit) for i in range(lax.axis_size(axis))])


def half_of(array, which, axis=0):
    rows = array.shape[axis] // 2
    return lax.dynamic_slice_in_dim(array, which * rows, rows, axis)


def gather(shard, parity):
    far = swap(half_of(shard, parity), "fsdp", 2)
    beside = swap(far, "dp", 1)
    return (
        shard,
        swap(shard, "fsdp", 1),
        far,
        beside,
        swap(far, "fsdp", 1),
        swap(beside, "fsdp", 1),
    )


def part_rows(index, rows):
    me, parity = index[0], index[1]
    half = rows // 2
    return (
        (me * rows, rows),
        ((me ^ 1) * rows, rows),
        ((me ^ 2) * rows + parity * half, half),
        ((me ^ 2) * rows + (1 - parity) * half, half),
        ((me ^ 3) * rows + parity * half, half),
        ((me ^ 3) * rows + (1 - parity) * half, half),
    )


PARTS = 6


def fetch_copies(index, parts, whole, sems):
    rows = whole.shape[0] // 4
    return [
        pltpu.make_async_copy(part, whole.at[pl.ds(pl.multiple_of(first, 16), count)], sems.at[at])
        for at, (part, (first, count)) in enumerate(zip(parts, part_rows(index, rows)))
    ]


ANY = pl.BlockSpec(memory_space=pl.ANY)
SMEM = pl.BlockSpec(memory_space=pltpu.SMEM)


def reduce_rows(keep, send, factor):
    place = lax.axis_index("dp")
    near, beside = place & 1, (place >> 1) & 1
    got = swap(send, "fsdp", 1)
    far = swap((keep[1].astype(F32) + got[1].astype(F32)).astype(BF), "fsdp", 2)

    def part(which, arrays):
        return sum(half_of(a, which).astype(F32) for a in arrays).astype(BF)

    terms = (keep[0], got[0], far)
    terms = (part(near, terms), swap(part(1 - near, terms), "dp", 1))
    other = swap(part(1 - beside, terms), "dp", 2)
    total = (part(beside, terms).astype(F32) + other.astype(F32)).astype(BF)
    bit = 4
    while bit < lax.axis_size("dp"):
        total = (total.astype(F32) + swap(total, "dp", bit).astype(F32)).astype(BF)
        bit *= 2
    other = swap(total, "dp", 2)
    total = in_order(total, other, beside)
    other = swap(total, "dp", 1)
    return in_order(total, other, near).astype(F32) * factor


def in_order(mine, other, which):
    return jnp.where(
        which == 0, jnp.concatenate([mine, other]), jnp.concatenate([other, mine])
    )


def table_places():
    span = np.arange(128)
    step = np.where(span < 64, span, span - 128)
    near = np.clip(step, -16, 15) + 16
    far = np.where(step <= -2, 0, np.where(step >= 2, 31, -1))
    wide = np.arange(256)
    wide = np.where(wide < 128, wide, wide - 256)
    return np.concatenate(
        [
            near + 32,
            near + 64,
            far,
            np.clip(wide, -16, 15) + 16,
            np.clip(-wide, -16, 15) + 16,
        ]
    ).astype(np.int32)


LANES = 896


def iota(shape, axis):
    return lax.broadcasted_iota(jnp.int32, shape, axis)


def as_bf(mask):
    return jnp.where(mask, 1.0, 0.0).astype(BF)


def near_tile(row):
    rolled = pltpu.roll(jnp.broadcast_to(row, (128, 256)), 0, 1, stride=1, stride_axis=0)
    r, c = iota((128, 256), 0), iota((128, 256), 1)
    gap = (r >> 4) - (c >> 4)
    inside = (c < 128) & (gap <= 1) & (gap >= -1)
    corner = ((r >= 112) & (c >= 128) & (c < 144)) | ((r < 16) & (c >= 240))
    return jnp.where(inside | corner, rolled, 0.0)


def prep_kernel(cols_ref, rows_ref, lanes_ref, e_ref, ke_ref, ket_ref, oh_ref, d_ref, dt_ref, own):
    tokens = cols_ref.shape[0]

    @pl.when(pl.program_id(0) == 0)
    def _():
        x, y, valid = cols_ref[:, 0:1], cols_ref[:, 1:2], cols_ref[:, 2:3]
        lane = iota((tokens, 128), 1)
        block = (iota((tokens, 128), 0) & (WIN - 1)) >> 4
        third = lane >> 5
        hot = jnp.where(third == 0, x, jnp.where(third == 1, y + 32, block + 64)) == lane
        hot = hot & (lane < 96)
        own[...] = as_bf(hot | (lane == 96))
        back = jnp.where(third == 0, 31 - x, jnp.where(third == 1, 63 - y, 95 - block)) == lane
        oh_ref[...] = as_bf(back & (lane < 96))
        masked = jnp.where((lane == 99) & (valid <= 0), -1e30, 0.0)
        ones = hot | ((lane >= 96) & (lane < 99))
        ke_ref[...] = jnp.where(ones, 1.0, masked).astype(BF)
        x, y, valid = rows_ref[0:1, :], rows_ref[1:2, :], rows_ref[2:3, :]
        lane = iota((128, tokens), 0)
        block = (iota((128, tokens), 1) & (WIN - 1)) >> 4
        third = lane >> 5
        hot = jnp.where(third == 0, x, jnp.where(third == 1, y + 32, block + 64)) == lane
        hot = hot & (lane < 96)
        masked = jnp.where((lane == 99) & (valid <= 0), -1e30, 0.0)
        ones = hot | ((lane >= 96) & (lane < 99))
        ket_ref[...] = jnp.where(ones, 1.0, masked).astype(BF)

    row = lanes_ref[0]
    lane = iota((32, 128), 1)
    blocks = []
    for at in range(3):
        spread = jnp.broadcast_to(row[:, at * 128 : at * 128 + 128], (32, 128))
        spread = pltpu.roll(spread, at * 32, 1, stride=1, stride_axis=0)
        blocks.append(jnp.where(lane >> 5 == at, spread, 0.0))
    blocks.append(jnp.where((iota((32, 128), 0) == 0) & (lane == 99), 1.0, 0.0))
    e_ref[...] = dot(own[...], jnp.concatenate(blocks, axis=0).astype(BF)).astype(BF)
    d_ref[0] = near_tile(row[:, 384:640])
    dt_ref[0] = near_tile(row[:, 640:896])


def prepare(layout_cells, pad_mask, table):
    tokens = pad_mask.shape[0]
    rows = jnp.concatenate([layout_cells, pad_mask[None], jnp.zeros_like(layout_cells)[:1]])
    places = jnp.asarray(table_places())
    pick = (jnp.arange(96, dtype=jnp.int32)[:, None] == places[None, :]).astype(BF)
    lanes = jnp.dot(table, pick, preferred_element_type=F32).reshape(HEADS, 1, LANES)
    whole = lambda h: (0, 0)
    return pl.pallas_call(
        prep_kernel,
        grid=(HEADS,),
        in_specs=[
            pl.BlockSpec((tokens, 4), whole),
            pl.BlockSpec((4, tokens), whole),
            pl.BlockSpec((1, 1, LANES), lambda h: (h, 0, 0)),
        ],
        out_specs=[
            pl.BlockSpec((tokens, 128), lambda h: (0, h)),
            pl.BlockSpec((tokens, 128), whole),
            pl.BlockSpec((128, tokens), whole),
            pl.BlockSpec((tokens, 128), whole),
            pl.BlockSpec((1, 128, 256), lambda h: (h, 0, 0)),
            pl.BlockSpec((1, 128, 256), lambda h: (h, 0, 0)),
        ],
        out_shape=[
            struct((tokens, HEADS * 128), BF),
            struct((tokens, 128), BF),
            struct((128, tokens), BF),
            struct((tokens, 128), BF),
            struct((HEADS, 128, 256), F32),
            struct((HEADS, 128, 256), F32),
        ],
        scratch_shapes=[pltpu.VMEM((tokens, 128), BF)],
        compiler_params=params(),
        cost_estimate=cost(2 * tokens * 128 * 128 * HEADS, 7e6),
        name="prepare",
    )(rows.T, rows, lanes)


def project_kernel(index, *refs):
    parts, (x_ref, bias_ref, out_ref, weight, sems) = refs[:PARTS], refs[PARTS:]

    @pl.when(pl.program_id(0) == 0)
    def _():
        copies = fetch_copies(index, parts, weight, sems)
        for copy in copies:
            copy.start()
        for copy in copies:
            copy.wait()

    width = out_ref.shape[1] // 3
    for at in range(3):
        span = slice(at * width, (at + 1) * width)
        values = dot(x_ref[...], weight[:, span])
        if at == 0:
            values = (values + bias_ref[0:1, :]).astype(BF) * SCALE
        if at == 2:
            values = values + bias_ref[1:2, :]
        out_ref[:, span] = values.astype(BF)


def project(index, parts, tokens, biases, block=256):
    rows, width = tokens.shape
    return pl.pallas_call(
        project_kernel,
        grid=(rows // block,),
        in_specs=[SMEM]
        + [ANY] * PARTS
        + [
            pl.BlockSpec((block, width), lambda i: (i, 0)),
            pl.BlockSpec((2, width), lambda i: (0, 0)),
        ],
        out_specs=pl.BlockSpec((block, 3 * width), lambda i: (i, 0)),
        out_shape=struct((rows, 3 * width), BF),
        scratch_shapes=[pltpu.VMEM((width, 3 * width), BF), pltpu.SemaphoreType.DMA((PARTS,))],
        compiler_params=params(),
        cost_estimate=cost(6 * rows * width * width, 10e6),
        name="project",
    )(index, *parts, tokens, biases)


def input_kernel(index, *refs):
    count = len(GROUPS) * 3
    parts, grads = refs[:PARTS], refs[PARTS : PARTS + count]
    dresid_ref, out_ref, weight, sems = refs[PARTS + count :]

    @pl.when(pl.program_id(0) == 0)
    def _():
        copies = fetch_copies(index, parts, weight, sems)
        for copy in copies:
            copy.start()
        for copy in copies:
            copy.wait()

    joined = jnp.concatenate(
        [grads[3 * group + at][...] for at in range(3) for group in range(len(GROUPS))], axis=1
    )
    out_ref[...] = (dresid_ref[...] + dot_t(joined, weight[...])).astype(BF)


def input_gradient(index, parts, grads, dresid, block=256):
    rows, width = dresid.shape
    spec = lambda a: pl.BlockSpec((block, a.shape[1]), lambda i: (i, 0))
    return pl.pallas_call(
        input_kernel,
        grid=(rows // block,),
        in_specs=[SMEM] + [ANY] * PARTS + [spec(a) for a in grads] + [spec(dresid)],
        out_specs=spec(dresid),
        out_shape=struct((rows, width), BF),
        scratch_shapes=[pltpu.VMEM((width, 3 * width), BF), pltpu.SemaphoreType.DMA((PARTS,))],
        compiler_params=params(),
        cost_estimate=cost(6 * rows * width * width, 13e6),
        name="input_gradient",
    )(index, *parts, *grads, dresid)


def with_near(pieces, tile, at):
    pieces = list(pieces)
    pieces[at] = pieces[at] + tile[:, :128]
    if at > 0:
        left = pieces[at - 1]
        pieces[at - 1] = jnp.concatenate([left[:16] + tile[:16, 128:], left[16:]], axis=0)
    if at < 3:
        right = pieces[at + 1]
        pieces[at + 1] = jnp.concatenate([right[:112], right[112:] + tile[112:, 128:]], axis=0)
    return pieces


def lane_blocks(values):
    return [values[:, c * 128 : c * 128 + 128] for c in range(WIN // 128)]


def attend_kernel(q_ref, k_ref, v_ref, e_ref, ket_ref, d_ref, out_ref, eout_ref):
    first = iota((WIN, 128), 1) < HD
    keys = jnp.concatenate([k_ref[...].T, ket_ref[...]], axis=0)
    mixed = []
    for head in range(2):
        mine = first if head == 0 else ~first
        span = slice(head * 128, head * 128 + 128)
        extra = e_ref[:, span]
        query = jnp.concatenate([jnp.where(mine, q_ref[...], jnp.zeros((), BF)), extra], axis=1)
        tile = d_ref[head]
        rows, logs = [], []
        for at in range(WIN // 128):
            scores = dot(query[at * 128 : at * 128 + 128], keys)
            pieces = with_near(lane_blocks(scores), tile, at)
            top = jnp.maximum(
                jnp.maximum(pieces[0], pieces[1]), jnp.maximum(pieces[2], pieces[3])
            )
            top = jnp.max(top, axis=1, keepdims=True)
            pieces = [jnp.exp(piece - top) for piece in pieces]
            total = jnp.sum(
                (pieces[0] + pieces[1]) + (pieces[2] + pieces[3]), axis=1, keepdims=True
            )
            weights = jnp.concatenate([piece.astype(BF) for piece in pieces], axis=1)
            rows.append(dot(weights, v_ref[...]) / total)
            logs.append(top + jnp.log(total))
        mixed.append(jnp.concatenate(rows, axis=0))
        lane = iota((WIN, 128), 1)
        parts = split3(-jnp.concatenate(logs, axis=0))
        for at in range(3):
            extra = jnp.where(lane == 96 + at, parts[at], extra)
        eout_ref[:, span] = extra
    out_ref[...] = jnp.where(first, mixed[0], mixed[1]).astype(BF)


def attend(qkv, extra, ket, near):
    tokens = qkv.shape[0]
    windows = tokens // WIN
    head_block = lambda shift: pl.BlockSpec((WIN, 128), lambda p, w: (w, p + shift))
    wide = pl.BlockSpec((WIN, 256), lambda p, w: (w, p))
    return pl.pallas_call(
        attend_kernel,
        grid=(PAIRS, windows),
        in_specs=[
            head_block(0),
            head_block(PAIRS),
            head_block(2 * PAIRS),
            wide,
            pl.BlockSpec((128, WIN), lambda p, w: (0, w)),
            pl.BlockSpec((2, 128, 256), lambda p, w: (p, 0, 0)),
        ],
        out_specs=[pl.BlockSpec((WIN, 128), lambda p, w: (w, p)), wide],
        out_shape=[struct((tokens, PAIRS * 128), BF), struct((tokens, HEADS * 128), BF)],
        compiler_params=params(),
        cost_estimate=cost(tokens * WIN * HEADS * 768, 17e6, tokens * WIN * HEADS),
        name="attend",
    )(qkv, qkv, qkv, extra, ket, near)


def diagonal_rows(sums):
    lane = iota((32, 128), 1)
    rows = []
    for at in range(3):
        block = jnp.where(lane >> 5 == at, sums[at * 32 : at * 32 + 32], 0.0)
        rolled = pltpu.roll(block, 0, 1, stride=1, stride_axis=0)
        rows.append(jnp.sum(rolled, axis=0, keepdims=True))
    return rows


def near_rows(tile):
    r, c = iota((128, 256), 0), iota((128, 256), 1)
    gap = (r >> 4) - (c >> 4)
    inside = (c < 128) & (gap <= 1) & (gap >= -1)
    corner = ((r >= 112) & (c >= 128) & (c < 144)) | ((r < 16) & (c >= 240))
    tile = jnp.where(inside | corner, tile, 0.0)
    turn = as_bf(iota((128, 128), 0) + iota((128, 128), 1) == 127)
    high, middle, low = split3(tile)
    turned = dot(turn, high) + dot(turn, middle) + dot(turn, low)
    rolled = pltpu.roll(turned, 0, 1, stride=1, stride_axis=0)
    return jnp.sum(rolled, axis=0, keepdims=True)


def attend_back_kernel(
    q_ref, k_ref, v_ref, e_ref, ke_ref, ket_ref, oh_ref, dt_ref, do_ref, o_ref,
    dq_ref, dk_ref, dv_ref, far_ref, near_ref,
    p_scr, ds_scr, sums, tiles,
):
    window = pl.program_id(1)
    zero = jnp.zeros((), BF)
    first = iota((WIN, 128), 1) < HD
    lane = iota((WIN, 128), 1)
    keys = jnp.concatenate([k_ref[...], ke_ref[...]], axis=1)
    values = jnp.concatenate([v_ref[...], ke_ref[...]], axis=1)
    keys_t = k_ref[...].T
    product = do_ref[...].astype(F32) * o_ref[...].astype(F32)
    dq_t, dk, dv = [], None, None
    for head in range(2):
        mine = first if head == 0 else ~first
        query = jnp.where(mine, q_ref[...], zero)
        grad = jnp.where(mine, do_ref[...], zero)
        delta = -jnp.sum(jnp.where(mine, product, 0.0), axis=1, keepdims=True)
        parts = split3(delta)
        minus = jnp.zeros((WIN, 128), BF)
        for at in range(3):
            minus = jnp.where(lane == 96 + at, parts[at], minus)
        query_all = jnp.concatenate([query, e_ref[:, head * 128 : head * 128 + 128]], axis=1)
        grad_all = jnp.concatenate([grad, minus], axis=1)
        tile = dt_ref[head]
        diag, low, high = None, None, None
        for at in range(WIN // 128):
            rows = slice(at * 128, at * 128 + 128)
            scores = with_near(lane_blocks(dot_t(keys[rows], query_all)), tile, at)
            probs = [jnp.exp(piece) for piece in scores]
            dprobs = lane_blocks(dot_t(values[rows], grad_all))
            dscores = [a * b for a, b in zip(probs, dprobs)]
            p_scr[rows] = jnp.concatenate([a.astype(BF) for a in probs], axis=1)
            ds_scr[rows] = jnp.concatenate([a.astype(BF) for a in dscores], axis=1)
            add = lambda total, term: term if total is None else total + term
            diag = add(diag, dscores[at])
            if at > 0:
                low = add(low, dscores[at - 1][:16])
            if at < 3:
                high = add(high, dscores[at + 1][112:])
        dscores = ds_scr[...]
        dv_head = dot(p_scr[...], grad)
        dk_head = dot(dscores, query)
        dv = dv_head if dv is None else dv + dv_head
        dk = dk_head if dk is None else dk + dk_head
        left = jnp.concatenate([keys_t[head * HD : head * HD + HD], ket_ref[:96]], axis=0)
        both = dot(left, dscores)
        dq_t.append(both[:HD] * SCALE)
        extra = both[HD:]
        extra_high = extra.astype(BF)
        extra_low = (extra - extra_high.astype(F32)).astype(BF)
        far = dot(extra_high, oh_ref[...]) + dot(extra_low, oh_ref[...])

        @pl.when(window == 0)
        def _():
            sums[head] = far
            tiles[head] = jnp.zeros((128, 256), F32)

        @pl.when(window > 0)
        def _():
            sums[head] = sums[head] + far

        tiles[head, :, :128] = tiles[head, :, :128] + diag
        tiles[head, :16, 128:] = tiles[head, :16, 128:] + low
        tiles[head, 112:, 128:] = tiles[head, 112:, 128:] + high
    dq_ref[...] = jnp.concatenate(dq_t, axis=0).T.astype(BF)
    dk_ref[...] = dk.astype(BF)
    dv_ref[...] = dv.astype(BF)

    @pl.when(window == pl.num_programs(1) - 1)
    def _():
        for head in range(2):
            rows = diagonal_rows(sums[head])
            far_ref[head] = jnp.concatenate(rows + [jnp.zeros((5, 128), F32)], axis=0)
            near_ref[head] = jnp.broadcast_to(near_rows(tiles[head]), (8, 256))


def attend_back(group, qkv, extra, ke, ket, oh, near_t, dmixed, mixed):
    start, pairs = group
    tokens = qkv.shape[0]
    windows = tokens // WIN
    block = lambda shift: pl.BlockSpec((WIN, 128), lambda p, w: (w, p + start + shift))
    per_window = pl.BlockSpec((WIN, 128), lambda p, w: (w, 0))
    out = pl.BlockSpec((WIN, 128), lambda p, w: (w, p))
    out_rows = struct((tokens, pairs * 128), BF)
    return pl.pallas_call(
        attend_back_kernel,
        grid=(pairs, windows),
        in_specs=[
            block(0),
            block(PAIRS),
            block(2 * PAIRS),
            pl.BlockSpec((WIN, 256), lambda p, w: (w, p + start)),
            per_window,
            pl.BlockSpec((128, WIN), lambda p, w: (0, w)),
            per_window,
            pl.BlockSpec((2, 128, 256), lambda p, w: (p + start, 0, 0)),
            block(0),
            block(0),
        ],
        out_specs=[
            out,
            out,
            out,
            pl.BlockSpec((2, 8, 128), lambda p, w: (p, 0, 0)),
            pl.BlockSpec((2, 8, 256), lambda p, w: (p, 0, 0)),
        ],
        out_shape=[
            out_rows,
            out_rows,
            out_rows,
            struct((2 * pairs, 8, 128), F32),
            struct((2 * pairs, 8, 256), F32),
        ],
        scratch_shapes=[
            pltpu.VMEM((WIN, WIN), BF),
            pltpu.VMEM((WIN, WIN), BF),
            pltpu.VMEM((2, 96, 128), F32),
            pltpu.VMEM((2, 128, 256), F32),
        ],
        compiler_params=params(),
        cost_estimate=cost(
            tokens * WIN * pairs * 2 * 2048, 12e6, tokens * WIN * pairs * 2
        ),
        name="attend_back",
    )(qkv, qkv, qkv, extra, ke, ket, oh, near_t, dmixed, mixed)


def table_gradient(far, near):
    lane = np.arange(128)
    entry = np.clip(lane - 31, -16, 15) + 16
    x_place = np.where(lane < 63, entry + 32, -1)
    y_place = np.where((lane >= 32) & (lane < 95), np.clip(lane - 63, -16, 15) + 16 + 64, -1)
    block_step = lane - 95
    blk_place = np.where(
        (lane >= 64) & (block_step <= -2), 0, np.where((lane < 127) & (block_step >= 2), 31, -1)
    )
    wide = np.arange(256)
    step = (127 - wide + 128) % 256 - 128
    near_place = np.clip(step, -16, 15) + 16
    places = np.concatenate([x_place, y_place, blk_place, near_place]).astype(np.int32)
    sums = jnp.concatenate([far[:, 0], far[:, 1], far[:, 2], near[:, 0]], axis=1)
    pick = (jnp.asarray(places)[:, None] == jnp.arange(96, dtype=jnp.int32)[None, :]).astype(F32)
    return jnp.dot(sums, pick, precision=lax.Precision.HIGHEST, preferred_element_type=F32)


def norm_parts(values):
    centre = values - jnp.mean(values, axis=-1, keepdims=True)
    spread = jnp.mean(centre * centre, axis=-1, keepdims=True)
    scale = lax.rsqrt(spread + EPS)
    return centre * scale, scale


def norm_back(grad, hat, scale):
    mean = jnp.mean(grad, axis=-1, keepdims=True)
    along = jnp.mean(grad * hat, axis=-1, keepdims=True)
    return scale * (grad - mean - hat * along)


def add_rows(ref, rows):
    for at, values in enumerate(rows):
        ref[at : at + 1, :] += jnp.sum(values.astype(F32), axis=0, keepdims=True)


def start_copies(copies):
    for copy in copies:
        copy.start()


def wait_copies(copies):
    for copy in copies:
        copy.wait()


def forward_kernel(index, *refs):
    parts = [refs[at * PARTS : at * PARTS + PARTS] for at in range(3)]
    (
        mixed_ref, x_ref, cot_ref, small_ref, up_bias_ref,
        out_ref, dfinal_ref, dbranch_ref, active_ref, slope_ref, normed_ref, resid_ref, sums_ref,
        w_out, w_up, w_down, sems,
    ) = refs[3 * PARTS :]
    step = pl.program_id(0)
    weights = (w_out, w_up, w_down)
    copies = [fetch_copies(index, parts[at], weights[at], sems.at[at]) for at in range(3)]

    @pl.when(step == 0)
    def _():
        sums_ref[...] = jnp.zeros_like(sums_ref)
        for group in copies:
            start_copies(group)
        wait_copies(copies[0])

    small = lambda at: small_ref[at : at + 1, :]
    attended = dot(mixed_ref[...], w_out[...]) + small(0)
    resid = x_ref[...].astype(F32) + attended
    resid_ref[...] = resid
    hat, _ = norm_parts(resid)
    normed = hat * small(1) + small(2)
    low = normed.astype(BF)
    normed_ref[...] = low

    @pl.when(step == 0)
    def _():
        wait_copies(copies[1])
        wait_copies(copies[2])

    width = w_down.shape[1]
    branch = None
    for at in range(w_up.shape[1] // width):
        span = slice(at * width, at * width + width)
        hidden = dot(low, w_up[:, span]) + up_bias_ref[:, span]
        upto = 0.5 + 0.5 * lax.erf(hidden * math.sqrt(0.5))
        density = jnp.exp(hidden * hidden * -0.5) * (1.0 / math.sqrt(2.0 * math.pi))
        slope_ref[:, span] = (upto + hidden * density).astype(BF)
        active = (hidden * upto).astype(BF)
        active_ref[:, span] = active
        term = dot(active, w_down[span, :])
        branch = term if branch is None else branch + term
    final = normed + branch + small(3)
    hat, scale = norm_parts(final)
    out_ref[...] = (hat * small(4) + small(5)).astype(BF)
    cot = cot_ref[...].astype(F32)
    dfinal = norm_back(cot * small(4), hat, scale)
    dfinal_ref[...] = dfinal
    dbranch = dfinal.astype(BF)
    dbranch_ref[...] = dbranch
    add_rows(sums_ref, (cot * hat, cot, dbranch))


def forward(index, parts, mixed, tokens, cotangent, smalls, up_bias, block=256):
    rows, width = tokens.shape
    hidden = up_bias.shape[1]
    narrow = pl.BlockSpec((block, width), lambda i: (i, 0))
    wide = pl.BlockSpec((block, hidden), lambda i: (i, 0))
    whole = lambda a: pl.BlockSpec(a.shape, lambda i: (0, 0))
    return pl.pallas_call(
        forward_kernel,
        grid=(rows // block,),
        in_specs=[SMEM]
        + [ANY] * (3 * PARTS)
        + [narrow, narrow, narrow, whole(smalls), whole(up_bias)],
        out_specs=[
            narrow, narrow, narrow, wide, wide, narrow, narrow,
            pl.BlockSpec((8, width), lambda i: (0, 0)),
        ],
        out_shape=[
            struct((rows, width), BF),
            struct((rows, width), F32),
            struct((rows, width), BF),
            struct((rows, hidden), BF),
            struct((rows, hidden), BF),
            struct((rows, width), BF),
            struct((rows, width), F32),
            struct((8, width), F32),
        ],
        scratch_shapes=[
            pltpu.VMEM((width, width), BF),
            pltpu.VMEM((width, hidden), BF),
            pltpu.VMEM((hidden, width), BF),
            pltpu.SemaphoreType.DMA((3, PARTS)),
        ],
        compiler_params=params(),
        cost_estimate=cost(2 * rows * width * (width + 2 * hidden), 40e6, 3 * rows * hidden),
        name="forward",
    )(index, *parts[0], *parts[1], *parts[2], mixed, tokens, cotangent, smalls, up_bias)


def backward_kernel(index, *refs):
    parts = [refs[at * PARTS : at * PARTS + PARTS] for at in range(3)]
    (
        dbranch_ref, slope_ref, dfinal_ref, resid_ref, small_ref,
        dhidden_ref, dresid_ref, dattn_ref, dmixed_ref, sums_ref, up_sums_ref,
        w_out, w_up, w_down, sems,
    ) = refs[3 * PARTS :]
    step = pl.program_id(0)
    weights = (w_out, w_up, w_down)
    copies = [fetch_copies(index, parts[at], weights[at], sems.at[at]) for at in range(3)]

    @pl.when(step == 0)
    def _():
        sums_ref[...] = jnp.zeros_like(sums_ref)
        up_sums_ref[...] = jnp.zeros_like(up_sums_ref)
        for group in (copies[2], copies[1], copies[0]):
            start_copies(group)
        for group in (copies[2], copies[1], copies[0]):
            wait_copies(group)

    width = w_down.shape[1]
    dnormed = dfinal_ref[...]
    for at in range(w_up.shape[1] // width):
        span = slice(at * width, at * width + width)
        dactive = dot_t(dbranch_ref[...], w_down[span, :])
        dhidden = (dactive * slope_ref[:, span].astype(F32)).astype(BF)
        dhidden_ref[:, span] = dhidden
        up_sums_ref[:, span] += jnp.sum(dhidden.astype(F32), axis=0, keepdims=True)
        dnormed = dnormed + dot_t(dhidden, w_up[:, span])
    hat, scale = norm_parts(resid_ref[...])
    dresid = norm_back(dnormed * small_ref[1:2, :], hat, scale)
    dresid_ref[...] = dresid
    dattn = dresid.astype(BF)
    dattn_ref[...] = dattn
    dmixed_ref[...] = dot_t(dattn, w_out[...]).astype(BF)
    add_rows(sums_ref, (dnormed * hat, dnormed, dattn))


def backward(index, parts, dbranch, slope, dfinal, resid, smalls, block=256):
    rows, width = resid.shape
    hidden = slope.shape[1]
    narrow = pl.BlockSpec((block, width), lambda i: (i, 0))
    wide = pl.BlockSpec((block, hidden), lambda i: (i, 0))
    whole = lambda a: pl.BlockSpec(a.shape, lambda i: (0, 0))
    return pl.pallas_call(
        backward_kernel,
        grid=(rows // block,),
        in_specs=[SMEM]
        + [ANY] * (3 * PARTS)
        + [narrow, wide, narrow, narrow, whole(smalls)],
        out_specs=[
            wide, narrow, narrow, narrow,
            pl.BlockSpec((8, width), lambda i: (0, 0)),
            pl.BlockSpec((1, hidden), lambda i: (0, 0)),
        ],
        out_shape=[
            struct((rows, hidden), BF),
            struct((rows, width), F32),
            struct((rows, width), BF),
            struct((rows, width), BF),
            struct((8, width), F32),
            struct((1, hidden), F32),
        ],
        scratch_shapes=[
            pltpu.VMEM((width, width), BF),
            pltpu.VMEM((width, hidden), BF),
            pltpu.VMEM((hidden, width), BF),
            pltpu.SemaphoreType.DMA((3, PARTS)),
        ],
        compiler_params=params(),
        cost_estimate=cost(2 * rows * width * (width + 2 * hidden), 40e6),
        name="backward",
    )(index, *parts[0], *parts[1], *parts[2], dbranch, slope, dfinal, resid, smalls)


def rows_kernel(index, left_ref, *refs):
    count = (len(refs) - 3) // 1
    rights, (keep_ref, send_ref, total) = refs[:count], refs[count:]
    right = jnp.concatenate([ref[...] for ref in rights], axis=1)
    total[...] = tdot(left_ref[...], right).astype(BF).reshape(total.shape)
    me = index[0]
    keep_ref[0] = total[me]
    keep_ref[1] = total[me ^ 2]
    send_ref[0] = total[me ^ 1]
    send_ref[1] = total[me ^ 3]


def weight_rows(index, left, rights, block=None):
    tokens, width = left.shape
    columns = sum(right.shape[1] for right in rights)
    block = block or columns
    shard = width // 4
    if len(rights) == 1:
        right_specs = [pl.BlockSpec((tokens, block), lambda i: (0, i))]
    else:
        right_specs = [pl.BlockSpec(right.shape, lambda i: (0, 0)) for right in rights]
    out = pl.BlockSpec((2, shard, block), lambda i: (0, 0, i))
    return pl.pallas_call(
        rows_kernel,
        grid=(columns // block,),
        in_specs=[SMEM, pl.BlockSpec((tokens, width), lambda i: (0, 0))] + right_specs,
        out_specs=[out, out],
        out_shape=[struct((2, shard, columns), BF)] * 2,
        scratch_shapes=[pltpu.VMEM((4, shard, block), BF)],
        compiler_params=params(),
        cost_estimate=cost(2 * tokens * width * columns, 4 * width * columns),
        name="weight_rows",
    )(index, left, *rights)


def down_kernel(index, left_ref, right_ref, send_ref, keep_ref):
    del index
    total = tdot(left_ref[...], right_ref[...]).astype(BF)

    @pl.when(pl.program_id(0) < 2)
    def _():
        send_ref[0] = total

    @pl.when(pl.program_id(0) >= 2)
    def _():
        keep_ref[0] = total


def down_rows(index, left, right):
    tokens, hidden = left.shape
    width = right.shape[1]
    shard = hidden // 4
    block = lambda i, s: (0, s[0] ^ jnp.where(i < 2, 2 * i + 1, 2 * i - 4))
    out = lambda shift: lambda i, s: (jnp.clip(i - shift, 0, 1), 0, 0)
    send, keep = pl.pallas_call(
        down_kernel,
        grid_spec=pltpu.PrefetchScalarGridSpec(
            num_scalar_prefetch=1,
            grid=(4,),
            in_specs=[
                pl.BlockSpec((tokens, shard), block),
                pl.BlockSpec((tokens, width), lambda i, s: (0, 0)),
            ],
            out_specs=[
                pl.BlockSpec((1, shard, width), out(0)),
                pl.BlockSpec((1, shard, width), out(2)),
            ],
        ),
        out_shape=[struct((2, shard, width), BF)] * 2,
        compiler_params=params(),
        cost_estimate=cost(2 * tokens * width * hidden, 13e6),
        name="down_rows",
    )(index, left, right)
    return keep, send


def on_device(
    tokens,
    layout_cells,
    pad_mask,
    query_weight,
    key_weight,
    value_weight,
    out_weight,
    query_bias,
    value_bias,
    out_bias,
    bias_table,
    first_gain,
    first_shift,
    up_weight,
    up_bias,
    down_weight,
    down_bias,
    second_gain,
    second_shift,
    cotangent,
):
    rows, width = tokens.shape
    hidden = down_weight.shape[0] * 4
    shard = width // 4
    me = lax.axis_index("fsdp")
    parity = lax.axis_index("dp") & 1
    index = jnp.stack([me, parity]).astype(jnp.int32)
    factor = 1.0 / math.sqrt(rows * lax.axis_size("dp") * lax.axis_size("fsdp"))

    vectors = (
        query_bias, value_bias, out_bias, first_gain, first_shift, down_bias, second_gain,
        second_shift,
    )
    table_row = jnp.pad(bias_table.reshape(-1), (0, width - bias_table.size))
    pack = jnp.concatenate(vectors + (up_bias, table_row)).reshape(4, width)
    packs = jnp.stack([pack, swap(pack, "fsdp", 1), swap(pack, "fsdp", 2), swap(pack, "fsdp", 3)])
    packs = jnp.stack(
        [lax.dynamic_index_in_dim(packs, me ^ at, 0, keepdims=False) for at in range(4)]
    )
    full_vectors = packs[:, :2].reshape(4, 8, shard).transpose(1, 0, 2).reshape(8, width)
    full_vectors = full_vectors.astype(F32)
    full_up_bias = packs[:, 2].reshape(1, hidden).astype(F32)
    table = packs[:, 3, : bias_table.size].reshape(HEADS, 3 * BUCKETS)
    smalls = full_vectors[2:8]

    qkv_parts = gather(jnp.concatenate([query_weight, key_weight, value_weight], axis=1), parity)
    out_parts = gather(out_weight, parity)
    up_parts = gather(up_weight, parity)
    down_parts = gather(down_weight, parity)

    extra, ke, ket, oh, near, near_t = prepare(layout_cells, pad_mask, table)
    qkv = project(index, qkv_parts, tokens, full_vectors[:2])
    mixed, extra = attend(qkv, extra, ket, near)
    weights = (out_parts, up_parts, down_parts)
    result, dfinal, dbranch, active, slope, normed, resid, sums_two = forward(
        index, weights, mixed, tokens, cotangent, smalls, full_up_bias
    )
    down_grad = down_rows(index, active, dbranch)
    dhidden, dresid, dattn, dmixed, sums_one, up_sums = backward(
        index, weights, dbranch, slope, dfinal, resid, smalls
    )
    up_grad = weight_rows(index, normed, (dhidden,), 768)
    out_grad = weight_rows(index, mixed, (dattn,))
    grad_down = reduce_rows(*down_grad, factor)
    grad_up = reduce_rows(*up_grad, factor)
    grad_out = reduce_rows(*out_grad, factor)

    grads, fars, nears, totals = [], [], [], []
    for group in GROUPS:
        dq, dk, dv, far, near_sums = attend_back(
            group, qkv, extra, ke, ket, oh, near_t, dmixed, mixed
        )
        grads += [dq, dk, dv]
        fars.append(far)
        nears.append(near_sums)
        totals.append(reduce_rows(*weight_rows(index, tokens, (dq, dk, dv)), factor))
    thirds = [[] for _ in range(3)]
    for total in totals:
        for at, piece in enumerate(jnp.split(total, 3, axis=1)):
            thirds[at].append(piece)
    grad_query, grad_key, grad_value = (jnp.concatenate(third, axis=1) for third in thirds)
    input_grad = input_gradient(index, qkv_parts, grads, dresid)

    table_grad = table_gradient(jnp.concatenate(fars), jnp.concatenate(nears))
    column_sum = lambda arrays: jnp.concatenate(
        [jnp.sum(a, axis=0, dtype=F32) for a in arrays]
    )
    sums = jnp.stack(
        [
            column_sum(grads[0::3]),
            column_sum(grads[2::3]),
            sums_one[2],
            sums_one[0],
            sums_one[1],
            sums_two[2],
            sums_two[0],
            sums_two[1],
        ]
    )
    sums, up_sums, table_grad = lax.psum((sums, up_sums, table_grad), ("dp", "fsdp"))
    sums = lax.dynamic_slice_in_dim(sums, me * shard, shard, 1) * factor
    up_sums = lax.dynamic_slice_in_dim(up_sums[0], me * (hidden // 4), hidden // 4, 0) * factor
    table_grad = lax.dynamic_slice_in_dim(table_grad, me * (HEADS // 4), HEADS // 4, 0) * factor
    return (
        result,
        input_grad,
        grad_query,
        grad_key,
        grad_value,
        grad_out,
        sums[0],
        sums[1],
        sums[2],
        table_grad,
        sums[3],
        sums[4],
        grad_up,
        up_sums,
        grad_down,
        sums[5],
        sums[6],
        sums[7],
    )


def solution(mesh):
    rows = P(("dp", "fsdp"), None)
    matrix, vector = P("fsdp", None), P("fsdp")
    return jax.shard_map(
        on_device,
        mesh=mesh,
        in_specs=(
            rows, P(None, ("dp", "fsdp")), P(("dp", "fsdp")),
            matrix, matrix, matrix, matrix,
            vector, vector, vector, matrix, vector, vector,
            matrix, vector, matrix, vector, vector, vector,
            rows,
        ),
        out_specs=(
            rows, rows,
            matrix, matrix, matrix, matrix,
            vector, vector, vector, matrix, vector, vector,
            matrix, vector, matrix, vector, vector, vector,
        ),
        check_vma=False,
    )
```

```python
import functools
import math

import jax
import jax.numpy as jnp
import numpy as np
from jax import lax
from jax.experimental import pallas as pl
from jax.experimental.pallas import tpu as pltpu
from jax.sharding import PartitionSpec as P

HEADS = 12
HD = 64
WIN = 512
BUCKETS = 32
PAIRS = HEADS // 2
SCALE = HD ** (-0.5)
EPS = 1e-05
BF = jnp.bfloat16
F32 = jnp.float32
VMEM_LIMIT = 60 * 1024 * 1024
GROUPS = ((0, 2), (2, 2), (4, 2))


def params():
    return pltpu.CompilerParams(vmem_limit_bytes=VMEM_LIMIT)


def cost(flops, nbytes, transcendentals=0):
    return pl.CostEstimate(
        flops=int(flops / 100),
        bytes_accessed=int(nbytes / 100),
        transcendentals=int(transcendentals / 100),
    )


def struct(shape, dtype):
    return jax.ShapeDtypeStruct(shape, dtype)


def dot(left, right):
    return lax.dot_general(left, right, (((1,), (0,)), ((), ())), preferred_element_type=F32)


def dot_t(left, right):
    return lax.dot_general(left, right, (((1,), (1,)), ((), ())), preferred_element_type=F32)


def tdot(left, right):
    return lax.dot_general(left, right, (((0,), (0,)), ((), ())), preferred_element_type=F32)


def split3(values):
    high = values.astype(BF)
    rest = values - high.astype(F32)
    middle = rest.astype(BF)
    return high, middle, (rest - middle.astype(F32)).astype(BF)


def swap(array, axis, bit):
    return lax.ppermute(array, axis, [(i, i ^ bit) for i in range(lax.axis_size(axis))])


def together(*groups):
    flat, tree = jax.tree.flatten(groups)
    return jax.tree.unflatten(tree, lax.optimization_barrier(tuple(flat)))


def half_of(array, which, axis=0):
    rows = array.shape[axis] // 2
    return lax.dynamic_slice_in_dim(array, which * rows, rows, axis)


class Chain:
    def __init__(self, steps):
        self.steps = steps
        self.result = None
        self.move = next(steps)

    def advance(self, arrived):
        try:
            self.move = self.steps.send(arrived)
        except StopIteration as stop:
            self.result = stop.value


def run(call, arrays, begin=(), finish=None):
    finish = begin if finish is None else finish
    arrays, sent = together(arrays, [chain.move[0] for chain in begin])
    for chain, array in zip(begin, sent):
        chain.flight = swap(array, chain.move[1], chain.move[2])
    out = call(*arrays) if call is not None else ()
    out, arrived = together(out, [chain.flight for chain in finish])
    for chain, array in zip(finish, arrived):
        chain.advance(array)
    return out


def gather_far(shard, which, bit):
    far = yield half_of(shard, which), "fsdp", 2
    beside = yield far, "dp", bit
    return far, beside


def send_once(array, axis, bit):
    arrived = yield array, axis, bit
    return arrived


def part_rows(me, which, rows):
    half = rows // 2
    mine, other = which * half, (1 - which) * half
    return (
        (me * rows, rows),
        ((me ^ 1) * rows, rows),
        ((me ^ 2) * rows + mine, half),
        ((me ^ 2) * rows + other, half),
        ((me ^ 3) * rows + mine, half),
        ((me ^ 3) * rows + other, half),
    )


PARTS = 6


def fetch_copies(index, which, parts, whole, sems):
    rows = whole.shape[0] // 4
    places = part_rows(index[0], index[which], rows)
    return [
        pltpu.make_async_copy(part, whole.at[pl.ds(pl.multiple_of(first, 16), count)], sems.at[at])
        for at, (part, (first, count)) in enumerate(zip(parts, places))
    ]


def start_copies(copies):
    for copy in copies:
        copy.start()


def wait_copies(copies):
    for copy in copies:
        copy.wait()


ANY = pl.BlockSpec(memory_space=pl.ANY)
SMEM = pl.BlockSpec(memory_space=pltpu.SMEM)


def reduce_steps(keep, send, factor):
    place = lax.axis_index("dp")
    near, beside = place & 1, (place >> 1) & 1

    def part(which, arrays):
        return sum(half_of(a, which).astype(F32) for a in arrays).astype(BF)

    got = yield send, "fsdp", 1
    far = yield (keep[1].astype(F32) + got[1].astype(F32)).astype(BF), "fsdp", 2
    terms = (keep[0], got[0], far)
    got = yield part(1 - near, terms), "dp", 1
    terms = (part(near, terms), got)
    got = yield part(1 - beside, terms), "dp", 2
    total = (part(beside, terms).astype(F32) + got.astype(F32)).astype(BF)
    bit = 4
    while bit < lax.axis_size("dp"):
        got = yield total, "dp", bit
        total = (total.astype(F32) + got.astype(F32)).astype(BF)
        bit *= 2
    got = yield total, "dp", 2
    total = in_order(total, got, beside)
    got = yield total, "dp", 1
    return in_order(total, got, near).astype(F32) * factor


def in_order(mine, other, which):
    return jnp.where(
        which == 0, jnp.concatenate([mine, other]), jnp.concatenate([other, mine])
    )


def table_places():
    step = np.arange(128)
    step = np.where(step < 64, -step, 128 - step)
    near = np.clip(step, -16, 15) + 16
    far = np.where(step <= -2, 0, np.where(step >= 2, 31, -1))
    wide = np.arange(256)
    wide = np.where(wide < 128, -wide, 256 - wide)
    places = np.concatenate([near + 32, near + 64, far, np.clip(wide, -16, 15) + 16])
    return places.astype(np.int32)[None, :]


def diagonal_places():
    lane = np.arange(128)
    x_place = np.where(lane < 63, np.clip(lane - 31, -16, 15) + 48, -1)
    y_place = np.where((lane >= 32) & (lane < 95), np.clip(lane - 63, -16, 15) + 80, -1)
    step = lane - 95
    block_place = np.where(
        (lane >= 64) & (step <= -2), 0, np.where((lane < 127) & (step >= 2), 31, -1)
    )
    step = (127 - np.arange(256) + 128) % 256 - 128
    places = np.concatenate([x_place, y_place, block_place, np.clip(step, -16, 15) + 16])
    return places.astype(np.int32)[:, None]


LANES = 640


def iota(shape, axis):
    return lax.broadcasted_iota(jnp.int32, shape, axis)


def as_bf(mask):
    return jnp.where(mask, 1.0, 0.0).astype(BF)


def near_mask():
    r, c = iota((128, 256), 0), iota((128, 256), 1)
    gap = (r >> 4) - (c >> 4)
    inside = (c < 128) & (gap <= 1) & (gap >= -1)
    return inside | ((r >= 112) & (c >= 128) & (c < 144)) | ((r < 16) & (c >= 240))


def hot_places(x, y, shape, axis):
    column = iota(shape, axis)
    block = (iota(shape, 1 - axis) & (WIN - 1)) >> 4
    third = column >> 5
    hot = jnp.where(third == 0, x, jnp.where(third == 1, y + 32, block + 64)) == column
    return column, hot & (column < 96)


PACK_ROWS, UP_ROW, TABLE_ROW = 16, 8, 10


def pack_vectors(vectors, up_bias, table):
    width, shard = up_bias.shape[0], vectors[0].shape[0]
    row = lax.broadcasted_iota(jnp.int32, (PACK_ROWS, shard), 0)
    pack = jnp.zeros((PACK_ROWS, shard), BF)
    for at, vector in enumerate(vectors):
        pack = jnp.where(row == at, vector[None, :], pack)
    pack = jnp.pad(pack, ((0, 0), (0, width - shard)))
    row = lax.broadcasted_iota(jnp.int32, (PACK_ROWS, width), 0)
    pack = jnp.where(row == UP_ROW, up_bias[None, :], pack)
    below = PACK_ROWS - TABLE_ROW - table.shape[0]
    return pack + jnp.pad(table, ((TABLE_ROW, below), (0, width - table.shape[1])))


def prep_kernel(
    index, p0, p1, p2, p3, cells_ref, mask_ref, places_ref,
    e_ref, ke_ref, ket_ref, oh_ref, dt_ref, vectors_ref, up_bias_ref, own, packs,
):
    tokens = cells_ref.shape[1]
    me = index[0]
    head = pl.program_id(0)

    @pl.when(head == 0)
    def _():
        for at, ref in enumerate((p0, p1, p2, p3)):
            packs[at] = ref[...]
        vectors = 0.0
        width = vectors_ref.shape[1]
        for at in range(4):
            rows = packs[me ^ at].astype(F32)
            vectors = vectors + pltpu.roll(rows[:8], at * (width // 4), 1)
            up_bias_ref[:, at * width : at * width + width] = rows[UP_ROW : UP_ROW + 1]
        vectors_ref[...] = vectors
        x, y, valid = cells_ref[0:1, :], cells_ref[1:2, :], mask_ref[...]
        column, hot = hot_places(x, y, (128, tokens), 0)
        ket_ref[...] = as_bf(hot)
        own[...] = as_bf(hot | (column == 96))
        sub = iota((8, tokens), 0)
        columns = jnp.where(sub == 0, x, jnp.where(sub == 1, y, valid)).astype(F32)
        columns = columns.T.astype(jnp.int32)
        x, y, valid = columns[:, 0:1], columns[:, 1:2], columns[:, 2:3]
        column, hot = hot_places(x, y, (tokens, 128), 1)
        masked = jnp.where((column == 99) & (valid <= 0), -1e30, 0.0)
        ones = hot | ((column >= 96) & (column < 99))
        ke_ref[...] = jnp.where(ones, 1.0, masked).astype(BF)
        block = (iota((tokens, 128), 0) & (WIN - 1)) >> 4
        third = column >> 5
        back = jnp.where(third == 0, 31 - x, jnp.where(third == 1, 63 - y, 95 - block)) == column
        oh_ref[...] = as_bf(back & (column < 96))

    table = packs[me ^ (head // 3)][:, :128].astype(F32)
    table = jnp.where(iota((PACK_ROWS, 128), 0) == TABLE_ROW + head % 3, table, 0.0)
    pick = as_bf(iota((128, LANES), 0) == places_ref[...])
    row = jnp.sum(dot(table.astype(BF), pick), axis=0, keepdims=True)
    lane = iota((32, 128), 1)
    blocks = []
    for at in range(3):
        spread = jnp.broadcast_to(row[:, at * 128 : at * 128 + 128], (32, 128))
        spread = pltpu.roll(spread, at * 32, 1, stride=1, stride_axis=0)
        blocks.append(jnp.where(lane >> 5 == at, spread, 0.0))
    blocks.append(jnp.where((iota((32, 128), 0) == 3) & (lane == 96), 1.0, 0.0))
    e_ref[...] = dot(jnp.concatenate(blocks, axis=0).astype(BF), own[...]).astype(BF)
    wide = jnp.broadcast_to(row[:, 384:640], (128, 256))
    rolled = pltpu.roll(wide, 0, 1, stride=1, stride_axis=0)
    dt_ref[0] = jnp.where(near_mask(), rolled, 0.0)


def prepare(index, packs, layout_cells, pad_mask):
    tokens = pad_mask.shape[0]
    width = packs[0].shape[1]
    whole = lambda h: (0, 0)
    pack = pl.BlockSpec((PACK_ROWS, width), whole)
    return pl.pallas_call(
        prep_kernel,
        grid=(HEADS,),
        in_specs=[SMEM, pack, pack, pack, pack]
        + [
            pl.BlockSpec((2, tokens), whole),
            pl.BlockSpec((1, tokens), whole),
            pl.BlockSpec((1, LANES), whole),
        ],
        out_specs=[
            pl.BlockSpec((128, tokens), lambda h: (h, 0)),
            pl.BlockSpec((tokens, 128), whole),
            pl.BlockSpec((128, tokens), whole),
            pl.BlockSpec((tokens, 128), whole),
            pl.BlockSpec((1, 128, 256), lambda h: (h, 0, 0)),
            pl.BlockSpec((8, width), whole),
            pl.BlockSpec((1, 4 * width), whole),
        ],
        out_shape=[
            struct((HEADS * 128, tokens), BF),
            struct((tokens, 128), BF),
            struct((128, tokens), BF),
            struct((tokens, 128), BF),
            struct((HEADS, 128, 256), F32),
            struct((8, width), F32),
            struct((1, 4 * width), F32),
        ],
        scratch_shapes=[
            pltpu.VMEM((128, tokens), BF),
            pltpu.VMEM((4, PACK_ROWS, width), BF),
        ],
        compiler_params=params(),
        cost_estimate=cost(2 * tokens * 128 * 128 * HEADS, 7e6),
        name="prepare",
    )(index, *packs, layout_cells, pad_mask.reshape(1, tokens), jnp.asarray(table_places()))


def project_kernel(index, *refs):
    parts, (x_ref, bias_ref, out_ref, weight, sems) = refs[:PARTS], refs[PARTS:]

    @pl.when(pl.program_id(0) == 0)
    def _():
        copies = fetch_copies(index, 1, parts, weight, sems)
        start_copies(copies)
        wait_copies(copies)

    width = out_ref.shape[1] // 3
    for at in range(3):
        span = slice(at * width, (at + 1) * width)
        values = dot(x_ref[...], weight[:, span])
        if at == 0:
            values = (values + bias_ref[0:1, :]).astype(BF) * SCALE
        if at == 2:
            values = values + bias_ref[1:2, :]
        out_ref[:, span] = values.astype(BF)


def project(index, parts, tokens, biases, block=512):
    rows, width = tokens.shape
    return pl.pallas_call(
        project_kernel,
        grid=(rows // block,),
        in_specs=[SMEM]
        + [ANY] * PARTS
        + [
            pl.BlockSpec((block, width), lambda i: (i, 0)),
            pl.BlockSpec((8, width), lambda i: (0, 0)),
        ],
        out_specs=pl.BlockSpec((block, 3 * width), lambda i: (i, 0)),
        out_shape=struct((rows, 3 * width), BF),
        scratch_shapes=[pltpu.VMEM((width, 3 * width), BF), pltpu.SemaphoreType.DMA((PARTS,))],
        compiler_params=params(),
        cost_estimate=cost(6 * rows * width * width, 10e6),
        name="project",
    )(index, *parts, tokens, biases)


def input_kernel(index, *refs):
    count = len(GROUPS) * 3
    parts, grads = refs[:PARTS], refs[PARTS : PARTS + count]
    dresid_ref, out_ref, weight, sems = refs[PARTS + count :]

    @pl.when(pl.program_id(0) == 0)
    def _():
        copies = fetch_copies(index, 1, parts, weight, sems)
        start_copies(copies)
        wait_copies(copies)

    joined = jnp.concatenate(
        [grads[3 * group + at][...] for at in range(3) for group in range(len(GROUPS))], axis=1
    )
    out_ref[...] = (dresid_ref[...] + dot_t(joined, weight[...])).astype(BF)


def input_gradient(index, parts, grads, dresid, block=512):
    rows, width = dresid.shape
    spec = lambda a: pl.BlockSpec((block, a.shape[1]), lambda i: (i, 0))
    return pl.pallas_call(
        input_kernel,
        grid=(rows // block,),
        in_specs=[SMEM] + [ANY] * PARTS + [spec(a) for a in grads] + [spec(dresid)],
        out_specs=spec(dresid),
        out_shape=struct((rows, width), BF),
        scratch_shapes=[pltpu.VMEM((width, 3 * width), BF), pltpu.SemaphoreType.DMA((PARTS,))],
        compiler_params=params(),
        cost_estimate=cost(6 * rows * width * width, 13e6),
        name="input_gradient",
    )(index, *parts, *grads, dresid)


def with_near(pieces, tile, at):
    pieces = list(pieces)
    pieces[at] = pieces[at] + tile[:, :128]
    if at > 0:
        left = pieces[at - 1]
        pieces[at - 1] = jnp.concatenate([left[:16] + tile[:16, 128:], left[16:]], axis=0)
    if at < 3:
        right = pieces[at + 1]
        pieces[at + 1] = jnp.concatenate([right[:112], right[112:] + tile[112:, 128:]], axis=0)
    return pieces


def lane_blocks(values):
    return [values[:, c * 128 : c * 128 + 128] for c in range(WIN // 128)]


def attend_kernel(q_ref, k_ref, v_ref, e_ref, ke_ref, dt_ref, out_ref, eout_ref, s_scr, p_scr):
    first = iota((128, WIN), 0) < HD
    place = iota((128, WIN), 0)
    keys = jnp.concatenate([k_ref[...], ke_ref[...]], axis=1)
    query_t = q_ref[...].T
    value_t = v_ref[...].T
    for head in range(2):
        mine = first if head == 0 else ~first
        query = jnp.where(mine, query_t, jnp.zeros((), BF))
        extra = e_ref[head * 128 : head * 128 + 128, :]
        s_scr[head] = dot(keys, jnp.concatenate([query, extra], axis=0))
    mixed = []
    for head in range(2):
        tile = dt_ref[head]
        scores = [
            with_near(lane_blocks(s_scr[head, at * 128 : at * 128 + 128, :]), tile, at)
            for at in range(WIN // 128)
        ]
        tops, totals = [], []
        for column in range(WIN // 128):
            pieces = [row[column] for row in scores]
            top = jnp.maximum(
                jnp.maximum(pieces[0], pieces[1]), jnp.maximum(pieces[2], pieces[3])
            )
            top = jnp.max(top, axis=0, keepdims=True)
            pieces = [jnp.exp(piece - top) for piece in pieces]
            total = (pieces[0] + pieces[1]) + (pieces[2] + pieces[3])
            totals.append(jnp.sum(total, axis=0, keepdims=True))
            tops.append(top)
            for at, piece in enumerate(pieces):
                p_scr[
                    head, at * 128 : at * 128 + 128, column * 128 : column * 128 + 128
                ] = piece.astype(BF)
        total = jnp.concatenate(totals, axis=1)
        mixed.append(dot(value_t[head * HD : head * HD + HD], p_scr[head]) / total)
        parts = split3(-(jnp.concatenate(tops, axis=1) + jnp.log(total)))
        extra = e_ref[head * 128 : head * 128 + 128, :]
        for at in range(3):
            extra = jnp.where(place == 96 + at, parts[at], extra)
        eout_ref[head * 128 : head * 128 + 128, :] = extra
    out_ref[...] = jnp.concatenate(mixed, axis=0).astype(BF).T


def attend(group, qkv, extra, ke, near_t, mixed=None):
    start, pairs = group
    tokens = qkv.shape[0]
    windows = tokens // WIN
    block = lambda shift: pl.BlockSpec((WIN, 128), lambda p, w: (w, p + start + shift))
    extra_block = pl.BlockSpec((256, WIN), lambda p, w: (p + start, w))
    kernel, more, aliases = attend_kernel, (), {3: 1}
    if mixed is not None:
        kernel = lambda *refs: attend_kernel(*refs[:6], *refs[7:])
        more, aliases = (mixed,), {3: 1, 6: 0}
    return pl.pallas_call(
        kernel,
        grid=(pairs, windows),
        in_specs=[
            block(0),
            block(PAIRS),
            block(2 * PAIRS),
            extra_block,
            pl.BlockSpec((WIN, 128), lambda p, w: (w, 0)),
            pl.BlockSpec((2, 128, 256), lambda p, w: (p + start, 0, 0)),
        ]
        + [ANY] * len(more),
        out_specs=[block(0), extra_block],
        out_shape=[struct((tokens, PAIRS * 128), BF), struct(extra.shape, BF)],
        input_output_aliases=aliases,
        scratch_shapes=[pltpu.VMEM((2, WIN, WIN), F32), pltpu.VMEM((2, WIN, WIN), BF)],
        compiler_params=params(),
        cost_estimate=cost(tokens * WIN * pairs * 1536, 6e6 * pairs / 2, tokens * WIN * 2 * pairs),
        name="attend",
    )(qkv, qkv, qkv, extra, ke, near_t, *more)


def diagonal_rows(sums):
    lane = iota((32, 128), 1)
    rows = []
    for at in range(3):
        block = jnp.where(lane >> 5 == at, sums[at * 32 : at * 32 + 32], 0.0)
        rolled = pltpu.roll(block, 0, 1, stride=1, stride_axis=0)
        rows.append(jnp.sum(rolled, axis=0, keepdims=True))
    return rows


def near_rows(tile):
    tile = jnp.where(near_mask(), tile, 0.0)
    turn = as_bf(iota((128, 128), 0) + iota((128, 128), 1) == 127)
    high, middle, low = split3(tile)
    turned = dot(turn, high) + dot(turn, middle) + dot(turn, low)
    rolled = pltpu.roll(turned, 0, 1, stride=1, stride_axis=0)
    return jnp.sum(rolled, axis=0, keepdims=True)


def attend_back_kernel(
    q_ref, k_ref, v_ref, e_ref, ke_ref, ket_ref, oh_ref, dt_ref, do_ref, o_ref,
    dq_ref, dk_ref, dv_ref, bias_ref, far_ref, near_ref,
    s_scr, dp_scr, p_scr, ds_scr, sums, tiles,
):
    window = pl.program_id(1)

    @pl.when(window == 0)
    def _():
        sums[...] = jnp.zeros_like(sums)
        tiles[...] = jnp.zeros_like(tiles)
        bias_ref[...] = jnp.zeros_like(bias_ref)

    zero = jnp.zeros((), BF)
    first = iota((WIN, 128), 1) < HD
    first_t = iota((128, WIN), 0) < HD
    place = iota((128, WIN), 0)
    keys = jnp.concatenate([k_ref[...], ke_ref[...]], axis=1)
    values = jnp.concatenate([v_ref[...], ke_ref[...]], axis=1)
    keys_t, query_t, grad_t = k_ref[...].T, q_ref[...].T, do_ref[...].T
    product = grad_t.astype(F32) * o_ref[...].T.astype(F32)
    dq_t, dk, dv = [], None, None
    for head in range(2):
        mine = first_t if head == 0 else ~first_t
        delta = -jnp.sum(product[head * HD : head * HD + HD], axis=0, keepdims=True)
        parts = split3(delta)
        minus = jnp.zeros((128, WIN), BF)
        for at in range(3):
            minus = jnp.where(place == 96 + at, parts[at], minus)
        extra = e_ref[head * 128 : head * 128 + 128, :]
        s_scr[head] = dot(keys, jnp.concatenate([jnp.where(mine, query_t, zero), extra], axis=0))
        dp_scr[head] = dot(values, jnp.concatenate([jnp.where(mine, grad_t, zero), minus], axis=0))
    for head in range(2):
        mine = first if head == 0 else ~first
        query = jnp.where(mine, q_ref[...], zero)
        grad = jnp.where(mine, do_ref[...], zero)
        tile = dt_ref[head]
        diag, low, high = None, None, None
        for at in range(WIN // 128):
            rows = slice(at * 128, at * 128 + 128)
            scores = with_near(lane_blocks(s_scr[head, rows, :]), tile, at)
            probs = [jnp.exp(piece) for piece in scores]
            dprobs = lane_blocks(dp_scr[head, rows, :])
            dscores = [a * b for a, b in zip(probs, dprobs)]
            p_scr[head, rows, :] = jnp.concatenate([a.astype(BF) for a in probs], axis=1)
            ds_scr[head, rows, :] = jnp.concatenate([a.astype(BF) for a in dscores], axis=1)
            add = lambda total, term: term if total is None else total + term
            diag = add(diag, dscores[at])
            if at > 0:
                low = add(low, dscores[at - 1][:16])
            if at < 3:
                high = add(high, dscores[at + 1][112:])
        dscores = ds_scr[head]
        dv_head = dot(p_scr[head], grad)
        dk_head = dot(dscores, query)
        dv = dv_head if dv is None else dv + dv_head
        dk = dk_head if dk is None else dk + dk_head
        left = jnp.concatenate([keys_t[head * HD : head * HD + HD], ket_ref[:96]], axis=0)
        both = dot(left, dscores)
        dq_t.append(both[:HD] * SCALE)
        extra = both[HD:]
        extra_high = extra.astype(BF)
        extra_low = (extra - extra_high.astype(F32)).astype(BF)
        far = dot(extra_high, oh_ref[...]) + dot(extra_low, oh_ref[...])
        sums[head] = sums[head] + far
        tiles[head, :, :128] = tiles[head, :, :128] + diag
        tiles[head, :16, 128:] = tiles[head, :16, 128:] + low
        tiles[head, 112:, 128:] = tiles[head, 112:, 128:] + high
    dq = jnp.concatenate(dq_t, axis=0).astype(BF).T
    dv = dv.astype(BF)
    dq_ref[...] = dq
    dk_ref[...] = dk.astype(BF)
    dv_ref[...] = dv
    for at, values in enumerate((dq, dv)):
        bias_ref[0, at : at + 1, :] += jnp.sum(values.astype(F32), axis=0, keepdims=True)

    @pl.when(window == pl.num_programs(1) - 1)
    def _():
        for head in range(2):
            rows = diagonal_rows(sums[head])
            far_ref[head] = jnp.concatenate(rows + [jnp.zeros((5, 128), F32)], axis=0)
            near_ref[head] = jnp.broadcast_to(near_rows(tiles[head]), (8, 256))


def attend_back(group, qkv, extra, ke, ket, oh, near_t, dmixed, mixed):
    start, pairs = group
    tokens = qkv.shape[0]
    windows = tokens // WIN
    block = lambda shift: pl.BlockSpec((WIN, 128), lambda p, w: (w, p + start + shift))
    per_window = pl.BlockSpec((WIN, 128), lambda p, w: (w, 0))
    out = pl.BlockSpec((WIN, 128), lambda p, w: (w, p))
    out_rows = struct((tokens, pairs * 128), BF)
    return pl.pallas_call(
        attend_back_kernel,
        grid=(pairs, windows),
        in_specs=[
            block(0),
            block(PAIRS),
            block(2 * PAIRS),
            pl.BlockSpec((256, WIN), lambda p, w: (p + start, w)),
            per_window,
            pl.BlockSpec((128, WIN), lambda p, w: (0, w)),
            per_window,
            pl.BlockSpec((2, 128, 256), lambda p, w: (p + start, 0, 0)),
            block(0),
            block(0),
        ],
        out_specs=[
            out,
            out,
            out,
            pl.BlockSpec((1, 8, 128), lambda p, w: (p, 0, 0)),
            pl.BlockSpec((2, 8, 128), lambda p, w: (p, 0, 0)),
            pl.BlockSpec((2, 8, 256), lambda p, w: (p, 0, 0)),
        ],
        out_shape=[
            out_rows,
            out_rows,
            out_rows,
            struct((pairs, 8, 128), F32),
            struct((2 * pairs, 8, 128), F32),
            struct((2 * pairs, 8, 256), F32),
        ],
        scratch_shapes=[
            pltpu.VMEM((2, WIN, WIN), F32),
            pltpu.VMEM((2, WIN, WIN), F32),
            pltpu.VMEM((2, WIN, WIN), BF),
            pltpu.VMEM((2, WIN, WIN), BF),
            pltpu.VMEM((2, 96, 128), F32),
            pltpu.VMEM((2, 128, 256), F32),
        ],
        compiler_params=params(),
        cost_estimate=cost(
            tokens * WIN * pairs * 2 * 2048, 12e6, tokens * WIN * pairs * 2
        ),
        name="attend_back",
    )(qkv, qkv, qkv, extra, ke, ket, oh, near_t, dmixed, mixed)


def norm_parts(values):
    centre = values - jnp.mean(values, axis=-1, keepdims=True)
    spread = jnp.mean(centre * centre, axis=-1, keepdims=True)
    scale = lax.rsqrt(spread + EPS)
    return centre * scale, scale


def norm_back(grad, hat, scale):
    mean = jnp.mean(grad, axis=-1, keepdims=True)
    along = jnp.mean(grad * hat, axis=-1, keepdims=True)
    return scale * (grad - mean - hat * along)


def row_blocks(ref, rows=256):
    return [slice(at, at + rows) for at in range(0, ref.shape[0], rows)]


def add_rows(ref, rows):
    for at, values in enumerate(rows):
        ref[at : at + 1, :] += jnp.sum(values.astype(F32), axis=0, keepdims=True)


def gelu_and_slope(values):
    upto = 0.5 + 0.5 * lax.erf(values * math.sqrt(0.5))
    density = jnp.exp(values * values * -0.5) * (1.0 / math.sqrt(2.0 * math.pi))
    return values * upto, upto + values * density


def up_kernel(index, *refs):
    (
        mixed_ref, x_ref, small_ref, up_bias_ref,
        active_ref, slope_ref, normed_ref, resid_ref,
        weight, sems,
    ) = refs[PARTS:]

    @pl.when(pl.program_id(0) == 0)
    def _():
        copies = fetch_copies(index, 1, refs[:PARTS], weight, sems)
        start_copies(copies)
        wait_copies(copies)

    small = lambda at: small_ref[at + 2 : at + 3, :]
    width = x_ref.shape[1]
    for rows in row_blocks(x_ref):
        attended = dot(mixed_ref[rows, :], weight[:, :width]) + small(0)
        resid = x_ref[rows, :].astype(F32) + attended
        resid_ref[rows, :] = resid
        hat, _ = norm_parts(resid)
        low = (hat * small(1) + small(2)).astype(BF)
        normed_ref[rows, :] = low
        for at in range(up_bias_ref.shape[1] // width):
            span = slice(at * width, at * width + width)
            hidden = dot(low, weight[:, (at + 1) * width : (at + 2) * width])
            active, slope = gelu_and_slope(hidden + up_bias_ref[:, span])
            slope_ref[rows, span] = slope.astype(BF)
            active_ref[rows, span] = active.astype(BF)


def go_up(index, parts, mixed, tokens, smalls, up_bias, block=512):
    rows, width = tokens.shape
    hidden = up_bias.shape[1]
    spec = lambda columns: pl.BlockSpec((block, columns), lambda i: (i, 0))
    whole = lambda a: pl.BlockSpec(a.shape, lambda i: (0, 0))
    return pl.pallas_call(
        up_kernel,
        grid=(rows // block,),
        in_specs=[SMEM]
        + [ANY] * PARTS
        + [spec(width), spec(width), whole(smalls), whole(up_bias)],
        out_specs=[spec(hidden), spec(hidden), spec(width), spec(width)],
        out_shape=[
            struct((rows, hidden), BF),
            struct((rows, hidden), BF),
            struct((rows, width), BF),
            struct((rows, width), F32),
        ],
        scratch_shapes=[
            pltpu.VMEM((width, width + hidden), BF),
            pltpu.SemaphoreType.DMA((PARTS,)),
        ],
        compiler_params=params(),
        cost_estimate=cost(2 * rows * width * (width + hidden), 26e6, 3 * rows * hidden),
        name="go_up",
    )(index, *parts, mixed, tokens, smalls, up_bias)


def down_kernel(index, *refs):
    parts = refs[:PARTS]
    (
        active_ref, resid_ref, cot_ref, small_ref,
        out_ref, dfinal_ref, dbranch_ref, sums_ref,
        weight, sems,
    ) = refs[PARTS:]

    @pl.when(pl.program_id(0) == 0)
    def _():
        sums_ref[...] = jnp.zeros_like(sums_ref)
        copies = fetch_copies(index, 2, parts, weight, sems)
        start_copies(copies)
        wait_copies(copies)

    small = lambda at: small_ref[at + 2 : at + 3, :]
    for rows in row_blocks(resid_ref, 128):
        hat, _ = norm_parts(resid_ref[rows, :])
        normed = hat * small(1) + small(2)
        final = normed + dot(active_ref[rows, :], weight[...]) + small(3)
        hat, scale = norm_parts(final)
        out_ref[rows, :] = (hat * small(4) + small(5)).astype(BF)
        cot = cot_ref[rows, :].astype(F32)
        dfinal = norm_back(cot * small(4), hat, scale)
        dfinal_ref[rows, :] = dfinal
        dbranch = dfinal.astype(BF)
        dbranch_ref[rows, :] = dbranch
        add_rows(sums_ref, (cot * hat, cot, dbranch))


def go_down(index, parts, active, resid, cotangent, smalls, block=512):
    rows, width = resid.shape
    hidden = active.shape[1]
    spec = lambda columns: pl.BlockSpec((block, columns), lambda i: (i, 0))
    whole = lambda a: pl.BlockSpec(a.shape, lambda i: (0, 0))
    return pl.pallas_call(
        down_kernel,
        grid=(rows // block,),
        in_specs=[SMEM]
        + [ANY] * PARTS
        + [spec(hidden), spec(width), spec(width), whole(smalls)],
        out_specs=[spec(width), spec(width), spec(width), whole(struct((8, width), F32))],
        out_shape=[
            struct((rows, width), BF),
            struct((rows, width), F32),
            struct((rows, width), BF),
            struct((8, width), F32),
        ],
        scratch_shapes=[
            pltpu.VMEM((hidden, width), BF),
            pltpu.SemaphoreType.DMA((PARTS,)),
        ],
        compiler_params=params(),
        cost_estimate=cost(2 * rows * width * hidden, 26e6),
        name="go_down",
    )(index, *parts, active, resid, cotangent, smalls)


def backward_kernel(index, *refs):
    up_parts, down_parts = refs[:PARTS], refs[PARTS : 2 * PARTS]
    (
        dbranch_ref, slope_ref, dfinal_ref, resid_ref, small_ref,
        dhidden_ref, dresid_ref, dattn_ref, dmixed_ref, sums_ref, up_sums_ref,
        w_up, w_down, sems,
    ) = refs[2 * PARTS :]

    @pl.when(pl.program_id(0) == 0)
    def _():
        sums_ref[...] = jnp.zeros_like(sums_ref)
        up_sums_ref[...] = jnp.zeros_like(up_sums_ref)
        copies = fetch_copies(index, 2, down_parts, w_down, sems.at[0])
        copies += fetch_copies(index, 1, up_parts, w_up, sems.at[1])
        start_copies(copies)
        wait_copies(copies)

    width = w_down.shape[1]
    for rows in row_blocks(resid_ref):
        dnormed = dfinal_ref[rows, :]
        for at in range(w_down.shape[0] // width):
            span = slice(at * width, at * width + width)
            dactive = dot_t(dbranch_ref[rows, :], w_down[span, :])
            dhidden = (dactive * slope_ref[rows, span].astype(F32)).astype(BF)
            dhidden_ref[rows, span] = dhidden
            up_sums_ref[:, span] += jnp.sum(dhidden.astype(F32), axis=0, keepdims=True)
            dnormed = dnormed + dot_t(dhidden, w_up[:, (at + 1) * width : (at + 2) * width])
        hat, scale = norm_parts(resid_ref[rows, :])
        dresid = norm_back(dnormed * small_ref[3:4, :], hat, scale)
        dresid_ref[rows, :] = dresid
        dattn = dresid.astype(BF)
        dattn_ref[rows, :] = dattn
        dmixed_ref[rows, :] = dot_t(dattn, w_up[:, :width]).astype(BF)
        add_rows(sums_ref, (dnormed * hat, dnormed, dattn))


def backward(index, up_parts, down_parts, dbranch, slope, dfinal, resid, smalls, block=512):
    rows, width = resid.shape
    hidden = slope.shape[1]
    spec = lambda columns: pl.BlockSpec((block, columns), lambda i: (i, 0))
    whole = lambda a: pl.BlockSpec(a.shape, lambda i: (0, 0))
    return pl.pallas_call(
        backward_kernel,
        grid=(rows // block,),
        in_specs=[SMEM]
        + [ANY] * (2 * PARTS)
        + [spec(width), spec(hidden), spec(width), spec(width), whole(smalls)],
        out_specs=[
            spec(hidden), spec(width), spec(width), spec(width),
            whole(struct((8, width), F32)),
            whole(struct((1, hidden), F32)),
        ],
        out_shape=[
            struct((rows, hidden), BF),
            struct((rows, width), F32),
            struct((rows, width), BF),
            struct((rows, width), BF),
            struct((8, width), F32),
            struct((1, hidden), F32),
        ],
        scratch_shapes=[
            pltpu.VMEM((width, width + hidden), BF),
            pltpu.VMEM((hidden, width), BF),
            pltpu.SemaphoreType.DMA((2, PARTS)),
        ],
        compiler_params=params(),
        cost_estimate=cost(2 * rows * width * (width + 2 * hidden), 40e6),
        name="backward",
    )(index, *up_parts, *down_parts, dbranch, slope, dfinal, resid, smalls)


def place_rows(index, total, keep_ref, send_ref):
    me = index[0]
    keep_ref[0] = total[me]
    keep_ref[1] = total[me ^ 2]
    send_ref[0] = total[me ^ 1]
    send_ref[1] = total[me ^ 3]


def rows_kernel(index, left_ref, *refs):
    *rights, keep_ref, send_ref, left_t, total = refs

    @pl.when(pl.program_id(0) == 0)
    def _():
        left_t[...] = left_ref[...].T

    right = jnp.concatenate([ref[...] for ref in rights], axis=1)
    total[...] = dot(left_t[...], right).astype(BF).reshape(total.shape)
    place_rows(index, total, keep_ref, send_ref)


def weight_rows(index, left, rights, block=None):
    tokens, width = left.shape
    shard = width // 4
    columns = sum(right.shape[1] for right in rights)
    specs = [pl.BlockSpec(right.shape, lambda i: (0, 0)) for right in rights]
    if block is not None:
        specs = [pl.BlockSpec((tokens, block), lambda i: (0, i))]
    block = block or columns
    out = pl.BlockSpec((2, shard, block), lambda i: (0, 0, i))
    return pl.pallas_call(
        rows_kernel,
        grid=(columns // block,),
        in_specs=[SMEM, pl.BlockSpec((tokens, width), lambda i: (0, 0))] + specs,
        out_specs=[out, out],
        out_shape=[struct((2, shard, columns), BF)] * 2,
        scratch_shapes=[pltpu.VMEM((width, tokens), BF), pltpu.VMEM((4, shard, block), BF)],
        compiler_params=params(),
        cost_estimate=cost(2 * tokens * width * columns, 4 * width * columns),
        name="weight_rows",
    )(index, left, *rights)


def small_rows(refs, places, sums_one, sums_two, up_sums, rows, sums):
    width = rows.shape[1]
    shard = width // 4
    rows[...] = jnp.zeros_like(rows)
    sums[...] = jnp.zeros_like(sums)
    pair, head = 0, 0
    for bias, far, near in refs:
        for at in range(bias.shape[0]):
            for row in range(2):
                rows[row : row + 1, pair * 128 : pair * 128 + 128] = bias[at, row : row + 1, :]
            pair += 1
        for at in range(far.shape[0]):
            parts = [far[at, row : row + 1, :] for row in range(3)] + [near[at, 0:1, :]]
            sums[head : head + 1, :] = jnp.concatenate(parts, axis=1)
            head += 1
    for row, source in enumerate((2, 0, 1)):
        rows[row + 2 : row + 3, :] = sums_one[source : source + 1, :]
        rows[row + 5 : row + 6, :] = sums_two[source : source + 1, :]
    lane = iota((1, width), 1)
    for at in range(4):
        values = up_sums[:, at * width : at * width + width]
        inside = (lane >= at * shard) & (lane < (at + 1) * shard)
        for part in range(4):
            rolled = pltpu.roll(values, (at - part) % 4 * shard, 1)
            rows[8 + part : 9 + part, :] += jnp.where(inside, rolled, 0.0)
    pick = as_bf(places[...] == iota((LANES, 128), 1))
    table = sum(dot(part, pick) for part in split3(sums[...]))
    table = jnp.concatenate([table, jnp.zeros((table.shape[0], width - 128), F32)], axis=1)
    for at in range(HEADS):
        within = at % 3
        shift = at // 3 * shard + within % 2 * 96
        rolled = pltpu.roll(table[at : at + 1], shift, 1)
        rows[12 + within // 2 : 13 + within // 2, :] += rolled


def last_kernel(count, index, left_ref, *refs):
    rights, refs = refs[:3], refs[3:]
    groups, refs = refs[: 3 * count], refs[3 * count :]
    places, sums_one, sums_two, up_sums, keep_ref, send_ref, total, rows, sums = refs
    groups = [groups[at : at + 3] for at in range(0, 3 * count, 3)]
    small_rows(groups, places, sums_one, sums_two, up_sums, rows, sums)
    right = jnp.concatenate([ref[...] for ref in rights], axis=1)
    columns = right.shape[1]
    shape = total.shape[:2]
    total[:, :, :columns] = tdot(left_ref[...], right).astype(BF).reshape(shape + (columns,))
    total[:, :, columns:] = rows[...].T.astype(BF).reshape(shape + (128,))
    place_rows(index, total, keep_ref, send_ref)


def last_rows(index, left, rights, groups, sums_one, sums_two, up_sums):
    tokens, width = left.shape
    columns = sum(right.shape[1] for right in rights)
    flops = 2 * tokens * width * columns
    columns += 128
    arrays = [left, *rights, *(array for group in groups for array in group)]
    arrays += [jnp.asarray(diagonal_places()), sums_one, sums_two, up_sums]
    whole = lambda shape: pl.BlockSpec(shape, lambda i: (0,) * len(shape))
    out = (2, width // 4, columns)
    return pl.pallas_call(
        functools.partial(last_kernel, len(groups)),
        grid=(1,),
        in_specs=[SMEM] + [whole(array.shape) for array in arrays],
        out_specs=[whole(out), whole(out)],
        out_shape=[struct(out, BF)] * 2,
        scratch_shapes=[
            pltpu.VMEM((4, width // 4, columns), BF),
            pltpu.VMEM((128, width), F32),
            pltpu.VMEM((16, LANES), F32),
        ],
        compiler_params=params(),
        cost_estimate=cost(flops, 4 * width * columns),
        name="last_rows",
    )(index, *arrays)


def down_rows_kernel(index, left_ref, right_ref, out_ref):
    del index
    out_ref[0] = tdot(left_ref[...], right_ref[...]).astype(BF)


def down_rows(other, index, left, right):
    tokens, hidden = left.shape
    width = right.shape[1]
    shard = hidden // 4
    return pl.pallas_call(
        down_rows_kernel,
        grid_spec=pltpu.PrefetchScalarGridSpec(
            num_scalar_prefetch=1,
            grid=(2,),
            in_specs=[
                pl.BlockSpec((tokens, shard), lambda i, s: (0, s[0] ^ (2 * i + other))),
                pl.BlockSpec((tokens, width), lambda i, s: (0, 0)),
            ],
            out_specs=pl.BlockSpec((1, shard, width), lambda i, s: (i, 0, 0)),
        ),
        out_shape=struct((2, shard, width), BF),
        compiler_params=params(),
        cost_estimate=cost(tokens * width * hidden, 7e6),
        name="down_rows",
    )(index, left, right)


def on_device(
    tokens,
    layout_cells,
    pad_mask,
    query_weight,
    key_weight,
    value_weight,
    out_weight,
    query_bias,
    value_bias,
    out_bias,
    bias_table,
    first_gain,
    first_shift,
    up_weight,
    up_bias,
    down_weight,
    down_bias,
    second_gain,
    second_shift,
    cotangent,
):
    rows, width = tokens.shape
    hidden = down_weight.shape[0] * 4
    shard = width // 4
    me = lax.axis_index("fsdp")
    parity = lax.axis_index("dp") & 1
    beside = (lax.axis_index("dp") >> 1) & 1
    index = jnp.stack([me, parity, beside]).astype(jnp.int32)
    factor = 1.0 / math.sqrt(rows * lax.axis_size("dp") * lax.axis_size("fsdp"))

    vectors = (
        query_bias, value_bias, out_bias, first_gain, first_shift, down_bias, second_gain,
        second_shift,
    )
    pack = pack_vectors(vectors, up_bias, bias_table)
    chain = lambda *args: Chain(send_once(*args))
    packs = [chain(pack, "fsdp", bit) for bit in (1, 2, 3)]

    side = jnp.concatenate
    qkv_shard = side([query_weight, key_weight, value_weight], axis=1)
    up_shard = side([out_weight, up_weight], axis=1)
    qkv_far = Chain(gather_far(qkv_shard, parity, 1))
    qkv_core = chain(qkv_shard, "fsdp", 1)
    up_far = Chain(gather_far(up_shard, parity, 1))
    up_core = chain(up_shard, "fsdp", 1)
    down_far = Chain(gather_far(down_weight, beside, 2))
    down_core = chain(down_weight, "fsdp", 1)
    run(None, (), packs + [qkv_core, qkv_far])
    extra, ke, ket, oh, near_t, smalls, full_up_bias = run(
        lambda *a: prepare(index, [pack] + [p.result for p in packs], *a),
        (layout_cells, pad_mask),
        [qkv_far, up_far],
        [qkv_far],
    )
    cores = [chain(part, "fsdp", 1) for part in qkv_far.result]
    run(None, (), cores + [up_core, down_core], cores)
    qkv_parts = (qkv_shard, qkv_core.result, *qkv_far.result, *(c.result for c in cores))
    qkv = run(
        lambda *a: project(index, qkv_parts, *a), (tokens, smalls), [down_far], [up_core, up_far]
    )
    mixed = None
    moves = (([up_far], [down_core]), ([], [down_far]), ([down_far], [up_far]))
    for group, (begin, finish) in zip(GROUPS, moves):
        old = () if mixed is None else (mixed,)
        mixed, extra = run(
            lambda *a: attend(group, *a), (qkv, extra, ke, near_t) + old, begin, finish
        )
    cores = [chain(part, "fsdp", 1) for part in up_far.result]
    run(None, (), cores, cores)
    up_parts = (up_shard, up_core.result, *up_far.result, *(c.result for c in cores))
    active, slope, normed, resid = run(
        lambda *a: go_up(index, up_parts, *a),
        (mixed, tokens, smalls, full_up_bias),
        [],
        [down_far],
    )
    cores = [chain(part, "fsdp", 1) for part in down_far.result]
    run(None, (), cores)
    down_parts = (down_weight, down_core.result, *down_far.result, *(c.result for c in cores))
    result, dfinal, dbranch, sums_two = run(
        lambda *a: go_down(index, down_parts, *a), (active, resid, cotangent, smalls)
    )

    down_send = run(functools.partial(down_rows, 1), (index, active, dbranch))
    core = chain(down_send, "fsdp", 1)
    down_keep = run(functools.partial(down_rows, 0), (index, active, dbranch), [core])
    down_sum = Chain(reduce_steps(down_keep, down_send, factor))
    down_sum.advance(core.result)
    dhidden, dresid, dattn, dmixed, sums_one, up_sums = run(
        lambda *a: backward(index, up_parts, down_parts, *a),
        (dbranch, slope, dfinal, resid, smalls),
        [down_sum],
    )
    up_rows = run(
        lambda left, right: weight_rows(index, left, (right,), 768), (normed, dhidden), [down_sum]
    )
    up_sum = Chain(reduce_steps(*up_rows, factor))
    out_rows = run(
        lambda left, right: weight_rows(index, left, (right,)), (mixed, dattn), [up_sum]
    )
    out_sum = Chain(reduce_steps(*out_rows, factor))

    def back(at, begin, finish):
        return run(
            lambda *a: attend_back(GROUPS[at], *a),
            (qkv, extra, ke, ket, oh, near_t, dmixed, mixed),
            begin,
            finish,
        )

    backs = [back(0, [up_sum, down_sum], [down_sum])]
    backs.append(back(1, [down_sum, out_sum], [down_sum, out_sum]))
    early = [array for at in range(3) for array in (backs[0][at], backs[1][at])]
    early_rows = run(
        lambda x, grads: weight_rows(index, x, grads),
        (tokens, early),
        [down_sum, out_sum],
        [up_sum, down_sum],
    )
    early_sum = Chain(reduce_steps(*early_rows, factor))
    backs.append(
        back(2, [up_sum, down_sum, early_sum], [early_sum, out_sum, up_sum, down_sum])
    )
    late_rows = run(
        lambda *a: last_rows(index, *a),
        (tokens, backs[2][:3], [group[3:] for group in backs], sums_one, sums_two, up_sums),
        [early_sum, up_sum, out_sum],
        [up_sum, out_sum],
    )
    late_sum = Chain(reduce_steps(*late_rows, factor))
    late = [array for group in backs for array in group[:3]]
    input_grad = run(
        lambda *a: input_gradient(index, qkv_parts, *a),
        (late, dresid),
        [late_sum, up_sum, out_sum],
        [late_sum, up_sum, early_sum, out_sum],
    )
    chains = [late_sum, early_sum, up_sum, out_sum, down_sum]
    while any(c.result is None for c in chains):
        run(None, (), [c for c in chains if c.result is None])
    thirds = [[] for _ in range(3)]
    for total, columns in ((early_sum.result, 512), (late_sum.result, 256)):
        for at in range(3):
            thirds[at].append(total[:, at * columns : at * columns + columns])
    grad_query, grad_key, grad_value = (side(third, axis=1) for third in thirds)
    tail = late_sum.result[:, width:].T
    return (
        result,
        input_grad,
        grad_query,
        grad_key,
        grad_value,
        out_sum.result,
        tail[0],
        tail[1],
        tail[2],
        tail[12:14].reshape(-1)[: 3 * 96].reshape(3, 96),
        tail[3],
        tail[4],
        up_sum.result,
        tail[8:12].reshape(-1),
        down_sum.result,
        tail[5],
        tail[6],
        tail[7],
    )


def solution(mesh):
    rows = P(("dp", "fsdp"), None)
    matrix, vector = P("fsdp", None), P("fsdp")
    return jax.shard_map(
        on_device,
        mesh=mesh,
        in_specs=(
            rows, P(None, ("dp", "fsdp")), P(("dp", "fsdp")),
            matrix, matrix, matrix, matrix,
            vector, vector, vector, matrix, vector, vector,
            matrix, vector, matrix, vector, vector, vector,
            rows,
        ),
        out_specs=(
            rows, rows,
            matrix, matrix, matrix, matrix,
            vector, vector, vector, matrix, vector, vector,
            matrix, vector, matrix, vector, vector, vector,
        ),
        check_vma=False,
    )
```

```python
import functools
import math

import jax
import jax.numpy as jnp
import numpy as np
from jax import lax
from jax.experimental import pallas as pl
from jax.experimental.pallas import tpu as pltpu
from jax.sharding import PartitionSpec as P

HEADS = 12
HD = 64
WIN = 512
BUCKETS = 32
PAIRS = HEADS // 2
SCALE = HD ** (-0.5)
EPS = 1e-05
BF = jnp.bfloat16
F32 = jnp.float32
VMEM_LIMIT = 60 * 1024 * 1024
GROUPS = ((0, 2), (2, 2), (4, 2))
FORWARD_GROUPS = ((0, 3), (3, 3))


def params():
    return pltpu.CompilerParams(vmem_limit_bytes=VMEM_LIMIT)


def cost(flops, nbytes, transcendentals=0):
    return pl.CostEstimate(
        flops=int(flops / 100),
        bytes_accessed=int(nbytes / 100),
        transcendentals=int(transcendentals / 100),
    )


def struct(shape, dtype):
    return jax.ShapeDtypeStruct(shape, dtype)


def whole(array):
    return pl.BlockSpec(array.shape, lambda *at: (0,) * len(array.shape))


def dot(left, right):
    return lax.dot_general(left, right, (((1,), (0,)), ((), ())), preferred_element_type=F32)


def dot_t(left, right):
    return lax.dot_general(left, right, (((1,), (1,)), ((), ())), preferred_element_type=F32)


def tdot(left, right):
    return lax.dot_general(left, right, (((0,), (0,)), ((), ())), preferred_element_type=F32)


def split3(values):
    high = values.astype(BF)
    rest = values - high.astype(F32)
    middle = rest.astype(BF)
    return high, middle, (rest - middle.astype(F32)).astype(BF)


def swap(array, axis, bit):
    return lax.ppermute(array, axis, [(i, i ^ bit) for i in range(lax.axis_size(axis))])


def together(*groups):
    flat, tree = jax.tree.flatten(groups)
    return jax.tree.unflatten(tree, lax.optimization_barrier(tuple(flat)))


def half_of(array, which, axis=0):
    rows = array.shape[axis] // 2
    return lax.dynamic_slice_in_dim(array, which * rows, rows, axis)


class Chain:
    def __init__(self, steps):
        self.steps = steps
        self.result = None
        self.move = next(steps)

    def advance(self, arrived):
        try:
            self.move = self.steps.send(arrived)
        except StopIteration as stop:
            self.move, self.result = None, stop.value


def run(call, arrays, begin=(), finish=None):
    finish = begin if finish is None else finish
    arrays, sent = together(arrays, [chain.move[0] for chain in begin])
    for chain, array in zip(begin, sent):
        chain.flight = swap(array, chain.move[1], chain.move[2])
    out = call(*arrays) if call is not None else ()
    out, arrived = together(out, [chain.flight for chain in finish])
    for chain, array in zip(finish, arrived):
        chain.advance(array)
    return out


def gather_far(piece, bit):
    far = yield piece, "fsdp", 2
    beside = yield far, "dp", bit
    return far, beside


def send_once(array, axis, bit):
    arrived = yield array, axis, bit
    return arrived


def part_rows(me, which, rows, pieces):
    half = rows // 2
    count = half // pieces
    places = [(me * rows, rows), ((me ^ 1) * rows, rows)]
    for piece in range(pieces):
        for other in (2, 3):
            for side in (which, 1 - which):
                places.append(((me ^ other) * rows + side * half + piece * count, count))
    return places


PARTS, BIG_PARTS = 6, 10


def fetch_copies(index, which, parts, whole, sems):
    rows = whole.shape[0] // 4
    places = part_rows(index[0], index[which], rows, (len(parts) - 2) // 4)
    return [
        pltpu.make_async_copy(part, whole.at[pl.ds(pl.multiple_of(first, 16), count)], sems.at[at])
        for at, (part, (first, count)) in enumerate(zip(parts, places))
    ]


def start_copies(copies):
    for copy in copies:
        copy.start()


def wait_copies(copies):
    for copy in copies:
        copy.wait()


ANY = pl.BlockSpec(memory_space=pl.ANY)
SMEM = pl.BlockSpec(memory_space=pltpu.SMEM)


def reduce_steps(keep, send, near_first=False):
    place = lax.axis_index("dp")
    near, beside = place & 1, (place >> 1) & 1

    def add(*arrays):
        return functools.reduce(jnp.add, [array.astype(F32) for array in arrays]).astype(BF)

    def half(which, arrays, axis=0):
        return add(*(half_of(array, which, axis) for array in arrays))

    got = yield send, "fsdp", 1
    if near_first:
        other = yield half(1 - near, (keep, got), 1), "dp", 1
        mine = half(near, (keep, got), 1)
        far = yield add(mine[1], other[1]), "fsdp", 2
        terms = (mine[0], other[0], far)
    else:
        far = yield add(keep[1], got[1]), "fsdp", 2
        terms = (keep[0], got[0], far)
        got = yield half(1 - near, terms), "dp", 1
        terms = (half(near, terms), got)
    got = yield half(1 - beside, terms), "dp", 2
    total = add(half(beside, terms), got)
    bit = 4
    while bit < lax.axis_size("dp"):
        got = yield total, "dp", bit
        total = add(total, got)
        bit *= 2
    got = yield total, "dp", 2
    total = in_order(total, got, beside)
    got = yield total, "dp", 1
    return total, got


def in_order(mine, other, which):
    return jnp.where(
        which == 0, jnp.concatenate([mine, other]), jnp.concatenate([other, mine])
    )


def table_places():
    step = np.arange(128)
    step = np.where(step < 64, -step, 128 - step)
    near = np.clip(step, -16, 15) + 16
    far = np.where(step <= -2, 0, np.where(step >= 2, 31, -1))
    wide = np.arange(256)
    wide = np.where(wide < 128, -wide, 256 - wide)
    places = np.concatenate([near + 32, near + 64, far, np.clip(wide, -16, 15) + 16])
    return places.astype(np.int32)[None, :]


def diagonal_places():
    lane = np.arange(128)
    x_place = np.where(lane < 63, np.clip(lane - 31, -16, 15) + 48, -1)
    y_place = np.where((lane >= 32) & (lane < 95), np.clip(lane - 63, -16, 15) + 80, -1)
    step = lane - 95
    block_place = np.where(
        (lane >= 64) & (step <= -2), 0, np.where((lane < 127) & (step >= 2), 31, -1)
    )
    step = (127 - np.arange(256) + 128) % 256 - 128
    places = np.concatenate([x_place, y_place, block_place, np.clip(step, -16, 15) + 16])
    return places.astype(np.int32)[:, None]


LANES = 640


def iota(shape, axis):
    return lax.broadcasted_iota(jnp.int32, shape, axis)


def as_bf(mask):
    return jnp.where(mask, 1.0, 0.0).astype(BF)


def near_mask():
    r, c = iota((128, 256), 0), iota((128, 256), 1)
    gap = (r >> 4) - (c >> 4)
    inside = (c < 128) & (gap <= 1) & (gap >= -1)
    return inside | ((r >= 112) & (c >= 128) & (c < 144)) | ((r < 16) & (c >= 240))


def hot_places(x, y, shape, axis):
    column = iota(shape, axis)
    block = (iota(shape, 1 - axis) & (WIN - 1)) >> 4
    third = column >> 5
    hot = jnp.where(third == 0, x, jnp.where(third == 1, y + 32, block + 64)) == column
    return column, hot & (column < 96)


PACK_ROWS, UP_ROW, TABLE_ROW = 16, 8, 10


def pack_vectors(vectors, up_bias, table):
    width, shard = up_bias.shape[0], vectors[0].shape[0]
    row = lax.broadcasted_iota(jnp.int32, (PACK_ROWS, shard), 0)
    pack = jnp.zeros((PACK_ROWS, shard), BF)
    for at, vector in enumerate(vectors):
        pack = jnp.where(row == at, vector[None, :], pack)
    pack = jnp.pad(pack, ((0, 0), (0, width - shard)))
    row = lax.broadcasted_iota(jnp.int32, (PACK_ROWS, width), 0)
    pack = jnp.where(row == UP_ROW, up_bias[None, :], pack)
    below = PACK_ROWS - TABLE_ROW - table.shape[0]
    return pack + jnp.pad(table, ((TABLE_ROW, below), (0, width - table.shape[1])))


def prep_kernel(
    index, p0, p1, p2, p3, cells_ref, mask_ref, places_ref,
    w_ref, own_ref, ke_ref, oh_ref, dt_ref, vectors_ref, up_bias_ref, packs,
):
    tokens = cells_ref.shape[1]
    me = index[0]
    for at, ref in enumerate((p0, p1, p2, p3)):
        packs[at] = ref[...]
    vectors = 0.0
    width = vectors_ref.shape[1]
    for at in range(4):
        rows = packs[me ^ at].astype(F32)
        vectors = vectors + pltpu.roll(rows[:8], at * (width // 4), 1)
        up_bias_ref[:, at * width : at * width + width] = rows[UP_ROW : UP_ROW + 1]
    vectors_ref[...] = vectors
    x, y, valid = cells_ref[0:1, :], cells_ref[1:2, :], mask_ref[...]
    column, hot = hot_places(x, y, (128, tokens), 0)
    own_ref[...] = as_bf(hot | (column == 96))
    sub = iota((8, tokens), 0)
    columns = jnp.where(sub == 0, x, jnp.where(sub == 1, y, valid)).astype(F32)
    columns = columns.T.astype(jnp.int32)
    x, y, valid = columns[:, 0:1], columns[:, 1:2], columns[:, 2:3]
    column, hot = hot_places(x, y, (tokens, 128), 1)
    masked = jnp.where((column == 99) & (valid <= 0), -1e30, 0.0)
    ones = hot | ((column >= 96) & (column < 99))
    ke_ref[...] = jnp.where(ones, 1.0, masked).astype(BF)
    block = (iota((tokens, 128), 0) & (WIN - 1)) >> 4
    third = column >> 5
    back = jnp.where(third == 0, 31 - x, jnp.where(third == 1, 63 - y, 95 - block)) == column
    oh_ref[...] = as_bf(back & (column < 96))

    pick = as_bf(iota((128, LANES), 0) == places_ref[...])
    lane = iota((32, 128), 1)
    mask = near_mask()
    for part in range(4):
        table = dot(packs[me ^ part][:, :128], pick)
        for head in range(HEADS // 4):
            row = table[TABLE_ROW + head : TABLE_ROW + head + 1]
            blocks = []
            for at in range(3):
                spread = jnp.broadcast_to(row[:, at * 128 : at * 128 + 128], (32, 128))
                spread = pltpu.roll(spread, at * 32, 1, stride=1, stride_axis=0)
                blocks.append(jnp.where(lane >> 5 == at, spread, 0.0))
            blocks.append(jnp.where((iota((32, 128), 0) == 3) & (lane == 96), 1.0, 0.0))
            place = part * (HEADS // 4) + head
            w_ref[place] = jnp.concatenate(blocks, axis=0).astype(BF)
            wide = jnp.broadcast_to(row[:, 384:640], (128, 256))
            rolled = pltpu.roll(wide, 0, 1, stride=1, stride_axis=0)
            dt_ref[place] = jnp.where(mask, rolled, 0.0).astype(BF)


def prepare(index, packs, layout_cells, pad_mask):
    tokens = pad_mask.shape[0]
    width = packs[0].shape[1]
    shapes = [
        struct((HEADS, 128, 128), BF),
        struct((128, tokens), BF),
        struct((tokens, 128), BF),
        struct((tokens, 128), BF),
        struct((HEADS, 128, 256), BF),
        struct((8, width), F32),
        struct((1, 4 * width), F32),
    ]
    arrays = [*packs, layout_cells, pad_mask.reshape(1, tokens), jnp.asarray(table_places())]
    return pl.pallas_call(
        prep_kernel,
        grid=(1,),
        in_specs=[SMEM] + [whole(array) for array in arrays],
        out_specs=[whole(shape) for shape in shapes],
        out_shape=shapes,
        scratch_shapes=[pltpu.VMEM((4, PACK_ROWS, width), BF)],
        compiler_params=params(),
        cost_estimate=cost(1e7, 3e6),
        name="prepare",
    )(index, *arrays)


def project_kernel(index, *refs):
    parts, (x_ref, bias_ref, out_ref, weight, sems) = refs[:PARTS], refs[PARTS:]

    @pl.when(pl.program_id(0) == 0)
    def _():
        copies = fetch_copies(index, 1, parts, weight, sems)
        start_copies(copies)
        wait_copies(copies)

    width = x_ref.shape[1]
    for at in range(3):
        values = dot(x_ref[...], weight[:, at * width : (at + 1) * width])
        if at == 0:
            values = (values + bias_ref[0:1, :]).astype(BF) * SCALE
        if at == 2:
            values = values + bias_ref[1:2, :]
        values = values.astype(BF)
        for pair in range(PAIRS):
            out_ref[at * PAIRS + pair] = values[:, pair * 128 : pair * 128 + 128]


def project(index, parts, tokens, biases, block=512):
    rows, width = tokens.shape
    return pl.pallas_call(
        project_kernel,
        grid=(rows // block,),
        in_specs=[SMEM]
        + [ANY] * PARTS
        + [
            pl.BlockSpec((block, width), lambda i: (i, 0)),
            pl.BlockSpec((8, width), lambda i: (0, 0)),
        ],
        out_specs=pl.BlockSpec((3 * PAIRS, block, 128), lambda i: (0, i, 0)),
        out_shape=struct((3 * PAIRS, rows, 128), BF),
        scratch_shapes=[pltpu.VMEM((width, 3 * width), BF), pltpu.SemaphoreType.DMA((PARTS,))],
        compiler_params=params(),
        cost_estimate=cost(6 * rows * width * width, 10e6),
        name="project",
    )(index, *parts, tokens, biases)


def join(ref):
    return jnp.concatenate([ref[at] for at in range(ref.shape[0])], axis=1)


def input_kernel(index, *refs):
    count = len(GROUPS) * 3
    parts, grads = refs[:PARTS], refs[PARTS : PARTS + count]
    dresid_ref, out_ref, weight, sems = refs[PARTS + count :]

    @pl.when(pl.program_id(0) == 0)
    def _():
        copies = fetch_copies(index, 1, parts, weight, sems)
        start_copies(copies)
        wait_copies(copies)

    joined = [join(grads[3 * group + at]) for at in range(3) for group in range(len(GROUPS))]
    total = dot_t(jnp.concatenate(joined, axis=1), weight[...])
    out_ref[...] = (dresid_ref[...] + total).astype(BF)


def input_gradient(index, parts, grads, dresid, block=256):
    rows, width = dresid.shape
    spec = pl.BlockSpec((block, width), lambda i: (i, 0))
    pairs = [pl.BlockSpec((a.shape[0], block, 128), lambda i: (0, i, 0)) for a in grads]
    return pl.pallas_call(
        input_kernel,
        grid=(rows // block,),
        in_specs=[SMEM] + [ANY] * PARTS + pairs + [spec],
        out_specs=spec,
        out_shape=struct((rows, width), BF),
        scratch_shapes=[pltpu.VMEM((width, 3 * width), BF), pltpu.SemaphoreType.DMA((PARTS,))],
        compiler_params=params(),
        cost_estimate=cost(6 * rows * width * width, 13e6),
        name="input_gradient",
    )(index, *parts, *grads, dresid)


def with_near(pieces, tile, at):
    pieces = list(pieces)
    pieces[at] = pieces[at] + tile[:, :128]
    if at > 0:
        left = pieces[at - 1]
        pieces[at - 1] = jnp.concatenate([left[:16] + tile[:16, 128:], left[16:]], axis=0)
    if at < 3:
        right = pieces[at + 1]
        pieces[at + 1] = jnp.concatenate([right[:112], right[112:] + tile[112:, 128:]], axis=0)
    return pieces


def lane_blocks(values):
    return [values[:, c * 128 : c * 128 + 128] for c in range(WIN // 128)]


def attend_kernel(
    q_ref, k_ref, v_ref, w_ref, own_ref, ke_ref, dt_ref, out_ref, lse_ref, s_scr, p_scr
):
    first = iota((128, WIN), 0) < HD
    windows = [slice(at, at + WIN) for at in range(0, q_ref.shape[0], WIN)]
    values = []
    for at, rows in enumerate(windows):
        keys = jnp.concatenate([k_ref[rows, :], ke_ref[rows, :]], axis=1)
        query_t = q_ref[rows, :].T
        values.append(v_ref[rows, :].T)
        for head in range(2):
            mine = first if head == 0 else ~first
            query = jnp.where(mine, query_t, jnp.zeros((), BF))
            extra = dot(w_ref[head], own_ref[:, rows]).astype(BF)
            s_scr[2 * at + head] = dot(keys, jnp.concatenate([query, extra], axis=0))
    for at, rows in enumerate(windows):
        mixed = []
        for head in range(2):
            place = 2 * at + head
            tile = dt_ref[head].astype(F32)
            scores = [
                with_near(lane_blocks(s_scr[place, row : row + 128, :]), tile, row // 128)
                for row in range(0, WIN, 128)
            ]
            tops, totals = [], []
            for column in range(WIN // 128):
                pieces = [row[column] for row in scores]
                top = jnp.maximum(
                    jnp.maximum(pieces[0], pieces[1]), jnp.maximum(pieces[2], pieces[3])
                )
                top = jnp.max(top, axis=0, keepdims=True)
                pieces = [jnp.exp(piece - top) for piece in pieces]
                total = (pieces[0] + pieces[1]) + (pieces[2] + pieces[3])
                totals.append(jnp.sum(total, axis=0, keepdims=True))
                tops.append(top)
                span = slice(column * 128, column * 128 + 128)
                for row, piece in enumerate(pieces):
                    p_scr[place, row * 128 : row * 128 + 128, span] = piece.astype(BF)
            total = jnp.concatenate(totals, axis=1)
            mixed.append(dot(values[at][head * HD : head * HD + HD], p_scr[place]) / total)
            lse_ref[head : head + 1, rows] = jnp.concatenate(tops, axis=1) + jnp.log(total)
        out_ref[rows, :] = jnp.concatenate(mixed, axis=0).astype(BF).T


def pair_block(tokens, shift):
    return pl.BlockSpec((None, tokens, 128), lambda p: (p + shift, 0, 0))


def attend(group, qkv, w, own, ke, near_t, old=()):
    start, pairs = group
    tokens = qkv.shape[1]
    scores = 2 * (tokens // WIN)
    kernel = attend_kernel
    if old:
        kernel = lambda *refs: attend_kernel(*refs[:7], *refs[9:])
    return pl.pallas_call(
        kernel,
        grid=(pairs,),
        in_specs=[
            pair_block(tokens, start),
            pair_block(tokens, start + PAIRS),
            pair_block(tokens, start + 2 * PAIRS),
            pl.BlockSpec((2, 128, 128), lambda p: (p + start, 0, 0)),
            whole(own),
            whole(ke),
            pl.BlockSpec((2, 128, 256), lambda p: (p + start, 0, 0)),
        ]
        + [ANY] * len(old),
        out_specs=[
            pair_block(tokens, start),
            pl.BlockSpec((None, 8, tokens), lambda p: (p + start, 0, 0)),
        ],
        out_shape=[struct((PAIRS, tokens, 128), BF), struct((PAIRS, 8, tokens), F32)],
        input_output_aliases={7: 0, 8: 1} if old else {},
        scratch_shapes=[pltpu.VMEM((scores, WIN, WIN), F32), pltpu.VMEM((scores, WIN, WIN), BF)],
        compiler_params=params(),
        cost_estimate=cost(tokens * WIN * pairs * 1536, 4e6 * pairs / 2, tokens * WIN * 2 * pairs),
        name="attend",
    )(qkv, qkv, qkv, w, own, ke, near_t, *old)


def diagonal_rows(sums):
    lane = iota((32, 128), 1)
    rows = []
    for at in range(3):
        block = jnp.where(lane >> 5 == at, sums[at * 32 : at * 32 + 32], 0.0)
        rolled = pltpu.roll(block, 0, 1, stride=1, stride_axis=0)
        rows.append(jnp.sum(rolled, axis=0, keepdims=True))
    return rows


def near_rows(tile):
    tile = jnp.where(near_mask(), tile, 0.0)
    turn = as_bf(iota((128, 128), 0) + iota((128, 128), 1) == 127)
    high, middle, low = split3(tile)
    turned = dot(turn, high) + dot(turn, middle) + dot(turn, low)
    rolled = pltpu.roll(turned, 0, 1, stride=1, stride_axis=0)
    return jnp.sum(rolled, axis=0, keepdims=True)


def attend_back_kernel(
    index, q_ref, k_ref, v_ref, w_ref, own_ref, ke_ref, oh_ref, dt_ref, do_ref, o_ref, lse_ref,
    x_ref, dq_ref, dk_ref, dv_ref, bias_ref, far_ref, near_ref, keep_ref, send_ref,
    s_scr, dp_scr, p_scr, ds_scr, x_t, products,
):
    @pl.when(pl.program_id(0) == 0)
    def _():
        x_t[...] = x_ref[...].T

    zero = jnp.zeros((), BF)
    first = iota((WIN, 128), 1) < HD
    first_t = iota((128, WIN), 0) < HD
    place = iota((128, WIN), 0)
    windows = [slice(at, at + WIN) for at in range(0, q_ref.shape[0], WIN)]
    keys_t = []
    for at, rows in enumerate(windows):
        keys = jnp.concatenate([k_ref[rows, :], ke_ref[rows, :]], axis=1)
        values = jnp.concatenate([v_ref[rows, :], ke_ref[rows, :]], axis=1)
        keys_t.append(k_ref[rows, :].T)
        query_t, grad_t = q_ref[rows, :].T, do_ref[rows, :].T
        product = grad_t.astype(F32) * o_ref[rows, :].T.astype(F32)
        for head in range(2):
            mine = first_t if head == 0 else ~first_t
            delta = -jnp.sum(product[head * HD : head * HD + HD], axis=0, keepdims=True)
            minus = jnp.zeros((128, WIN), BF)
            extra = dot(w_ref[head], own_ref[:, rows]).astype(BF)
            parts = split3(-lse_ref[head : head + 1, rows])
            for part, (less, less_delta) in enumerate(zip(parts, split3(delta))):
                extra = jnp.where(place == 96 + part, less, extra)
                minus = jnp.where(place == 96 + part, less_delta, minus)
            query = jnp.where(mine, query_t, zero)
            grad = jnp.where(mine, grad_t, zero)
            s_scr[2 * at + head] = dot(keys, jnp.concatenate([query, extra], axis=0))
            dp_scr[2 * at + head] = dot(values, jnp.concatenate([grad, minus], axis=0))
    plus = lambda total, term: term if total is None else total + term
    far, diag, low, high = None, [None] * 2, [None] * 2, [None] * 2
    bias_sums = [None] * 2
    for at, rows in enumerate(windows):
        dq_t, extras, dk, dv = [], [], None, None
        for head in range(2):
            mine = first if head == 0 else ~first
            query = jnp.where(mine, q_ref[rows, :], zero)
            grad = jnp.where(mine, do_ref[rows, :], zero)
            tile = dt_ref[head].astype(F32)
            place = 2 * at + head
            for block in range(WIN // 128):
                span = slice(block * 128, block * 128 + 128)
                scores = with_near(lane_blocks(s_scr[place, span, :]), tile, block)
                probs = [jnp.exp(piece) for piece in scores]
                dprobs = lane_blocks(dp_scr[place, span, :])
                dscores = [a * b for a, b in zip(probs, dprobs)]
                p_scr[place, span, :] = jnp.concatenate([a.astype(BF) for a in probs], axis=1)
                ds_scr[place, span, :] = jnp.concatenate([a.astype(BF) for a in dscores], axis=1)
                diag[head] = plus(diag[head], dscores[block])
                if block > 0:
                    low[head] = plus(low[head], dscores[block - 1][:16])
                if block < 3:
                    high[head] = plus(high[head], dscores[block + 1][112:])
            dv = plus(dv, dot(p_scr[place], grad))
            dk = plus(dk, dot(ds_scr[place], query))
            left = jnp.concatenate(
                [keys_t[at][head * HD : head * HD + HD], own_ref[:96, rows]], axis=0
            )
            both = dot(left, ds_scr[place])
            dq_t.append(both[:HD] * SCALE)
            extras.append(both[HD:].astype(BF))
        far = plus(far, dot(jnp.concatenate(extras, axis=0), oh_ref[rows, :]))
        dq = jnp.concatenate(dq_t, axis=0).astype(BF).T
        dv = dv.astype(BF)
        dq_ref[rows, :] = dq
        dk_ref[rows, :] = dk.astype(BF)
        dv_ref[rows, :] = dv
        for which, array in enumerate((dq, dv)):
            total = jnp.sum(array.astype(F32), axis=0, keepdims=True)
            bias_sums[which] = plus(bias_sums[which], total)
    grads = jnp.concatenate([dq_ref[...], dk_ref[...], dv_ref[...]], axis=1)
    products[...] = dot(x_t[...], grads)
    place_rows(index, products, keep_ref, send_ref)
    bias_ref[...] = jnp.zeros_like(bias_ref)
    for which in range(2):
        bias_ref[which : which + 1, :] = bias_sums[which]
    for head in range(2):
        sums = diagonal_rows(far[head * 96 : head * 96 + 96])
        far_ref[head] = jnp.concatenate(sums + [jnp.zeros((5, 128), F32)], axis=0)
        corners = jnp.concatenate([low[head], jnp.zeros((96, 128), F32), high[head]], axis=0)
        tile = jnp.concatenate([diag[head], corners], axis=1)
        near_ref[head] = jnp.broadcast_to(near_rows(tile), (8, 256))


def attend_back(
    group, room, index, qkv, w, own, ke, oh, near_t, dmixed, mixed, lse, x, old=()
):
    start, pairs = group
    kernel = attend_back_kernel
    if old:
        kernel = lambda *refs: attend_back_kernel(*refs[:13], *refs[15:])
    tokens, width = x.shape
    scores = 2 * (tokens // WIN)
    out = struct((pairs, tokens, 128), BF)
    weight_rows = struct((2, width // 4, room), BF)
    weight_block = pl.BlockSpec(
        (2, width // 4, 384), lambda p: (0, 0, p + (start if old else 0))
    )
    return pl.pallas_call(
        kernel,
        grid=(pairs,),
        in_specs=[
            SMEM,
            pair_block(tokens, start),
            pair_block(tokens, start + PAIRS),
            pair_block(tokens, start + 2 * PAIRS),
            pl.BlockSpec((2, 128, 128), lambda p: (p + start, 0, 0)),
            whole(own),
            whole(ke),
            whole(oh),
            pl.BlockSpec((2, 128, 256), lambda p: (p + start, 0, 0)),
            pair_block(tokens, start),
            pair_block(tokens, start),
            pl.BlockSpec((None, 8, tokens), lambda p: (p + start, 0, 0)),
            whole(x),
        ]
        + [ANY] * len(old),
        out_specs=[
            pair_block(tokens, 0),
            pair_block(tokens, 0),
            pair_block(tokens, 0),
            pl.BlockSpec((None, 8, 128), lambda p: (p, 0, 0)),
            pl.BlockSpec((2, 8, 128), lambda p: (p, 0, 0)),
            pl.BlockSpec((2, 8, 256), lambda p: (p, 0, 0)),
            weight_block,
            weight_block,
        ],
        out_shape=[
            out,
            out,
            out,
            struct((pairs, 8, 128), F32),
            struct((2 * pairs, 8, 128), F32),
            struct((2 * pairs, 8, 256), F32),
            weight_rows,
            weight_rows,
        ],
        input_output_aliases={13: 6, 14: 7} if old else {},
        scratch_shapes=[
            pltpu.VMEM((scores, WIN, WIN), F32),
            pltpu.VMEM((scores, WIN, WIN), F32),
            pltpu.VMEM((scores, WIN, WIN), BF),
            pltpu.VMEM((scores, WIN, WIN), BF),
            pltpu.VMEM((width, tokens), BF),
            pltpu.VMEM((width, 384), F32),
        ],
        compiler_params=params(),
        cost_estimate=cost(
            tokens * WIN * pairs * 2 * 2048, 12e6, tokens * WIN * pairs * 2
        ),
        name="attend_back",
    )(index, qkv, qkv, qkv, w, own, ke, oh, near_t, dmixed, mixed, lse, x, *old)


def norm_parts(values):
    centre = values - jnp.mean(values, axis=-1, keepdims=True)
    spread = jnp.mean(centre * centre, axis=-1, keepdims=True)
    scale = lax.rsqrt(spread + EPS)
    return centre * scale, scale


def norm_back(grad, hat, scale):
    mean = jnp.mean(grad, axis=-1, keepdims=True)
    along = jnp.mean(grad * hat, axis=-1, keepdims=True)
    return scale * (grad - mean - hat * along)


def add_rows(ref, rows):
    for at, values in enumerate(rows):
        ref[at : at + 1, :] += jnp.sum(values.astype(F32), axis=0, keepdims=True)


def gelu_and_slope(values):
    upto = 0.5 + 0.5 * lax.erf(values * math.sqrt(0.5))
    density = jnp.exp(values * values * -0.5) * (1.0 / math.sqrt(2.0 * math.pi))
    return values * upto, upto + values * density


def store_rows(index, total, keep, send, stage, sems):
    me, shard = index[0], keep.shape[1]
    copies = []
    for at, (which, ref) in enumerate(((1, send), (3, send), (2, keep), (0, keep))):
        rows = pl.ds(pl.multiple_of((me ^ which) * shard, 16), shard)
        stage[at] = total[rows, :].astype(BF)
        copies.append(pltpu.make_async_copy(stage.at[at], ref.at[which // 2], sems.at[at]))
        copies[-1].start()
    return copies


def forward_kernel(index, *refs):
    up_parts, down_parts = refs[:BIG_PARTS], refs[BIG_PARTS : 2 * BIG_PARTS]
    (
        mixed_ref, x_ref, cot_ref, small_ref, up_bias_ref,
        out_ref, dfinal_ref, resid_ref, slope_ref, sums_ref, keep_ref, send_ref,
        w_up, w_down, total, active_scr, stage, sems, out_sems,
    ) = refs[2 * BIG_PARTS :]
    step = pl.program_id(0)
    up_copies = fetch_copies(index, 1, up_parts, w_up, sems.at[0])
    down_copies = fetch_copies(index, 2, down_parts, w_down, sems.at[1])

    @pl.when(step == 0)
    def _():
        start_copies(up_copies)
        start_copies(down_copies)
        for ref in (sums_ref, total):
            ref[...] = jnp.zeros_like(ref)
        wait_copies(up_copies)

    width, hidden = w_down.shape[1], w_down.shape[0]
    small = lambda at: small_ref[at + 2 : at + 3, :]
    resid = x_ref[...].astype(F32) + (dot(join(mixed_ref), w_up[:, :width]) + small(0))
    resid_ref[...] = resid
    hat, _ = norm_parts(resid)
    normed = hat * small(1) + small(2)
    low = normed.astype(BF)
    for at in range(0, hidden, width):
        span = slice(at, at + width)
        values = dot(low, w_up[:, at + width : at + 2 * width]) + up_bias_ref[:, span]
        active, slope = gelu_and_slope(values)
        active_scr[:, span] = active.astype(BF)
        slope_ref[:, span] = slope.astype(BF)

    @pl.when(step == 0)
    def _():
        wait_copies(down_copies)

    final = normed + dot(active_scr[...], w_down[...]) + small(3)
    hat, scale = norm_parts(final)
    out_ref[...] = (hat * small(4) + small(5)).astype(BF)
    cot = cot_ref[...].astype(F32)
    dfinal = norm_back(cot * small(4), hat, scale)
    dfinal_ref[...] = dfinal
    dbranch = dfinal.astype(BF)
    for at in range(0, hidden, width):
        total[at : at + width, :] += tdot(active_scr[:, at : at + width], dbranch)
    add_rows(sums_ref, (cot * hat, cot, dbranch))

    @pl.when(step == pl.num_programs(0) - 1)
    def _():
        wait_copies(store_rows(index, total, keep_ref, send_ref, stage, out_sems))


def forward(index, up_parts, down_parts, mixed, tokens, cotangent, smalls, up_bias, block=256):
    rows, width = tokens.shape
    hidden = up_bias.shape[1]
    spec = lambda columns: pl.BlockSpec((block, columns), lambda i: (i, 0))
    pairs = pl.BlockSpec((PAIRS, block, 128), lambda i: (0, i, 0))
    sums = struct((8, width), F32)
    down_rows = struct((2, hidden // 4, width), BF)
    return pl.pallas_call(
        forward_kernel,
        grid=(rows // block,),
        in_specs=[SMEM]
        + [ANY] * (2 * BIG_PARTS)
        + [pairs, spec(width), spec(width), whole(smalls), whole(up_bias)],
        out_specs=[spec(width), spec(width), spec(width), spec(hidden), whole(sums), ANY, ANY],
        out_shape=[
            struct((rows, width), BF),
            struct((rows, width), F32),
            struct((rows, width), F32),
            struct((rows, hidden), BF),
            sums,
            down_rows,
            down_rows,
        ],
        scratch_shapes=[
            pltpu.VMEM((width, width + hidden), BF),
            pltpu.VMEM((hidden, width), BF),
            pltpu.VMEM((hidden, width), F32),
            pltpu.VMEM((block, hidden), BF),
            pltpu.VMEM((4, hidden // 4, width), BF),
            pltpu.SemaphoreType.DMA((2, BIG_PARTS)),
            pltpu.SemaphoreType.DMA((4,)),
        ],
        compiler_params=params(),
        cost_estimate=cost(2 * rows * width * (width + 3 * hidden), 40e6),
        name="forward",
    )(index, *up_parts, *down_parts, mixed, tokens, cotangent, smalls, up_bias)


def backward_kernel(index, *refs):
    up_parts, down_parts = refs[:BIG_PARTS], refs[BIG_PARTS : 2 * BIG_PARTS]
    (
        dfinal_ref, resid_ref, slope_ref, mixed_ref, small_ref,
        dresid_ref, dmixed_ref, sums_ref, up_sums_ref, *row_refs,
        w_up, w_down, total, stage, sems, out_sems,
    ) = refs[2 * BIG_PARTS :]
    step = pl.program_id(0)

    @pl.when(step == 0)
    def _():
        copies = fetch_copies(index, 2, down_parts, w_down, sems.at[0])
        copies += fetch_copies(index, 1, up_parts, w_up, sems.at[1])
        start_copies(copies)
        for ref in (sums_ref, up_sums_ref, total):
            ref[...] = jnp.zeros_like(ref)
        wait_copies(copies)

    width, hidden = w_down.shape[1], w_down.shape[0]
    small = lambda at: small_ref[at + 2 : at + 3, :]
    hat, scale = norm_parts(resid_ref[...])
    low_t = (hat * small(1) + small(2)).astype(BF).T
    dnormed = dfinal_ref[...]
    dbranch = dnormed.astype(BF)
    for at in range(0, hidden, width):
        span = slice(at, at + width)
        up_span = slice(at + width, at + 2 * width)
        dactive = dot_t(dbranch, w_down[span, :])
        dhidden = (dactive * slope_ref[:, span].astype(F32)).astype(BF)
        up_sums_ref[:, span] += jnp.sum(dhidden.astype(F32), axis=0, keepdims=True)
        total[:, up_span] += dot(low_t, dhidden)
        dnormed = dnormed + dot_t(dhidden, w_up[:, up_span])
    dresid = norm_back(dnormed * small(1), hat, scale)
    dresid_ref[...] = dresid
    dattn = dresid.astype(BF)
    dmixed = dot_t(dattn, w_up[:, :width]).astype(BF)
    for pair in range(PAIRS):
        dmixed_ref[pair] = dmixed[:, pair * 128 : pair * 128 + 128]
    total[:, :width] += tdot(join(mixed_ref), dattn)
    add_rows(sums_ref, (dnormed * hat, dnormed, dattn))

    @pl.when(step == pl.num_programs(0) - 1)
    def _():
        half = (width + hidden) // 2
        for at in range(2):
            columns = slice(at * half, at * half + half)
            wait_copies(
                store_rows(
                    index,
                    total.at[:, columns],
                    *row_refs[2 * at : 2 * at + 2],
                    stage.at[:, :, columns],
                    out_sems,
                )
            )


def backward(index, up_parts, down_parts, dfinal, resid, slope, mixed, smalls, block=256):
    rows, width = resid.shape
    hidden = slope.shape[1]
    spec = lambda columns: pl.BlockSpec((block, columns), lambda i: (i, 0))
    pairs = pl.BlockSpec((PAIRS, block, 128), lambda i: (0, i, 0))
    sums = [struct((8, width), F32), struct((1, hidden), F32)]
    up_rows = struct((2, width // 4, (width + hidden) // 2), BF)
    return pl.pallas_call(
        backward_kernel,
        grid=(rows // block,),
        in_specs=[SMEM]
        + [ANY] * (2 * BIG_PARTS)
        + [spec(width), spec(width), spec(hidden), pairs, whole(smalls)],
        out_specs=[spec(width), pairs] + [whole(shape) for shape in sums] + [ANY] * 4,
        out_shape=[struct((rows, width), F32), struct((PAIRS, rows, 128), BF)]
        + sums
        + [up_rows] * 4,
        scratch_shapes=[
            pltpu.VMEM((width, width + hidden), BF),
            pltpu.VMEM((hidden, width), BF),
            pltpu.VMEM((width, width + hidden), F32),
            pltpu.VMEM((4, width // 4, width + hidden), BF),
            pltpu.SemaphoreType.DMA((2, BIG_PARTS)),
            pltpu.SemaphoreType.DMA((4,)),
        ],
        compiler_params=params(),
        cost_estimate=cost(4 * rows * width * (width + 2 * hidden), 40e6),
        name="backward",
    )(index, *up_parts, *down_parts, dfinal, resid, slope, mixed, smalls)


def place_rows(index, total, keep_ref, send_ref):
    me, shard = index[0], keep_ref.shape[1]
    for at, ref in ((0, keep_ref), (2, keep_ref), (1, send_ref), (3, send_ref)):
        rows = pl.ds(pl.multiple_of((me ^ at) * shard, 16), shard)
        ref[at // 2] = total[rows, :].astype(BF)


def small_rows(refs, places, sums_one, sums_two, up_sums, rows, sums):
    width = rows.shape[1]
    shard = width // 4
    rows[...] = jnp.zeros_like(rows)
    sums[...] = jnp.zeros_like(sums)
    pair, head = 0, 0
    for bias, far, near in refs:
        for at in range(bias.shape[0]):
            rows[0:2, pair * 128 : pair * 128 + 128] = bias[at, 0:2, :]
            pair += 1
        for at in range(far.shape[0]):
            parts = [far[at, row : row + 1, :] for row in range(3)] + [near[at, 0:1, :]]
            sums[head : head + 1, :] = jnp.concatenate(parts, axis=1)
            head += 1
    for row, source in enumerate((2, 0, 1)):
        rows[row + 2 : row + 3, :] = sums_one[source : source + 1, :]
        rows[row + 5 : row + 6, :] = sums_two[source : source + 1, :]
    lane = iota((1, width), 1)
    for at in range(4):
        values = up_sums[:, at * width : at * width + width]
        inside = (lane >= at * shard) & (lane < (at + 1) * shard)
        for part in range(4):
            rolled = pltpu.roll(values, (at - part) % 4 * shard, 1)
            rows[8 + part : 9 + part, :] += jnp.where(inside, rolled, 0.0)
    pick = as_bf(places[...] == iota((LANES, 128), 1))
    table = sum(dot(part, pick) for part in split3(sums[...]))
    table = jnp.concatenate([table, jnp.zeros((table.shape[0], width - 128), F32)], axis=1)
    for at in range(HEADS):
        within = at % 3
        shift = at // 3 * shard + within % 2 * 96
        rolled = pltpu.roll(table[at : at + 1], shift, 1)
        rows[12 + within // 2 : 13 + within // 2, :] += rolled


def small_kernel(count, index, *refs):
    groups, refs = refs[: 3 * count], refs[3 * count :]
    (
        places, sums_one, sums_two, up_sums, keep_in, send_in, keep_ref, send_ref, total, rows, sums
    ) = refs
    del keep_in, send_in
    groups = [groups[at : at + 3] for at in range(0, 3 * count, 3)]
    small_rows(groups, places, sums_one, sums_two, up_sums, rows, sums)
    total[...] = rows[...].T
    place_rows(index, total, keep_ref, send_ref)


def small_gradients(index, groups, sums_one, sums_two, up_sums, keep, send):
    width = sums_one.shape[1]
    block = keep.shape[2] // 128 - 1
    arrays = [array for group in groups for array in group]
    arrays += [jnp.asarray(diagonal_places()), sums_one, sums_two, up_sums]
    out = pl.BlockSpec((2, width // 4, 128), lambda i: (0, 0, block))
    return pl.pallas_call(
        functools.partial(small_kernel, len(groups)),
        grid=(1,),
        in_specs=[SMEM] + [whole(array) for array in arrays] + [ANY, ANY],
        out_specs=[out, out],
        out_shape=[struct(keep.shape, BF)] * 2,
        input_output_aliases={len(arrays) + 1: 0, len(arrays) + 2: 1},
        scratch_shapes=[
            pltpu.VMEM((width, 128), F32),
            pltpu.VMEM((128, width), F32),
            pltpu.VMEM((16, LANES), F32),
        ],
        compiler_params=params(),
        cost_estimate=cost(1e7, 1e6),
        name="small_gradients",
    )(index, *arrays, keep, send)


def unpack_kernel(factor, index, *refs):
    halves, (query_ref, key_ref, value_ref, small_ref, small_scr) = refs[:4], refs[4:]
    half = halves[0].shape[0]
    for at in range(2):
        rows = pl.ds(pl.multiple_of((index[1] ^ at) * half, 16), half)
        first = 0
        for ref in (halves[at], halves[2 + at]):
            for column in range(0, ref.shape[1] // 384 * 384, 384):
                for which, out in enumerate((query_ref, key_ref, value_ref)):
                    place = column + which * 128
                    values = ref[:, place : place + 128].astype(F32) * factor
                    out[rows, first : first + 128] = values
                first += 128
        values = halves[2 + at][:, halves[2].shape[1] - 128 :]
        small_scr[rows, :] = values.astype(F32) * factor
    small_ref[...] = small_scr[...].T


def unpack(index, early, late, factor):
    half, width = early[0].shape[0], PAIRS * 128
    arrays = [*early, *late]
    outs = [struct((2 * half, width), F32)] * 3 + [struct((128, 2 * half), F32)]
    return pl.pallas_call(
        functools.partial(unpack_kernel, factor),
        grid=(1,),
        in_specs=[SMEM] + [whole(array) for array in arrays],
        out_specs=[whole(shape) for shape in outs],
        out_shape=outs,
        scratch_shapes=[pltpu.VMEM((2 * half, 128), F32)],
        compiler_params=params(),
        cost_estimate=cost(1e6, 3e6),
        name="unpack",
    )(index, *arrays)


def on_device(
    tokens,
    layout_cells,
    pad_mask,
    query_weight,
    key_weight,
    value_weight,
    out_weight,
    query_bias,
    value_bias,
    out_bias,
    bias_table,
    first_gain,
    first_shift,
    up_weight,
    up_bias,
    down_weight,
    down_bias,
    second_gain,
    second_shift,
    cotangent,
):
    rows, width = tokens.shape
    hidden = down_weight.shape[0] * 4
    shard = width // 4
    me = lax.axis_index("fsdp")
    parity = lax.axis_index("dp") & 1
    beside = (lax.axis_index("dp") >> 1) & 1
    index = jnp.stack([me, parity, beside]).astype(jnp.int32)
    factor = 1.0 / math.sqrt(rows * lax.axis_size("dp") * lax.axis_size("fsdp"))

    vectors = (
        query_bias, value_bias, out_bias, first_gain, first_shift, down_bias, second_gain,
        second_shift,
    )
    pack = pack_vectors(vectors, up_bias, bias_table)
    chain = lambda *args: Chain(send_once(*args))

    side = jnp.concatenate
    packs = [chain(pack, "fsdp", bit) for bit in (1, 2, 3)]
    qkv_shard = side([query_weight, key_weight, value_weight], axis=1)
    up_shard = side([out_weight, up_weight], axis=1)

    def far_pieces(shard, which, bit, count):
        half = half_of(shard, which)
        return [Chain(gather_far(piece, bit)) for piece in jnp.split(half, count)]

    def cores_of(chains):
        return [chain(part, "fsdp", 1) for far in chains for part in far.result]

    def parts_of(shard, core, chains, cores):
        parts = [shard, core.result]
        for at, far in enumerate(chains):
            parts += [*far.result, *(c.result for c in cores[2 * at : 2 * at + 2])]
        return parts

    qkv_far = far_pieces(qkv_shard, parity, 1, 1)
    up_far = far_pieces(up_shard, parity, 1, 2)
    down_far = far_pieces(down_weight, beside, 2, 2)
    qkv_core, up_core, down_core = (
        chain(shard, "fsdp", 1) for shard in (qkv_shard, up_shard, down_weight)
    )
    run(None, (), [*packs, *qkv_far, qkv_core], packs)
    w, own, ke, oh, near_t, smalls, full_up_bias = run(
        lambda *a: prepare(index, *a),
        ((pack, *(p.result for p in packs)), layout_cells, pad_mask),
        [],
        [*qkv_far, qkv_core],
    )
    run(None, (), [*qkv_far, *up_far], qkv_far)
    qkv_cores = cores_of(qkv_far)
    run(None, (), [*qkv_cores, up_core], [*qkv_cores, up_core])
    run(None, (), [], up_far)
    qkv_parts = parts_of(qkv_shard, qkv_core, qkv_far, qkv_cores)
    qkv = run(
        lambda *a: project(index, qkv_parts, *a),
        (tokens, smalls),
        [down_far[0], up_far[0], down_core],
    )
    old = run(
        lambda *a: attend(FORWARD_GROUPS[0], *a),
        (qkv, w, own, ke, near_t),
        [down_far[1], up_far[1], down_far[0]],
    )
    cores = cores_of([*up_far, down_far[0]])
    mixed, lse = run(
        lambda *a: attend(FORWARD_GROUPS[1], *a),
        (qkv, w, own, ke, near_t, old),
        [down_far[1], *cores],
    )
    more = cores_of(down_far[1:])
    run(None, (), more)
    up_parts = parts_of(up_shard, up_core, up_far, cores[:4])
    down_parts = parts_of(down_weight, down_core, down_far, cores[4:] + more)
    result, dfinal, resid, slope, sums_two, *down_rows = run(
        lambda *a: forward(index, up_parts, down_parts, *a),
        (mixed, tokens, cotangent, smalls, full_up_bias),
    )

    down_sum = Chain(reduce_steps(*down_rows))
    run(None, (), [down_sum])
    dresid, dmixed, sums_one, up_sums, *up_rows = run(
        lambda *a: backward(index, up_parts, down_parts, *a),
        (dfinal, resid, slope, mixed, smalls),
        [down_sum],
    )
    first_sum = Chain(reduce_steps(*up_rows[:2]))
    second_sum = Chain(reduce_steps(*up_rows[2:]))
    run(None, (), [first_sum])

    def back(at, room, begin, old=()):
        return run(
            lambda *a: attend_back(GROUPS[at], room, index, *a),
            (qkv, w, own, ke, oh, near_t, dmixed, mixed, lse, tokens, old),
            begin,
        )

    columns = 3 * width * 2 // 3
    backs = [back(0, columns, [first_sum, down_sum, second_sum])]
    backs.append(back(1, columns, [second_sum, down_sum, first_sum], tuple(backs[0][6:])))
    early_sum = Chain(reduce_steps(*backs[1][6:]))
    backs.append(back(2, columns // 2 + 128, [early_sum, down_sum, second_sum]))
    late_rows = run(
        lambda *a: small_gradients(index, *a),
        ([group[3:6] for group in backs], sums_one, sums_two, up_sums, *backs[2][6:]),
        [first_sum, down_sum],
    )
    late_sum = Chain(reduce_steps(*late_rows))
    run(None, (), [late_sum])
    input_grad = run(
        lambda *a: input_gradient(index, qkv_parts, *a),
        ([array for group in backs for array in group[:3]], dresid),
        [early_sum, first_sum, second_sum, down_sum],
    )
    chains = [late_sum, early_sum, first_sum, second_sum, down_sum]
    while any(c.result is None for c in chains):
        run(None, (), [c for c in chains if c.result is None])
    halves = [c.result for c in (down_sum, first_sum, second_sum)]
    ordered = [in_order(*pair, parity).astype(F32) * factor for pair in halves]
    grad_up = side([ordered[1][:, width:], ordered[2]], axis=1)
    *grad_qkv, tail = unpack(index, early_sum.result, late_sum.result, factor)
    return (
        result,
        input_grad,
        *grad_qkv,
        ordered[1][:, :width],
        tail[0],
        tail[1],
        tail[2],
        tail[12:14].reshape(-1)[: 3 * 96].reshape(3, 96),
        tail[3],
        tail[4],
        grad_up,
        tail[8:12].reshape(-1),
        ordered[0],
        tail[5],
        tail[6],
        tail[7],
    )


def solution(mesh):
    rows = P(("dp", "fsdp"), None)
    matrix, vector = P("fsdp", None), P("fsdp")
    return jax.shard_map(
        on_device,
        mesh=mesh,
        in_specs=(
            rows, P(None, ("dp", "fsdp")), P(("dp", "fsdp")),
            matrix, matrix, matrix, matrix,
            vector, vector, vector, matrix, vector, vector,
            matrix, vector, matrix, vector, vector, vector,
            rows,
        ),
        out_specs=(
            rows, rows,
            matrix, matrix, matrix, matrix,
            vector, vector, vector, matrix, vector, vector,
            matrix, vector, matrix, vector, vector, vector,
        ),
        check_vma=False,
    )
```

```python
import functools
import math

import jax
import jax.numpy as jnp
import numpy as np
from jax import lax
from jax.experimental import pallas as pl
from jax.experimental.pallas import tpu as pltpu
from jax.sharding import PartitionSpec as P

HEADS = 12
HD = 64
WIN = 512
BUCKETS = 32
PAIRS = HEADS // 2
SCALE = HD ** (-0.5)
EPS = 1e-05
BF = jnp.bfloat16
F32 = jnp.float32
VMEM_LIMIT = 60 * 1024 * 1024
GROUPS = ((0, 2), (2, 2), (4, 2))
FORWARD_GROUPS = ((0, 3), (3, 3))


def params():
    return pltpu.CompilerParams(vmem_limit_bytes=VMEM_LIMIT)


def cost(flops, nbytes, transcendentals=0):
    return pl.CostEstimate(
        flops=int(flops / 100),
        bytes_accessed=int(nbytes / 100),
        transcendentals=int(transcendentals / 100),
    )


def struct(shape, dtype):
    return jax.ShapeDtypeStruct(shape, dtype)


def whole(array):
    return pl.BlockSpec(array.shape, lambda *at: (0,) * len(array.shape))


def dot(left, right):
    return lax.dot_general(left, right, (((1,), (0,)), ((), ())), preferred_element_type=F32)


def dot_t(left, right):
    return lax.dot_general(left, right, (((1,), (1,)), ((), ())), preferred_element_type=F32)


def tdot(left, right):
    return lax.dot_general(left, right, (((0,), (0,)), ((), ())), preferred_element_type=F32)


def split3(values):
    high = values.astype(BF)
    rest = values - high.astype(F32)
    middle = rest.astype(BF)
    return high, middle, (rest - middle.astype(F32)).astype(BF)


def swap(array, axis, bit):
    return lax.ppermute(array, axis, [(i, i ^ bit) for i in range(lax.axis_size(axis))])


def together(*groups):
    flat, tree = jax.tree.flatten(groups)
    return jax.tree.unflatten(tree, lax.optimization_barrier(tuple(flat)))


def half_of(array, which, axis=0):
    rows = array.shape[axis] // 2
    return lax.dynamic_slice_in_dim(array, which * rows, rows, axis)


class Chain:
    def __init__(self, steps):
        self.steps = steps
        self.result = None
        self.move = next(steps)

    def advance(self, arrived):
        try:
            self.move = self.steps.send(arrived)
        except StopIteration as stop:
            self.move, self.result = None, stop.value


def run(call, arrays, begin=(), finish=None):
    finish = begin if finish is None else finish
    arrays, sent = together(arrays, [chain.move[0] for chain in begin])
    for chain, array in zip(begin, sent):
        chain.flight = swap(array, chain.move[1], chain.move[2])
    out = call(*arrays) if call is not None else ()
    out, arrived = together(out, [chain.flight for chain in finish])
    for chain, array in zip(finish, arrived):
        chain.advance(array)
    return out


def gather_far(piece, bit):
    far = yield piece, "fsdp", 2
    beside = yield far, "dp", bit
    return far, beside


def send_once(array, axis, bit):
    arrived = yield array, axis, bit
    return arrived


def part_rows(index, rows, count):
    me, near, beside = index[0], index[1], index[2]
    places = [(me * rows, rows), ((me ^ 1) * rows, rows)]
    if count == QUARTERS:
        quarter = rows // 4
        firsts = [
            (2 * line + side) * quarter
            for line in (beside, 1 - beside)
            for side in (near, 1 - near)
        ]
        return places + [
            ((me ^ other) * rows + first, quarter) for other in (2, 3) for first in firsts
        ]
    half, pieces = rows // 2, (count - 2) // 4
    size = half // pieces
    for piece in range(pieces):
        for other in (2, 3):
            for side in (near, 1 - near):
                places.append(((me ^ other) * rows + side * half + piece * size, size))
    return places


PARTS, BIG_PARTS, QUARTERS = 6, 10, 11


def fetch_copies(index, parts, whole, sems, count=None):
    places = part_rows(index, whole.shape[0] // 4, count or len(parts))
    return [
        pltpu.make_async_copy(part, whole.at[pl.ds(pl.multiple_of(first, 16), size)], sems.at[at])
        for at, (part, (first, size)) in enumerate(zip(parts, places))
    ]


def start_copies(copies):
    for copy in copies:
        copy.start()


def wait_copies(copies):
    for copy in copies:
        copy.wait()


ANY = pl.BlockSpec(memory_space=pl.ANY)
SMEM = pl.BlockSpec(memory_space=pltpu.SMEM)


def reduce_steps(keep, send):
    place = lax.axis_index("dp")

    def add(*arrays):
        return functools.reduce(jnp.add, [array.astype(F32) for array in arrays]).astype(BF)

    got = yield send, "fsdp", 1
    far = yield add(keep[1], got[1]), "fsdp", 2
    total = add(keep[0], got[0], far)
    for bit in (1, 2):
        which = (place // bit) & 1
        got = yield half_of(total, 1 - which), "dp", bit
        total = add(half_of(total, which), got)
    bit = 4
    while bit < lax.axis_size("dp"):
        got = yield total, "dp", bit
        total = add(total, got)
        bit *= 2
    got = yield total, "dp", 2
    total = in_order(total, got, (place // 2) & 1)
    got = yield total, "dp", 1
    return total, got


def in_order(mine, other, which):
    return jnp.where(
        which == 0, jnp.concatenate([mine, other]), jnp.concatenate([other, mine])
    )


def table_places():
    step = np.arange(128)
    step = np.where(step < 64, -step, 128 - step)
    near = np.clip(step, -16, 15) + 16
    far = np.where(step <= -2, 0, np.where(step >= 2, 31, -1))
    wide = np.arange(256)
    wide = np.where(wide < 128, -wide, 256 - wide)
    places = np.concatenate([near + 32, near + 64, far, np.clip(wide, -16, 15) + 16])
    return places.astype(np.int32)[None, :]


def diagonal_places():
    lane = np.arange(128)
    x_place = np.where(lane < 63, np.clip(lane - 31, -16, 15) + 48, -1)
    y_place = np.where((lane >= 32) & (lane < 95), np.clip(lane - 63, -16, 15) + 80, -1)
    step = lane - 95
    block_place = np.where(
        (lane >= 64) & (step <= -2), 0, np.where((lane < 127) & (step >= 2), 31, -1)
    )
    step = (127 - np.arange(256) + 128) % 256 - 128
    places = np.concatenate([x_place, y_place, block_place, np.clip(step, -16, 15) + 16])
    return places.astype(np.int32)[:, None]


LANES = 640


def iota(shape, axis):
    return lax.broadcasted_iota(jnp.int32, shape, axis)


def as_bf(mask):
    return jnp.where(mask, 1.0, 0.0).astype(BF)


def near_mask():
    r, c = iota((128, 256), 0), iota((128, 256), 1)
    gap = (r >> 4) - (c >> 4)
    inside = (c < 128) & (gap <= 1) & (gap >= -1)
    return inside | ((r >= 112) & (c >= 128) & (c < 144)) | ((r < 16) & (c >= 240))


def hot_places(x, y, shape, axis):
    column = iota(shape, axis)
    block = (iota(shape, 1 - axis) & (WIN - 1)) >> 4
    third = column >> 5
    hot = jnp.where(third == 0, x, jnp.where(third == 1, y + 32, block + 64)) == column
    return column, hot & (column < 96)


PACK_ROWS, UP_ROW, TABLE_ROW = 16, 8, 10


def pack_vectors(vectors, up_bias, table):
    width, shard = up_bias.shape[0], vectors[0].shape[0]
    row = lax.broadcasted_iota(jnp.int32, (PACK_ROWS, shard), 0)
    pack = jnp.zeros((PACK_ROWS, shard), BF)
    for at, vector in enumerate(vectors):
        pack = jnp.where(row == at, vector[None, :], pack)
    pack = jnp.pad(pack, ((0, 0), (0, width - shard)))
    row = lax.broadcasted_iota(jnp.int32, (PACK_ROWS, width), 0)
    pack = jnp.where(row == UP_ROW, up_bias[None, :], pack)
    below = PACK_ROWS - TABLE_ROW - table.shape[0]
    return pack + jnp.pad(table, ((TABLE_ROW, below), (0, width - table.shape[1])))


def prep_kernel(
    index, p0, p1, p2, p3, cells_ref, mask_ref, places_ref,
    w_ref, own_ref, ke_ref, oh_ref, dt_ref, vectors_ref, up_bias_ref, packs,
):
    tokens = cells_ref.shape[1]
    me = index[0]
    for at, ref in enumerate((p0, p1, p2, p3)):
        packs[at] = ref[...]
    vectors = 0.0
    width = vectors_ref.shape[1]
    for at in range(4):
        rows = packs[me ^ at].astype(F32)
        vectors = vectors + pltpu.roll(rows[:8], at * (width // 4), 1)
        up_bias_ref[:, at * width : at * width + width] = rows[UP_ROW : UP_ROW + 1]
    vectors_ref[...] = vectors
    x, y, valid = cells_ref[0:1, :], cells_ref[1:2, :], mask_ref[...]
    column, hot = hot_places(x, y, (128, tokens), 0)
    own_ref[...] = as_bf(hot | (column == 96))
    sub = iota((8, tokens), 0)
    columns = jnp.where(sub == 0, x, jnp.where(sub == 1, y, valid)).astype(F32)
    columns = columns.T.astype(jnp.int32)
    x, y, valid = columns[:, 0:1], columns[:, 1:2], columns[:, 2:3]
    column, hot = hot_places(x, y, (tokens, 128), 1)
    masked = jnp.where((column == 99) & (valid <= 0), -1e30, 0.0)
    ones = hot | ((column >= 96) & (column < 99))
    ke_ref[...] = jnp.where(ones, 1.0, masked).astype(BF)
    block = (iota((tokens, 128), 0) & (WIN - 1)) >> 4
    third = column >> 5
    back = jnp.where(third == 0, 31 - x, jnp.where(third == 1, 63 - y, 95 - block)) == column
    oh_ref[...] = as_bf(back & (column < 96))

    pick = as_bf(iota((128, LANES), 0) == places_ref[...])
    lane = iota((32, 128), 1)
    mask = near_mask()
    for part in range(4):
        table = dot(packs[me ^ part][:, :128], pick)
        for head in range(HEADS // 4):
            row = table[TABLE_ROW + head : TABLE_ROW + head + 1]
            blocks = []
            for at in range(3):
                spread = jnp.broadcast_to(row[:, at * 128 : at * 128 + 128], (32, 128))
                spread = pltpu.roll(spread, at * 32, 1, stride=1, stride_axis=0)
                blocks.append(jnp.where(lane >> 5 == at, spread, 0.0))
            blocks.append(jnp.where((iota((32, 128), 0) == 3) & (lane == 96), 1.0, 0.0))
            place = part * (HEADS // 4) + head
            w_ref[place] = jnp.concatenate(blocks, axis=0).astype(BF)
            wide = jnp.broadcast_to(row[:, 384:640], (128, 256))
            rolled = pltpu.roll(wide, 0, 1, stride=1, stride_axis=0)
            dt_ref[place] = jnp.where(mask, rolled, 0.0).astype(BF)


def prepare(index, packs, layout_cells, pad_mask):
    tokens = pad_mask.shape[0]
    width = packs[0].shape[1]
    shapes = [
        struct((HEADS, 128, 128), BF),
        struct((128, tokens), BF),
        struct((tokens, 128), BF),
        struct((tokens, 128), BF),
        struct((HEADS, 128, 256), BF),
        struct((8, width), F32),
        struct((1, 4 * width), F32),
    ]
    arrays = [*packs, layout_cells, pad_mask.reshape(1, tokens), jnp.asarray(table_places())]
    return pl.pallas_call(
        prep_kernel,
        grid=(1,),
        in_specs=[SMEM] + [whole(array) for array in arrays],
        out_specs=[whole(shape) for shape in shapes],
        out_shape=shapes,
        scratch_shapes=[pltpu.VMEM((4, PACK_ROWS, width), BF)],
        compiler_params=params(),
        cost_estimate=cost(1e7, 3e6),
        name="prepare",
    )(index, *arrays)


def project_kernel(index, *refs):
    parts, (x_ref, bias_ref, out_ref, weight, sems) = refs[:PARTS], refs[PARTS:]

    @pl.when(pl.program_id(0) == 0)
    def _():
        copies = fetch_copies(index, parts, weight, sems)
        start_copies(copies)
        wait_copies(copies)

    width = x_ref.shape[1]
    for at in range(3):
        values = dot(x_ref[...], weight[:, at * width : (at + 1) * width])
        if at == 0:
            values = (values + bias_ref[0:1, :]).astype(BF) * SCALE
        if at == 2:
            values = values + bias_ref[1:2, :]
        values = values.astype(BF)
        for pair in range(PAIRS):
            out_ref[at * PAIRS + pair] = values[:, pair * 128 : pair * 128 + 128]


def project(index, parts, tokens, biases, block=512):
    rows, width = tokens.shape
    return pl.pallas_call(
        project_kernel,
        grid=(rows // block,),
        in_specs=[SMEM]
        + [ANY] * PARTS
        + [
            pl.BlockSpec((block, width), lambda i: (i, 0)),
            pl.BlockSpec((8, width), lambda i: (0, 0)),
        ],
        out_specs=pl.BlockSpec((3 * PAIRS, block, 128), lambda i: (0, i, 0)),
        out_shape=struct((3 * PAIRS, rows, 128), BF),
        scratch_shapes=[pltpu.VMEM((width, 3 * width), BF), pltpu.SemaphoreType.DMA((PARTS,))],
        compiler_params=params(),
        cost_estimate=cost(6 * rows * width * width, 10e6),
        name="project",
    )(index, *parts, tokens, biases)


def join(ref):
    return jnp.concatenate([ref[at] for at in range(ref.shape[0])], axis=1)


def input_kernel(index, *refs):
    count = len(GROUPS) * 3
    parts, grads = refs[:PARTS], refs[PARTS : PARTS + count]
    dresid_ref, out_ref, weight, sems = refs[PARTS + count :]

    @pl.when(pl.program_id(0) == 0)
    def _():
        copies = fetch_copies(index, parts, weight, sems)
        start_copies(copies)
        wait_copies(copies)

    joined = [join(grads[3 * group + at]) for at in range(3) for group in range(len(GROUPS))]
    total = dot_t(jnp.concatenate(joined, axis=1), weight[...])
    out_ref[...] = (dresid_ref[...] + total).astype(BF)


def input_gradient(index, parts, grads, dresid, block=256):
    rows, width = dresid.shape
    spec = pl.BlockSpec((block, width), lambda i: (i, 0))
    pairs = [pl.BlockSpec((a.shape[0], block, 128), lambda i: (0, i, 0)) for a in grads]
    return pl.pallas_call(
        input_kernel,
        grid=(rows // block,),
        in_specs=[SMEM] + [ANY] * PARTS + pairs + [spec],
        out_specs=spec,
        out_shape=struct((rows, width), BF),
        scratch_shapes=[pltpu.VMEM((width, 3 * width), BF), pltpu.SemaphoreType.DMA((PARTS,))],
        compiler_params=params(),
        cost_estimate=cost(6 * rows * width * width, 13e6),
        name="input_gradient",
    )(index, *parts, *grads, dresid)


def with_near(pieces, tile, at):
    pieces = list(pieces)
    pieces[at] = pieces[at] + tile[:, :128]
    if at > 0:
        left = pieces[at - 1]
        pieces[at - 1] = jnp.concatenate([left[:16] + tile[:16, 128:], left[16:]], axis=0)
    if at < 3:
        right = pieces[at + 1]
        pieces[at + 1] = jnp.concatenate([right[:112], right[112:] + tile[112:, 128:]], axis=0)
    return pieces


def lane_blocks(values):
    return [values[:, c * 128 : c * 128 + 128] for c in range(WIN // 128)]


def attend_kernel(
    q_ref, k_ref, v_ref, w_ref, own_ref, ke_ref, dt_ref, out_ref, lse_ref, s_scr, p_scr
):
    first = iota((128, WIN), 0) < HD
    windows = [slice(at, at + WIN) for at in range(0, q_ref.shape[0], WIN)]
    extras = dot(w_ref[...].reshape(256, 128), own_ref[...]).astype(BF)
    values = []
    for at, rows in enumerate(windows):
        keys = jnp.concatenate([k_ref[rows, :], ke_ref[rows, :]], axis=1)
        query_t = q_ref[rows, :].T
        values.append(v_ref[rows, :].T)
        for head in range(2):
            mine = first if head == 0 else ~first
            query = jnp.where(mine, query_t, jnp.zeros((), BF))
            extra = extras[head * 128 : head * 128 + 128, rows]
            s_scr[2 * at + head] = dot(keys, jnp.concatenate([query, extra], axis=0))
    for at, rows in enumerate(windows):
        mixed = []
        for head in range(2):
            place = 2 * at + head
            tile = dt_ref[head].astype(F32)
            scores = [
                with_near(lane_blocks(s_scr[place, row : row + 128, :]), tile, row // 128)
                for row in range(0, WIN, 128)
            ]
            tops, totals = [], []
            for column in range(WIN // 128):
                pieces = [row[column] for row in scores]
                top = jnp.maximum(
                    jnp.maximum(pieces[0], pieces[1]), jnp.maximum(pieces[2], pieces[3])
                )
                top = jnp.max(top, axis=0, keepdims=True)
                pieces = [jnp.exp(piece - top) for piece in pieces]
                total = (pieces[0] + pieces[1]) + (pieces[2] + pieces[3])
                totals.append(jnp.sum(total, axis=0, keepdims=True))
                tops.append(top)
                span = slice(column * 128, column * 128 + 128)
                for row, piece in enumerate(pieces):
                    p_scr[place, row * 128 : row * 128 + 128, span] = piece.astype(BF)
            total = jnp.concatenate(totals, axis=1)
            mixed.append(dot(values[at][head * HD : head * HD + HD], p_scr[place]) / total)
            lse_ref[head : head + 1, rows] = jnp.concatenate(tops, axis=1) + jnp.log(total)
        out_ref[rows, :] = jnp.concatenate(mixed, axis=0).astype(BF).T


def pair_block(tokens, shift):
    return pl.BlockSpec((None, tokens, 128), lambda p: (p + shift, 0, 0))


def attend(group, qkv, w, own, ke, near_t, old=()):
    start, pairs = group
    tokens = qkv.shape[1]
    scores = 2 * (tokens // WIN)
    kernel = attend_kernel
    if old:
        kernel = lambda *refs: attend_kernel(*refs[:7], *refs[9:])
    return pl.pallas_call(
        kernel,
        grid=(pairs,),
        in_specs=[
            pair_block(tokens, start),
            pair_block(tokens, start + PAIRS),
            pair_block(tokens, start + 2 * PAIRS),
            pl.BlockSpec((2, 128, 128), lambda p: (p + start, 0, 0)),
            whole(own),
            whole(ke),
            pl.BlockSpec((2, 128, 256), lambda p: (p + start, 0, 0)),
        ]
        + [ANY] * len(old),
        out_specs=[
            pair_block(tokens, start),
            pl.BlockSpec((None, 8, tokens), lambda p: (p + start, 0, 0)),
        ],
        out_shape=[struct((PAIRS, tokens, 128), BF), struct((PAIRS, 8, tokens), F32)],
        input_output_aliases={7: 0, 8: 1} if old else {},
        scratch_shapes=[pltpu.VMEM((scores, WIN, WIN), F32), pltpu.VMEM((scores, WIN, WIN), BF)],
        compiler_params=params(),
        cost_estimate=cost(tokens * WIN * pairs * 1536, 4e6 * pairs / 2, tokens * WIN * 2 * pairs),
        name="attend",
    )(qkv, qkv, qkv, w, own, ke, near_t, *old)


def diagonal_rows(sums):
    lane = iota((32, 128), 1)
    rows = []
    for at in range(3):
        block = jnp.where(lane >> 5 == at, sums[at * 32 : at * 32 + 32], 0.0)
        rolled = pltpu.roll(block, 0, 1, stride=1, stride_axis=0)
        rows.append(jnp.sum(rolled, axis=0, keepdims=True))
    return rows


def near_rows(tile):
    tile = jnp.where(near_mask(), tile, 0.0)
    turn = as_bf(iota((128, 128), 0) + iota((128, 128), 1) == 127)
    high, middle, low = split3(tile)
    turned = dot(turn, high) + dot(turn, middle) + dot(turn, low)
    rolled = pltpu.roll(turned, 0, 1, stride=1, stride_axis=0)
    return jnp.sum(rolled, axis=0, keepdims=True)


def attend_back_kernel(
    index, q_ref, k_ref, v_ref, w_ref, own_ref, ke_ref, oh_ref, dt_ref, do_ref, o_ref, lse_ref,
    x_ref, dq_ref, dk_ref, dv_ref, bias_ref, far_ref, near_ref, keep_ref, send_ref,
    s_scr, dp_scr, p_scr, ds_scr, x_t, products,
):
    @pl.when(pl.program_id(0) == 0)
    def _():
        x_t[...] = x_ref[...].T

    zero = jnp.zeros((), BF)
    first = iota((WIN, 128), 1) < HD
    first_t = iota((128, WIN), 0) < HD
    place = iota((128, WIN), 0)
    windows = [slice(at, at + WIN) for at in range(0, q_ref.shape[0], WIN)]
    extra_columns = dot(w_ref[...].reshape(256, 128), own_ref[...]).astype(BF)
    keys_t = []
    for at, rows in enumerate(windows):
        keys = jnp.concatenate([k_ref[rows, :], ke_ref[rows, :]], axis=1)
        values = jnp.concatenate([v_ref[rows, :], ke_ref[rows, :]], axis=1)
        keys_t.append(k_ref[rows, :].T)
        query_t, grad_t = q_ref[rows, :].T, do_ref[rows, :].T
        product = grad_t.astype(F32) * o_ref[rows, :].T.astype(F32)
        for head in range(2):
            mine = first_t if head == 0 else ~first_t
            delta = -jnp.sum(product[head * HD : head * HD + HD], axis=0, keepdims=True)
            minus = jnp.zeros((128, WIN), BF)
            extra = extra_columns[head * 128 : head * 128 + 128, rows]
            parts = split3(-lse_ref[head : head + 1, rows])
            for part, (less, less_delta) in enumerate(zip(parts, split3(delta))):
                extra = jnp.where(place == 96 + part, less, extra)
                minus = jnp.where(place == 96 + part, less_delta, minus)
            query = jnp.where(mine, query_t, zero)
            grad = jnp.where(mine, grad_t, zero)
            s_scr[2 * at + head] = dot(keys, jnp.concatenate([query, extra], axis=0))
            dp_scr[2 * at + head] = dot(values, jnp.concatenate([grad, minus], axis=0))
    plus = lambda total, term: term if total is None else total + term
    far_left, diag, low, high = [], [None] * 2, [None] * 2, [None] * 2
    bias_sums = [None] * 2
    for at, rows in enumerate(windows):
        dq_t, extras, dk, dv = [], [], None, None
        for head in range(2):
            mine = first if head == 0 else ~first
            query = jnp.where(mine, q_ref[rows, :], zero)
            grad = jnp.where(mine, do_ref[rows, :], zero)
            tile = dt_ref[head].astype(F32)
            place = 2 * at + head
            for block in range(WIN // 128):
                span = slice(block * 128, block * 128 + 128)
                scores = with_near(lane_blocks(s_scr[place, span, :]), tile, block)
                probs = [jnp.exp(piece) for piece in scores]
                dprobs = lane_blocks(dp_scr[place, span, :])
                dscores = [a * b for a, b in zip(probs, dprobs)]
                p_scr[place, span, :] = jnp.concatenate([a.astype(BF) for a in probs], axis=1)
                ds_scr[place, span, :] = jnp.concatenate([a.astype(BF) for a in dscores], axis=1)
                diag[head] = plus(diag[head], dscores[block])
                if block > 0:
                    low[head] = plus(low[head], dscores[block - 1][:16])
                if block < 3:
                    high[head] = plus(high[head], dscores[block + 1][112:])
            dv = plus(dv, dot(p_scr[place], grad))
            dk = plus(dk, dot(ds_scr[place], query))
            left = jnp.concatenate(
                [keys_t[at][head * HD : head * HD + HD], own_ref[:96, rows]], axis=0
            )
            both = dot(left, ds_scr[place])
            dq_t.append(both[:HD] * SCALE)
            extras.append(both[HD:].astype(BF))
        far_left.append(jnp.concatenate(extras, axis=0))
        dq = jnp.concatenate(dq_t, axis=0).astype(BF).T
        dv = dv.astype(BF)
        dq_ref[rows, :] = dq
        dk_ref[rows, :] = dk.astype(BF)
        dv_ref[rows, :] = dv
        for which, array in enumerate((dq, dv)):
            total = jnp.sum(array.astype(F32), axis=0, keepdims=True)
            bias_sums[which] = plus(bias_sums[which], total)
    grads = jnp.concatenate([dq_ref[...], dk_ref[...], dv_ref[...]], axis=1)
    products[...] = dot(x_t[...], grads)
    place_rows(index, products, keep_ref, send_ref)
    bias_ref[...] = jnp.zeros_like(bias_ref)
    for which in range(2):
        bias_ref[which : which + 1, :] = bias_sums[which]
    far = dot(jnp.concatenate(far_left, axis=1), oh_ref[...])
    for head in range(2):
        sums = diagonal_rows(far[head * 96 : head * 96 + 96])
        far_ref[head] = jnp.concatenate(sums + [jnp.zeros((5, 128), F32)], axis=0)
        corners = jnp.concatenate([low[head], jnp.zeros((96, 128), F32), high[head]], axis=0)
        tile = jnp.concatenate([diag[head], corners], axis=1)
        near_ref[head] = jnp.broadcast_to(near_rows(tile), (8, 256))


def attend_back(
    group, room, index, qkv, w, own, ke, oh, near_t, dmixed, mixed, lse, x, old=()
):
    start, pairs = group
    kernel = attend_back_kernel
    if old:
        kernel = lambda *refs: attend_back_kernel(*refs[:13], *refs[15:])
    tokens, width = x.shape
    scores = 2 * (tokens // WIN)
    out = struct((pairs, tokens, 128), BF)
    weight_rows = struct((2, width // 4, room), BF)
    weight_block = pl.BlockSpec(
        (2, width // 4, 384), lambda p: (0, 0, p + (start if old else 0))
    )
    return pl.pallas_call(
        kernel,
        grid=(pairs,),
        in_specs=[
            SMEM,
            pair_block(tokens, start),
            pair_block(tokens, start + PAIRS),
            pair_block(tokens, start + 2 * PAIRS),
            pl.BlockSpec((2, 128, 128), lambda p: (p + start, 0, 0)),
            whole(own),
            whole(ke),
            whole(oh),
            pl.BlockSpec((2, 128, 256), lambda p: (p + start, 0, 0)),
            pair_block(tokens, start),
            pair_block(tokens, start),
            pl.BlockSpec((None, 8, tokens), lambda p: (p + start, 0, 0)),
            whole(x),
        ]
        + [ANY] * len(old),
        out_specs=[
            pair_block(tokens, 0),
            pair_block(tokens, 0),
            pair_block(tokens, 0),
            pl.BlockSpec((None, 8, 128), lambda p: (p, 0, 0)),
            pl.BlockSpec((2, 8, 128), lambda p: (p, 0, 0)),
            pl.BlockSpec((2, 8, 256), lambda p: (p, 0, 0)),
            weight_block,
            weight_block,
        ],
        out_shape=[
            out,
            out,
            out,
            struct((pairs, 8, 128), F32),
            struct((2 * pairs, 8, 128), F32),
            struct((2 * pairs, 8, 256), F32),
            weight_rows,
            weight_rows,
        ],
        input_output_aliases={13: 6, 14: 7} if old else {},
        scratch_shapes=[
            pltpu.VMEM((scores, WIN, WIN), F32),
            pltpu.VMEM((scores, WIN, WIN), F32),
            pltpu.VMEM((scores, WIN, WIN), BF),
            pltpu.VMEM((scores, WIN, WIN), BF),
            pltpu.VMEM((width, tokens), BF),
            pltpu.VMEM((width, 384), F32),
        ],
        compiler_params=params(),
        cost_estimate=cost(
            tokens * WIN * pairs * 2 * 2048, 12e6, tokens * WIN * pairs * 2
        ),
        name="attend_back",
    )(index, qkv, qkv, qkv, w, own, ke, oh, near_t, dmixed, mixed, lse, x, *old)


def norm_parts(values):
    centre = values - jnp.mean(values, axis=-1, keepdims=True)
    spread = jnp.mean(centre * centre, axis=-1, keepdims=True)
    scale = lax.rsqrt(spread + EPS)
    return centre * scale, scale


def norm_back(grad, hat, scale):
    mean = jnp.mean(grad, axis=-1, keepdims=True)
    along = jnp.mean(grad * hat, axis=-1, keepdims=True)
    return scale * (grad - mean - hat * along)


def add_rows(ref, rows):
    for at, values in enumerate(rows):
        ref[at : at + 1, :] += jnp.sum(values.astype(F32), axis=0, keepdims=True)


def gelu_and_slope(values):
    upto = 0.5 + 0.5 * lax.erf(values * math.sqrt(0.5))
    density = jnp.exp(values * values * -0.5) * (1.0 / math.sqrt(2.0 * math.pi))
    return values * upto, upto + values * density


def store_rows(index, total, keep, send, stage, sems):
    me, shard = index[0], keep.shape[1]
    copies = []
    for at, (which, ref) in enumerate(((1, send), (3, send), (2, keep), (0, keep))):
        rows = pl.ds(pl.multiple_of((me ^ which) * shard, 16), shard)
        stage[at] = total[rows, :].astype(BF)
        copies.append(pltpu.make_async_copy(stage.at[at], ref.at[which // 2], sems.at[at]))
        copies[-1].start()
    return copies


def forward_kernel(index, *refs):
    up_parts, down_parts = refs[:BIG_PARTS], refs[BIG_PARTS : 2 * BIG_PARTS]
    (
        mixed_ref, x_ref, cot_ref, small_ref, up_bias_ref,
        out_ref, dfinal_ref, resid_ref, slope_ref, sums_ref, keep_ref, send_ref,
        w_up, w_down, total, active_scr, stage, sems, out_sems,
    ) = refs[2 * BIG_PARTS :]
    step = pl.program_id(0)
    up_copies = fetch_copies(index, up_parts, w_up, sems.at[0])
    down_copies = fetch_copies(index, down_parts, w_down, sems.at[1], QUARTERS)

    @pl.when(step == 0)
    def _():
        start_copies(up_copies)
        start_copies(down_copies)
        for ref in (sums_ref, total):
            ref[...] = jnp.zeros_like(ref)
        wait_copies(up_copies)

    width, hidden = w_down.shape[1], w_down.shape[0]
    small = lambda at: small_ref[at + 2 : at + 3, :]
    resid = x_ref[...].astype(F32) + (dot(join(mixed_ref), w_up[:, :width]) + small(0))
    resid_ref[...] = resid
    hat, _ = norm_parts(resid)
    normed = hat * small(1) + small(2)
    low = normed.astype(BF)
    for at in range(0, hidden, width):
        span = slice(at, at + width)
        values = dot(low, w_up[:, at + width : at + 2 * width]) + up_bias_ref[:, span]
        active, slope = gelu_and_slope(values)
        active_scr[:, span] = active.astype(BF)
        slope_ref[:, span] = slope.astype(BF)

    @pl.when(step == 0)
    def _():
        wait_copies(down_copies)

    final = normed + dot(active_scr[...], w_down[...]) + small(3)
    hat, scale = norm_parts(final)
    out_ref[...] = (hat * small(4) + small(5)).astype(BF)
    cot = cot_ref[...].astype(F32)
    dfinal = norm_back(cot * small(4), hat, scale)
    dfinal_ref[...] = dfinal
    dbranch = dfinal.astype(BF)
    for at in range(0, hidden, width):
        total[at : at + width, :] += tdot(active_scr[:, at : at + width], dbranch)
    add_rows(sums_ref, (cot * hat, cot, dbranch))

    @pl.when(step == pl.num_programs(0) - 1)
    def _():
        wait_copies(store_rows(index, total, keep_ref, send_ref, stage, out_sems))


def forward(index, up_parts, down_parts, mixed, tokens, cotangent, smalls, up_bias, block=256):
    rows, width = tokens.shape
    hidden = up_bias.shape[1]
    spec = lambda columns: pl.BlockSpec((block, columns), lambda i: (i, 0))
    pairs = pl.BlockSpec((PAIRS, block, 128), lambda i: (0, i, 0))
    sums = struct((8, width), F32)
    down_rows = struct((2, hidden // 4, width), BF)
    return pl.pallas_call(
        forward_kernel,
        grid=(rows // block,),
        in_specs=[SMEM]
        + [ANY] * (2 * BIG_PARTS)
        + [pairs, spec(width), spec(width), whole(smalls), whole(up_bias)],
        out_specs=[spec(width), spec(width), spec(width), spec(hidden), whole(sums), ANY, ANY],
        out_shape=[
            struct((rows, width), BF),
            struct((rows, width), F32),
            struct((rows, width), F32),
            struct((rows, hidden), BF),
            sums,
            down_rows,
            down_rows,
        ],
        scratch_shapes=[
            pltpu.VMEM((width, width + hidden), BF),
            pltpu.VMEM((hidden, width), BF),
            pltpu.VMEM((hidden, width), F32),
            pltpu.VMEM((block, hidden), BF),
            pltpu.VMEM((4, hidden // 4, width), BF),
            pltpu.SemaphoreType.DMA((2, BIG_PARTS)),
            pltpu.SemaphoreType.DMA((4,)),
        ],
        compiler_params=params(),
        cost_estimate=cost(2 * rows * width * (width + 3 * hidden), 40e6),
        name="forward",
    )(index, *up_parts, *down_parts, mixed, tokens, cotangent, smalls, up_bias)


def backward_kernel(index, *refs):
    up_parts, down_parts = refs[:BIG_PARTS], refs[BIG_PARTS : 2 * BIG_PARTS]
    (
        dfinal_ref, resid_ref, slope_ref, mixed_ref, small_ref,
        dresid_ref, dmixed_ref, sums_ref, up_sums_ref, *row_refs,
        w_up, w_down, total, stage, sems, out_sems,
    ) = refs[2 * BIG_PARTS :]
    step = pl.program_id(0)

    @pl.when(step == 0)
    def _():
        copies = fetch_copies(index, down_parts, w_down, sems.at[0], QUARTERS)
        copies += fetch_copies(index, up_parts, w_up, sems.at[1])
        start_copies(copies)
        for ref in (sums_ref, up_sums_ref, total):
            ref[...] = jnp.zeros_like(ref)
        wait_copies(copies)

    width, hidden = w_down.shape[1], w_down.shape[0]
    small = lambda at: small_ref[at + 2 : at + 3, :]
    hat, scale = norm_parts(resid_ref[...])
    low_t = (hat * small(1) + small(2)).astype(BF).T
    dnormed = dfinal_ref[...]
    dbranch = dnormed.astype(BF)
    for at in range(0, hidden, width):
        span = slice(at, at + width)
        up_span = slice(at + width, at + 2 * width)
        dactive = dot_t(dbranch, w_down[span, :])
        dhidden = (dactive * slope_ref[:, span].astype(F32)).astype(BF)
        up_sums_ref[:, span] += jnp.sum(dhidden.astype(F32), axis=0, keepdims=True)
        total[:, up_span] += dot(low_t, dhidden)
        dnormed = dnormed + dot_t(dhidden, w_up[:, up_span])
    dresid = norm_back(dnormed * small(1), hat, scale)
    dresid_ref[...] = dresid
    dattn = dresid.astype(BF)
    dmixed = dot_t(dattn, w_up[:, :width]).astype(BF)
    for pair in range(PAIRS):
        dmixed_ref[pair] = dmixed[:, pair * 128 : pair * 128 + 128]
    total[:, :width] += tdot(join(mixed_ref), dattn)
    add_rows(sums_ref, (dnormed * hat, dnormed, dattn))

    @pl.when(step == pl.num_programs(0) - 1)
    def _():
        half = (width + hidden) // 2
        for at in range(2):
            columns = slice(at * half, at * half + half)
            wait_copies(
                store_rows(
                    index,
                    total.at[:, columns],
                    *row_refs[2 * at : 2 * at + 2],
                    stage.at[:, :, columns],
                    out_sems,
                )
            )


def backward(index, up_parts, down_parts, dfinal, resid, slope, mixed, smalls, block=256):
    rows, width = resid.shape
    hidden = slope.shape[1]
    spec = lambda columns: pl.BlockSpec((block, columns), lambda i: (i, 0))
    pairs = pl.BlockSpec((PAIRS, block, 128), lambda i: (0, i, 0))
    sums = [struct((8, width), F32), struct((1, hidden), F32)]
    up_rows = struct((2, width // 4, (width + hidden) // 2), BF)
    return pl.pallas_call(
        backward_kernel,
        grid=(rows // block,),
        in_specs=[SMEM]
        + [ANY] * (2 * BIG_PARTS)
        + [spec(width), spec(width), spec(hidden), pairs, whole(smalls)],
        out_specs=[spec(width), pairs] + [whole(shape) for shape in sums] + [ANY] * 4,
        out_shape=[struct((rows, width), F32), struct((PAIRS, rows, 128), BF)]
        + sums
        + [up_rows] * 4,
        scratch_shapes=[
            pltpu.VMEM((width, width + hidden), BF),
            pltpu.VMEM((hidden, width), BF),
            pltpu.VMEM((width, width + hidden), F32),
            pltpu.VMEM((4, width // 4, width + hidden), BF),
            pltpu.SemaphoreType.DMA((2, BIG_PARTS)),
            pltpu.SemaphoreType.DMA((4,)),
        ],
        compiler_params=params(),
        cost_estimate=cost(4 * rows * width * (width + 2 * hidden), 40e6),
        name="backward",
    )(index, *up_parts, *down_parts, dfinal, resid, slope, mixed, smalls)


def place_rows(index, total, keep_ref, send_ref):
    me, shard = index[0], keep_ref.shape[1]
    for at, ref in ((0, keep_ref), (2, keep_ref), (1, send_ref), (3, send_ref)):
        rows = pl.ds(pl.multiple_of((me ^ at) * shard, 16), shard)
        ref[at // 2] = total[rows, :].astype(BF)


def small_rows(refs, places, sums_one, sums_two, up_sums, rows, sums):
    width = rows.shape[1]
    shard = width // 4
    rows[...] = jnp.zeros_like(rows)
    sums[...] = jnp.zeros_like(sums)
    pair, head = 0, 0
    for bias, far, near in refs:
        for at in range(bias.shape[0]):
            rows[0:2, pair * 128 : pair * 128 + 128] = bias[at, 0:2, :]
            pair += 1
        for at in range(far.shape[0]):
            parts = [far[at, row : row + 1, :] for row in range(3)] + [near[at, 0:1, :]]
            sums[head : head + 1, :] = jnp.concatenate(parts, axis=1)
            head += 1
    for row, source in enumerate((2, 0, 1)):
        rows[row + 2 : row + 3, :] = sums_one[source : source + 1, :]
        rows[row + 5 : row + 6, :] = sums_two[source : source + 1, :]
    lane = iota((1, width), 1)
    for at in range(4):
        values = up_sums[:, at * width : at * width + width]
        inside = (lane >= at * shard) & (lane < (at + 1) * shard)
        for part in range(4):
            rolled = pltpu.roll(values, (at - part) % 4 * shard, 1)
            rows[8 + part : 9 + part, :] += jnp.where(inside, rolled, 0.0)
    pick = as_bf(places[...] == iota((LANES, 128), 1))
    table = sum(dot(part, pick) for part in split3(sums[...]))
    table = jnp.concatenate([table, jnp.zeros((table.shape[0], width - 128), F32)], axis=1)
    for at in range(HEADS):
        within = at % 3
        shift = at // 3 * shard + within % 2 * 96
        rolled = pltpu.roll(table[at : at + 1], shift, 1)
        rows[12 + within // 2 : 13 + within // 2, :] += rolled


def small_kernel(count, index, *refs):
    groups, refs = refs[: 3 * count], refs[3 * count :]
    (
        places, sums_one, sums_two, up_sums, keep_in, send_in, keep_ref, send_ref, total, rows, sums
    ) = refs
    del keep_in, send_in
    groups = [groups[at : at + 3] for at in range(0, 3 * count, 3)]
    small_rows(groups, places, sums_one, sums_two, up_sums, rows, sums)
    total[...] = rows[...].T
    place_rows(index, total, keep_ref, send_ref)


def small_gradients(index, groups, sums_one, sums_two, up_sums, keep, send):
    width = sums_one.shape[1]
    block = keep.shape[2] // 128 - 1
    arrays = [array for group in groups for array in group]
    arrays += [jnp.asarray(diagonal_places()), sums_one, sums_two, up_sums]
    out = pl.BlockSpec((2, width // 4, 128), lambda i: (0, 0, block))
    return pl.pallas_call(
        functools.partial(small_kernel, len(groups)),
        grid=(1,),
        in_specs=[SMEM] + [whole(array) for array in arrays] + [ANY, ANY],
        out_specs=[out, out],
        out_shape=[struct(keep.shape, BF)] * 2,
        input_output_aliases={len(arrays) + 1: 0, len(arrays) + 2: 1},
        scratch_shapes=[
            pltpu.VMEM((width, 128), F32),
            pltpu.VMEM((128, width), F32),
            pltpu.VMEM((16, LANES), F32),
        ],
        compiler_params=params(),
        cost_estimate=cost(1e7, 1e6),
        name="small_gradients",
    )(index, *arrays, keep, send)


def unpack_kernel(factor, index, *refs):
    halves, (query_ref, key_ref, value_ref, small_ref, small_scr) = refs[:4], refs[4:]
    half = halves[0].shape[0]
    for at in range(2):
        rows = pl.ds(pl.multiple_of((index[1] ^ at) * half, 16), half)
        first = 0
        for ref in (halves[at], halves[2 + at]):
            for column in range(0, ref.shape[1] // 384 * 384, 384):
                for which, out in enumerate((query_ref, key_ref, value_ref)):
                    place = column + which * 128
                    values = ref[:, place : place + 128].astype(F32) * factor
                    out[rows, first : first + 128] = values
                first += 128
        values = halves[2 + at][:, halves[2].shape[1] - 128 :]
        small_scr[rows, :] = values.astype(F32) * factor
    small_ref[...] = small_scr[...].T


def unpack(index, early, late, factor):
    half, width = early[0].shape[0], PAIRS * 128
    arrays = [*early, *late]
    outs = [struct((2 * half, width), F32)] * 3 + [struct((128, 2 * half), F32)]
    return pl.pallas_call(
        functools.partial(unpack_kernel, factor),
        grid=(1,),
        in_specs=[SMEM] + [whole(array) for array in arrays],
        out_specs=[whole(shape) for shape in outs],
        out_shape=outs,
        scratch_shapes=[pltpu.VMEM((2 * half, 128), F32)],
        compiler_params=params(),
        cost_estimate=cost(1e6, 3e6),
        name="unpack",
    )(index, *arrays)


def on_device(
    tokens,
    layout_cells,
    pad_mask,
    query_weight,
    key_weight,
    value_weight,
    out_weight,
    query_bias,
    value_bias,
    out_bias,
    bias_table,
    first_gain,
    first_shift,
    up_weight,
    up_bias,
    down_weight,
    down_bias,
    second_gain,
    second_shift,
    cotangent,
):
    rows, width = tokens.shape
    hidden = down_weight.shape[0] * 4
    shard = width // 4
    me = lax.axis_index("fsdp")
    parity = lax.axis_index("dp") & 1
    beside = (lax.axis_index("dp") >> 1) & 1
    index = jnp.stack([me, parity, beside]).astype(jnp.int32)
    factor = 1.0 / math.sqrt(rows * lax.axis_size("dp") * lax.axis_size("fsdp"))

    vectors = (
        query_bias, value_bias, out_bias, first_gain, first_shift, down_bias, second_gain,
        second_shift,
    )
    pack = pack_vectors(vectors, up_bias, bias_table)
    chain = lambda *args: Chain(send_once(*args))

    side = jnp.concatenate
    packs = [chain(pack, "fsdp", bit) for bit in (1, 2, 3)]
    qkv_shards = (query_weight, key_weight, value_weight)
    qkv_half = side([half_of(shard, parity) for shard in qkv_shards], axis=1)
    qkv_shard = side(qkv_shards, axis=1)
    up_shard = side([out_weight, up_weight], axis=1)

    def far_pieces(half, bit, count):
        return [Chain(gather_far(piece, bit)) for piece in jnp.split(half, count)]

    def cores_of(chains):
        return [chain(part, "fsdp", 1) for far in chains for part in far.result]

    def parts_of(shard, core, chains, cores):
        parts = [shard, core.result]
        for at, far in enumerate(chains):
            parts += [*far.result, *(c.result for c in cores[2 * at : 2 * at + 2])]
        return parts

    qkv_far = far_pieces(qkv_half, 1, 1)
    up_half = side([half_of(out_weight, parity), half_of(up_weight, parity)], axis=1)
    up_far = far_pieces(up_half, 1, 2)
    down_far = Chain(gather_far(half_of(half_of(down_weight, beside), parity), 1))
    qkv_core, up_core, down_core = (
        chain(shard, "fsdp", 1) for shard in (qkv_shard, up_shard, down_weight)
    )
    run(None, (), [*qkv_far, *packs, qkv_core], [*qkv_far, *packs])
    w, own, ke, oh, near_t, smalls, full_up_bias = run(
        lambda *a: prepare(index, *a),
        ((pack, *(p.result for p in packs)), layout_cells, pad_mask),
        [*qkv_far, down_far],
        [*qkv_far, down_far, qkv_core],
    )
    qkv_cores = cores_of(qkv_far)
    run(None, (), [*qkv_cores, up_core])
    qkv_parts = parts_of(qkv_shard, qkv_core, qkv_far, qkv_cores)
    qkv = run(
        lambda *a: project(index, qkv_parts, *a),
        (tokens, smalls),
        [up_far[0], down_far, down_core],
    )
    quarters = list(down_far.result)
    line = [chain(quarter, "dp", 2) for quarter in quarters]
    cores = [chain(quarter, "fsdp", 1) for quarter in quarters]
    old = run(
        lambda *a: attend(FORWARD_GROUPS[0], *a),
        (qkv, w, own, ke, near_t),
        [up_far[1], up_far[0], line[0], *cores],
    )
    up_cores = cores_of(up_far[:1])
    cores.append(chain(line[0].result, "fsdp", 1))
    mixed, lse = run(
        lambda *a: attend(FORWARD_GROUPS[1], *a),
        (qkv, w, own, ke, near_t, old),
        [up_far[1], line[1], *up_cores, cores[2]],
    )
    up_cores += cores_of(up_far[1:])
    cores.append(chain(line[1].result, "fsdp", 1))
    run(None, (), [*up_cores[2:], cores[3]])
    up_parts = parts_of(up_shard, up_core, up_far, up_cores)
    quarters += [c.result for c in line]
    down_parts = [down_weight, down_core.result, *quarters, *(c.result for c in cores)]
    result, dfinal, resid, slope, sums_two, *down_rows = run(
        lambda *a: forward(index, up_parts, down_parts, *a),
        (mixed, tokens, cotangent, smalls, full_up_bias),
    )

    down_sum = Chain(reduce_steps(*down_rows))
    run(None, (), [down_sum])
    dresid, dmixed, sums_one, up_sums, *up_rows = run(
        lambda *a: backward(index, up_parts, down_parts, *a),
        (dfinal, resid, slope, mixed, smalls),
        [down_sum],
    )
    first_sum = Chain(reduce_steps(*up_rows[:2]))
    second_sum = Chain(reduce_steps(*up_rows[2:]))
    run(None, (), [first_sum])

    def back(at, room, begin, old=()):
        return run(
            lambda *a: attend_back(GROUPS[at], room, index, *a),
            (qkv, w, own, ke, oh, near_t, dmixed, mixed, lse, tokens, old),
            begin,
        )

    columns = 3 * width * 2 // 3
    backs = [back(0, columns, [first_sum, down_sum, second_sum])]
    backs.append(back(1, columns, [second_sum, down_sum, first_sum], tuple(backs[0][6:])))
    early_sum = Chain(reduce_steps(*backs[1][6:]))
    run(None, (), [early_sum])
    backs.append(back(2, columns // 2 + 128, [early_sum, down_sum, second_sum]))
    late_rows = run(
        lambda *a: small_gradients(index, *a),
        ([group[3:6] for group in backs], sums_one, sums_two, up_sums, *backs[2][6:]),
        [early_sum, first_sum, down_sum],
    )
    late_sum = Chain(reduce_steps(*late_rows))
    run(None, (), [late_sum])
    input_grad = run(
        lambda *a: input_gradient(index, qkv_parts, *a),
        ([array for group in backs for array in group[:3]], dresid),
        [late_sum, early_sum, first_sum, second_sum, down_sum],
    )
    chains = [late_sum, early_sum, second_sum, first_sum, down_sum]
    while any(c.move is not None for c in chains):
        left = [c for c in chains if c.move is not None]
        for c in left:
            run(None, (), [c], [])
        for c in left:
            run(None, (), [], [c])
    halves = [c.result for c in (down_sum, first_sum, second_sum)]
    ordered = [in_order(*pair, parity).astype(F32) * factor for pair in halves]
    grad_up = side([ordered[1][:, width:], ordered[2]], axis=1)
    *grad_qkv, tail = unpack(index, early_sum.result, late_sum.result, factor)
    return (
        result,
        input_grad,
        *grad_qkv,
        ordered[1][:, :width],
        tail[0],
        tail[1],
        tail[2],
        tail[12:14].reshape(-1)[: 3 * 96].reshape(3, 96),
        tail[3],
        tail[4],
        grad_up,
        tail[8:12].reshape(-1),
        ordered[0],
        tail[5],
        tail[6],
        tail[7],
    )


def solution(mesh):
    rows = P(("dp", "fsdp"), None)
    matrix, vector = P("fsdp", None), P("fsdp")
    return jax.shard_map(
        on_device,
        mesh=mesh,
        in_specs=(
            rows, P(None, ("dp", "fsdp")), P(("dp", "fsdp")),
            matrix, matrix, matrix, matrix,
            vector, vector, vector, matrix, vector, vector,
            matrix, vector, matrix, vector, vector, vector,
            rows,
        ),
        out_specs=(
            rows, rows,
            matrix, matrix, matrix, matrix,
            vector, vector, vector, matrix, vector, vector,
            matrix, vector, matrix, vector, vector, vector,
        ),
        check_vma=False,
    )
```

```python
import functools
import math

import jax
import jax.numpy as jnp
import numpy as np
from jax import lax
from jax.experimental import pallas as pl
from jax.experimental.pallas import tpu as pltpu
from jax.sharding import PartitionSpec as P

HEADS = 12
HD = 64
WIN = 512
BUCKETS = 32
PAIRS = HEADS // 2
SCALE = HD ** (-0.5)
EPS = 1e-05
BF = jnp.bfloat16
F32 = jnp.float32
VMEM_LIMIT = 60 * 1024 * 1024
GROUPS = ((0, 2), (2, 2), (4, 2))
FORWARD_GROUPS = ((0, 3), (3, 3))


def params():
    return pltpu.CompilerParams(vmem_limit_bytes=VMEM_LIMIT)


def cost(flops, nbytes, transcendentals=0):
    return pl.CostEstimate(
        flops=int(flops / 100),
        bytes_accessed=int(nbytes / 100),
        transcendentals=int(transcendentals / 100),
    )


def struct(shape, dtype):
    return jax.ShapeDtypeStruct(shape, dtype)


def whole(array):
    return pl.BlockSpec(array.shape, lambda *at: (0,) * len(array.shape))


def dot(left, right):
    return lax.dot_general(left, right, (((1,), (0,)), ((), ())), preferred_element_type=F32)


def dot_t(left, right):
    return lax.dot_general(left, right, (((1,), (1,)), ((), ())), preferred_element_type=F32)


def tdot(left, right):
    return lax.dot_general(left, right, (((0,), (0,)), ((), ())), preferred_element_type=F32)


def split3(values):
    high = values.astype(BF)
    rest = values - high.astype(F32)
    middle = rest.astype(BF)
    return high, middle, (rest - middle.astype(F32)).astype(BF)


def swap(array, axis, bit):
    return lax.ppermute(array, axis, [(i, i ^ bit) for i in range(lax.axis_size(axis))])


def together(*groups):
    flat, tree = jax.tree.flatten(groups)
    return jax.tree.unflatten(tree, lax.optimization_barrier(tuple(flat)))


def half_of(array, which, axis=0):
    rows = array.shape[axis] // 2
    return lax.dynamic_slice_in_dim(array, which * rows, rows, axis)


class Chain:
    def __init__(self, steps):
        self.steps = steps
        self.result = None
        self.move = next(steps)

    def advance(self, arrived):
        try:
            self.move = self.steps.send(arrived)
        except StopIteration as stop:
            self.move, self.result = None, stop.value


def run(call, arrays, begin=(), finish=None):
    finish = begin if finish is None else finish
    arrays, sent = together(arrays, [chain.move[0] for chain in begin])
    for chain, array in zip(begin, sent):
        chain.flight = swap(array, chain.move[1], chain.move[2])
    out = call(*arrays) if call is not None else ()
    out, arrived = together(out, [chain.flight for chain in finish])
    for chain, array in zip(finish, arrived):
        chain.advance(array)
    return out


def gather_far(piece, bit):
    far = yield piece, "fsdp", 2
    beside = yield far, "dp", bit
    return far, beside


def send_once(array, axis, bit):
    arrived = yield array, axis, bit
    return arrived


def part_rows(index, rows, count):
    me, near, beside = index[0], index[1], index[2]
    places = [(me * rows, rows), ((me ^ 1) * rows, rows)]
    if count == QUARTERS:
        quarter = rows // 4
        firsts = [
            (2 * line + side) * quarter
            for line in (beside, 1 - beside)
            for side in (near, 1 - near)
        ]
        return places + [
            ((me ^ other) * rows + first, quarter) for other in (2, 3) for first in firsts
        ]
    if count == PARTS:
        third = rows // 3
        firsts = (near * third, (1 - near) * third, 2 * third)
        return places + [((me ^ other) * rows + first, third) for other in (2, 3) for first in firsts]
    half, pieces = rows // 2, (count - 2) // 4
    size = half // pieces
    for piece in range(pieces):
        for other in (2, 3):
            for side in (near, 1 - near):
                places.append(((me ^ other) * rows + side * half + piece * size, size))
    return places


PARTS, BIG_PARTS, QUARTERS = 8, 10, 11


def fetch_copies(index, parts, whole, sems, count=None):
    places = part_rows(index, whole.shape[0] // 4, count or len(parts))
    return [
        pltpu.make_async_copy(part, whole.at[pl.ds(pl.multiple_of(first, 16), size)], sems.at[at])
        for at, (part, (first, size)) in enumerate(zip(parts, places))
    ]


def start_copies(copies):
    for copy in copies:
        copy.start()


def wait_copies(copies):
    for copy in copies:
        copy.wait()


ANY = pl.BlockSpec(memory_space=pl.ANY)
SMEM = pl.BlockSpec(memory_space=pltpu.SMEM)


def reduce_steps(keep, send, line_first=False):
    place = lax.axis_index("dp")

    def add(*arrays):
        return functools.reduce(jnp.add, [array.astype(F32) for array in arrays]).astype(BF)

    got = yield send, "fsdp", 1
    bits = [1, 2]
    if line_first:
        bits = [2, 1]
        total = add(keep, got)
        which = (place // 2) & 1
        got = yield half_of(total, 1 - which, 1), "dp", 2
        total = add(half_of(total, which, 1), got)
        far = yield total[1], "fsdp", 2
        total = add(total[0], far)
    else:
        far = yield add(keep[1], got[1]), "fsdp", 2
        total = add(keep[0], got[0], far)
    for bit in bits[1:] if line_first else bits:
        which = (place // bit) & 1
        got = yield half_of(total, 1 - which), "dp", bit
        total = add(half_of(total, which), got)
    bit = 4
    while bit < lax.axis_size("dp"):
        got = yield total, "dp", bit
        total = add(total, got)
        bit *= 2
    got = yield total, "dp", bits[1]
    total = in_order(total, got, (place // bits[1]) & 1)
    got = yield total, "dp", bits[0]
    return total, got, (place // bits[0]) & 1


def in_order(mine, other, which):
    return jnp.where(
        which == 0, jnp.concatenate([mine, other]), jnp.concatenate([other, mine])
    )


def table_places():
    step = np.arange(128)
    step = np.where(step < 64, -step, 128 - step)
    near = np.clip(step, -16, 15) + 16
    far = np.where(step <= -2, 0, np.where(step >= 2, 31, -1))
    wide = np.arange(256)
    wide = np.where(wide < 128, -wide, 256 - wide)
    places = np.concatenate([near + 32, near + 64, far, np.clip(wide, -16, 15) + 16])
    return places.astype(np.int32)[None, :]


def diagonal_places():
    lane = np.arange(128)
    x_place = np.where(lane < 63, np.clip(lane - 31, -16, 15) + 48, -1)
    y_place = np.where((lane >= 32) & (lane < 95), np.clip(lane - 63, -16, 15) + 80, -1)
    step = lane - 95
    block_place = np.where(
        (lane >= 64) & (step <= -2), 0, np.where((lane < 127) & (step >= 2), 31, -1)
    )
    step = (127 - np.arange(256) + 128) % 256 - 128
    places = np.concatenate([x_place, y_place, block_place, np.clip(step, -16, 15) + 16])
    return places.astype(np.int32)[:, None]


LANES = 640


def iota(shape, axis):
    return lax.broadcasted_iota(jnp.int32, shape, axis)


def as_bf(mask):
    return jnp.where(mask, 1.0, 0.0).astype(BF)


def near_mask():
    r, c = iota((128, 256), 0), iota((128, 256), 1)
    gap = (r >> 4) - (c >> 4)
    inside = (c < 128) & (gap <= 1) & (gap >= -1)
    return inside | ((r >= 112) & (c >= 128) & (c < 144)) | ((r < 16) & (c >= 240))


def hot_places(x, y, shape, axis):
    column = iota(shape, axis)
    block = (iota(shape, 1 - axis) & (WIN - 1)) >> 4
    third = column >> 5
    hot = jnp.where(third == 0, x, jnp.where(third == 1, y + 32, block + 64)) == column
    return column, hot & (column < 96)


PACK_ROWS, UP_ROW, TABLE_ROW = 16, 8, 10


def pack_vectors(vectors, up_bias, table):
    width, shard = up_bias.shape[0], vectors[0].shape[0]
    row = lax.broadcasted_iota(jnp.int32, (PACK_ROWS, shard), 0)
    pack = jnp.zeros((PACK_ROWS, shard), BF)
    for at, vector in enumerate(vectors):
        pack = jnp.where(row == at, vector[None, :], pack)
    pack = jnp.pad(pack, ((0, 0), (0, width - shard)))
    row = lax.broadcasted_iota(jnp.int32, (PACK_ROWS, width), 0)
    pack = jnp.where(row == UP_ROW, up_bias[None, :], pack)
    below = PACK_ROWS - TABLE_ROW - table.shape[0]
    return pack + jnp.pad(table, ((TABLE_ROW, below), (0, width - table.shape[1])))


def prep_kernel(
    index, p0, p1, p2, p3, cells_ref, mask_ref, places_ref,
    w_ref, own_ref, ke_ref, oh_ref, dt_ref, vectors_ref, up_bias_ref, packs,
):
    tokens = cells_ref.shape[1]
    me = index[0]
    for at, ref in enumerate((p0, p1, p2, p3)):
        packs[at] = ref[...]
    vectors = 0.0
    width = vectors_ref.shape[1]
    for at in range(4):
        rows = packs[me ^ at].astype(F32)
        vectors = vectors + pltpu.roll(rows[:8], at * (width // 4), 1)
        up_bias_ref[:, at * width : at * width + width] = rows[UP_ROW : UP_ROW + 1]
    vectors_ref[...] = vectors
    x, y, valid = cells_ref[0:1, :], cells_ref[1:2, :], mask_ref[...]
    column, hot = hot_places(x, y, (128, tokens), 0)
    own_ref[...] = as_bf(hot | (column == 96))
    sub = iota((8, tokens), 0)
    columns = jnp.where(sub == 0, x, jnp.where(sub == 1, y, valid)).astype(F32)
    columns = columns.T.astype(jnp.int32)
    x, y, valid = columns[:, 0:1], columns[:, 1:2], columns[:, 2:3]
    column, hot = hot_places(x, y, (tokens, 128), 1)
    masked = jnp.where((column == 99) & (valid <= 0), -1e30, 0.0)
    ones = hot | ((column >= 96) & (column < 99))
    ke_ref[...] = jnp.where(ones, 1.0, masked).astype(BF)
    block = (iota((tokens, 128), 0) & (WIN - 1)) >> 4
    third = column >> 5
    back = jnp.where(third == 0, 31 - x, jnp.where(third == 1, 63 - y, 95 - block)) == column
    oh_ref[...] = as_bf(back & (column < 96))

    pick = as_bf(iota((128, LANES), 0) == places_ref[...])
    lane = iota((32, 128), 1)
    mask = near_mask()
    for part in range(4):
        table = dot(packs[me ^ part][:, :128], pick)
        for head in range(HEADS // 4):
            row = table[TABLE_ROW + head : TABLE_ROW + head + 1]
            blocks = []
            for at in range(3):
                spread = jnp.broadcast_to(row[:, at * 128 : at * 128 + 128], (32, 128))
                spread = pltpu.roll(spread, at * 32, 1, stride=1, stride_axis=0)
                blocks.append(jnp.where(lane >> 5 == at, spread, 0.0))
            blocks.append(jnp.where((iota((32, 128), 0) == 3) & (lane == 96), 1.0, 0.0))
            place = part * (HEADS // 4) + head
            w_ref[place] = jnp.concatenate(blocks, axis=0).astype(BF)
            wide = jnp.broadcast_to(row[:, 384:640], (128, 256))
            rolled = pltpu.roll(wide, 0, 1, stride=1, stride_axis=0)
            dt_ref[place] = jnp.where(mask, rolled, 0.0).astype(BF)


def prepare(index, packs, layout_cells, pad_mask):
    tokens = pad_mask.shape[0]
    width = packs[0].shape[1]
    shapes = [
        struct((HEADS, 128, 128), BF),
        struct((128, tokens), BF),
        struct((tokens, 128), BF),
        struct((tokens, 128), BF),
        struct((HEADS, 128, 256), BF),
        struct((8, width), F32),
        struct((1, 4 * width), F32),
    ]
    arrays = [*packs, layout_cells, pad_mask.reshape(1, tokens), jnp.asarray(table_places())]
    return pl.pallas_call(
        prep_kernel,
        grid=(1,),
        in_specs=[SMEM] + [whole(array) for array in arrays],
        out_specs=[whole(shape) for shape in shapes],
        out_shape=shapes,
        scratch_shapes=[pltpu.VMEM((4, PACK_ROWS, width), BF)],
        compiler_params=params(),
        cost_estimate=cost(1e7, 3e6),
        name="prepare",
    )(index, *arrays)


def side_kernel(pieces, index, *refs):
    shards, outs = refs[: -1 - len(pieces)], refs[-1 - len(pieces) :]
    first = 0
    for ref in shards:
        columns = slice(first, first + ref.shape[1])
        first += ref.shape[1]
        outs[0][:, columns] = ref[...]
        for out, (start, step) in zip(outs[1:], pieces):
            row = pl.multiple_of(start + index[1] * step, 16)
            out[:, columns] = ref[pl.ds(row, out.shape[0]), :]


def side_by_side(index, shards, rows, pieces):
    columns = sum(shard.shape[1] for shard in shards)
    outs = [struct((shards[0].shape[0], columns), BF)] + [struct((rows, columns), BF)] * len(pieces)
    return pl.pallas_call(
        functools.partial(side_kernel, pieces),
        grid=(1,),
        in_specs=[SMEM] + [whole(shard) for shard in shards],
        out_specs=[whole(shape) for shape in outs],
        out_shape=outs,
        compiler_params=params(),
        cost_estimate=cost(0, 3e6),
        name="side_by_side",
    )(index, *shards)


def project_kernel(index, *refs):
    parts, (x_ref, bias_ref, out_ref, weight, sems) = refs[:PARTS], refs[PARTS:]

    @pl.when(pl.program_id(0) == 0)
    def _():
        copies = fetch_copies(index, parts, weight, sems)
        start_copies(copies)
        wait_copies(copies)

    width = x_ref.shape[1]
    for at in range(3):
        values = dot(x_ref[...], weight[:, at * width : (at + 1) * width])
        if at == 0:
            values = (values + bias_ref[0:1, :]).astype(BF) * SCALE
        if at == 2:
            values = values + bias_ref[1:2, :]
        values = values.astype(BF)
        for pair in range(PAIRS):
            out_ref[at * PAIRS + pair] = values[:, pair * 128 : pair * 128 + 128]


def project(index, parts, tokens, biases, block=512):
    rows, width = tokens.shape
    return pl.pallas_call(
        project_kernel,
        grid=(rows // block,),
        in_specs=[SMEM]
        + [ANY] * PARTS
        + [
            pl.BlockSpec((block, width), lambda i: (i, 0)),
            pl.BlockSpec((8, width), lambda i: (0, 0)),
        ],
        out_specs=pl.BlockSpec((3 * PAIRS, block, 128), lambda i: (0, i, 0)),
        out_shape=struct((3 * PAIRS, rows, 128), BF),
        scratch_shapes=[pltpu.VMEM((width, 3 * width), BF), pltpu.SemaphoreType.DMA((PARTS,))],
        compiler_params=params(),
        cost_estimate=cost(6 * rows * width * width, 10e6),
        name="project",
    )(index, *parts, tokens, biases)


def join(ref):
    return jnp.concatenate([ref[at] for at in range(ref.shape[0])], axis=1)


def input_kernel(index, *refs):
    count = len(GROUPS) * 3
    parts, grads = refs[:PARTS], refs[PARTS : PARTS + count]
    dresid_ref, out_ref, weight, sems = refs[PARTS + count :]

    @pl.when(pl.program_id(0) == 0)
    def _():
        copies = fetch_copies(index, parts, weight, sems)
        start_copies(copies)
        wait_copies(copies)

    joined = [join(grads[3 * group + at]) for at in range(3) for group in range(len(GROUPS))]
    total = dot_t(jnp.concatenate(joined, axis=1), weight[...])
    out_ref[...] = (dresid_ref[...] + total).astype(BF)


def input_gradient(index, parts, grads, dresid, block=256):
    rows, width = dresid.shape
    spec = pl.BlockSpec((block, width), lambda i: (i, 0))
    pairs = [pl.BlockSpec((a.shape[0], block, 128), lambda i: (0, i, 0)) for a in grads]
    return pl.pallas_call(
        input_kernel,
        grid=(rows // block,),
        in_specs=[SMEM] + [ANY] * PARTS + pairs + [spec],
        out_specs=spec,
        out_shape=struct((rows, width), BF),
        scratch_shapes=[pltpu.VMEM((width, 3 * width), BF), pltpu.SemaphoreType.DMA((PARTS,))],
        compiler_params=params(),
        cost_estimate=cost(6 * rows * width * width, 13e6),
        name="input_gradient",
    )(index, *parts, *grads, dresid)


def with_near(pieces, tile, at):
    pieces = list(pieces)
    pieces[at] = pieces[at] + tile[:, :128]
    if at > 0:
        left = pieces[at - 1]
        pieces[at - 1] = jnp.concatenate([left[:16] + tile[:16, 128:], left[16:]], axis=0)
    if at < 3:
        right = pieces[at + 1]
        pieces[at + 1] = jnp.concatenate([right[:112], right[112:] + tile[112:, 128:]], axis=0)
    return pieces


def lane_blocks(values):
    return [values[:, c * 128 : c * 128 + 128] for c in range(WIN // 128)]


def attend_kernel(
    q_ref, k_ref, v_ref, w_ref, own_ref, ke_ref, dt_ref, out_ref, lse_ref, s_scr, p_scr
):
    first = iota((128, WIN), 0) < HD
    windows = [slice(at, at + WIN) for at in range(0, q_ref.shape[0], WIN)]
    extras = dot(w_ref[...].reshape(256, 128), own_ref[...]).astype(BF)
    values = []
    for at, rows in enumerate(windows):
        keys = jnp.concatenate([k_ref[rows, :], ke_ref[rows, :]], axis=1)
        query_t = q_ref[rows, :].T
        values.append(v_ref[rows, :].T)
        for head in range(2):
            mine = first if head == 0 else ~first
            query = jnp.where(mine, query_t, jnp.zeros((), BF))
            extra = extras[head * 128 : head * 128 + 128, rows]
            s_scr[2 * at + head] = dot(keys, jnp.concatenate([query, extra], axis=0))
    for at, rows in enumerate(windows):
        mixed = []
        for head in range(2):
            place = 2 * at + head
            tile = dt_ref[head].astype(F32)
            scores = [
                with_near(lane_blocks(s_scr[place, row : row + 128, :]), tile, row // 128)
                for row in range(0, WIN, 128)
            ]
            tops, totals = [], []
            for column in range(WIN // 128):
                pieces = [row[column] for row in scores]
                top = jnp.maximum(
                    jnp.maximum(pieces[0], pieces[1]), jnp.maximum(pieces[2], pieces[3])
                )
                top = jnp.max(top, axis=0, keepdims=True)
                pieces = [jnp.exp(piece - top) for piece in pieces]
                total = (pieces[0] + pieces[1]) + (pieces[2] + pieces[3])
                totals.append(jnp.sum(total, axis=0, keepdims=True))
                tops.append(top)
                span = slice(column * 128, column * 128 + 128)
                for row, piece in enumerate(pieces):
                    p_scr[place, row * 128 : row * 128 + 128, span] = piece.astype(BF)
            total = jnp.concatenate(totals, axis=1)
            mixed.append(dot(values[at][head * HD : head * HD + HD], p_scr[place]) / total)
            lse_ref[head : head + 1, rows] = jnp.concatenate(tops, axis=1) + jnp.log(total)
        out_ref[rows, :] = jnp.concatenate(mixed, axis=0).astype(BF).T


def pair_block(tokens, shift):
    return pl.BlockSpec((None, tokens, 128), lambda p: (p + shift, 0, 0))


def attend(group, qkv, w, own, ke, near_t, old=()):
    start, pairs = group
    tokens = qkv.shape[1]
    scores = 2 * (tokens // WIN)
    kernel = attend_kernel
    if old:
        kernel = lambda *refs: attend_kernel(*refs[:7], *refs[9:])
    return pl.pallas_call(
        kernel,
        grid=(pairs,),
        in_specs=[
            pair_block(tokens, start),
            pair_block(tokens, start + PAIRS),
            pair_block(tokens, start + 2 * PAIRS),
            pl.BlockSpec((2, 128, 128), lambda p: (p + start, 0, 0)),
            whole(own),
            whole(ke),
            pl.BlockSpec((2, 128, 256), lambda p: (p + start, 0, 0)),
        ]
        + [ANY] * len(old),
        out_specs=[
            pair_block(tokens, start),
            pl.BlockSpec((None, 8, tokens), lambda p: (p + start, 0, 0)),
        ],
        out_shape=[struct((PAIRS, tokens, 128), BF), struct((PAIRS, 8, tokens), F32)],
        input_output_aliases={7: 0, 8: 1} if old else {},
        scratch_shapes=[pltpu.VMEM((scores, WIN, WIN), F32), pltpu.VMEM((scores, WIN, WIN), BF)],
        compiler_params=params(),
        cost_estimate=cost(tokens * WIN * pairs * 1536, 4e6 * pairs / 2, tokens * WIN * 2 * pairs),
        name="attend",
    )(qkv, qkv, qkv, w, own, ke, near_t, *old)


def diagonal_rows(sums):
    lane = iota((32, 128), 1)
    rows = []
    for at in range(3):
        block = jnp.where(lane >> 5 == at, sums[at * 32 : at * 32 + 32], 0.0)
        rolled = pltpu.roll(block, 0, 1, stride=1, stride_axis=0)
        rows.append(jnp.sum(rolled, axis=0, keepdims=True))
    return rows


def near_rows(tile):
    tile = jnp.where(near_mask(), tile, 0.0)
    turn = as_bf(iota((128, 128), 0) + iota((128, 128), 1) == 127)
    high, middle, low = split3(tile)
    turned = dot(turn, high) + dot(turn, middle) + dot(turn, low)
    rolled = pltpu.roll(turned, 0, 1, stride=1, stride_axis=0)
    return jnp.sum(rolled, axis=0, keepdims=True)


def attend_back_kernel(
    index, q_ref, k_ref, v_ref, w_ref, own_ref, ke_ref, oh_ref, dt_ref, do_ref, o_ref, lse_ref,
    x_ref, dq_ref, dk_ref, dv_ref, bias_ref, far_ref, near_ref, keep_ref, send_ref,
    s_scr, dp_scr, p_scr, ds_scr, x_t, products,
):
    @pl.when(pl.program_id(0) == 0)
    def _():
        x_t[...] = x_ref[...].T

    zero = jnp.zeros((), BF)
    first = iota((WIN, 128), 1) < HD
    first_t = iota((128, WIN), 0) < HD
    place = iota((128, WIN), 0)
    windows = [slice(at, at + WIN) for at in range(0, q_ref.shape[0], WIN)]
    extra_columns = dot(w_ref[...].reshape(256, 128), own_ref[...]).astype(BF)
    keys_t = []
    for at, rows in enumerate(windows):
        keys = jnp.concatenate([k_ref[rows, :], ke_ref[rows, :]], axis=1)
        values = jnp.concatenate([v_ref[rows, :], ke_ref[rows, :]], axis=1)
        keys_t.append(k_ref[rows, :].T)
        query_t, grad_t = q_ref[rows, :].T, do_ref[rows, :].T
        product = grad_t.astype(F32) * o_ref[rows, :].T.astype(F32)
        for head in range(2):
            mine = first_t if head == 0 else ~first_t
            delta = -jnp.sum(product[head * HD : head * HD + HD], axis=0, keepdims=True)
            minus = jnp.zeros((128, WIN), BF)
            extra = extra_columns[head * 128 : head * 128 + 128, rows]
            parts = split3(-lse_ref[head : head + 1, rows])
            for part, (less, less_delta) in enumerate(zip(parts, split3(delta))):
                extra = jnp.where(place == 96 + part, less, extra)
                minus = jnp.where(place == 96 + part, less_delta, minus)
            query = jnp.where(mine, query_t, zero)
            grad = jnp.where(mine, grad_t, zero)
            s_scr[2 * at + head] = dot(keys, jnp.concatenate([query, extra], axis=0))
            dp_scr[2 * at + head] = dot(values, jnp.concatenate([grad, minus], axis=0))
    plus = lambda total, term: term if total is None else total + term
    far_left, diag, low, high = [], [None] * 2, [None] * 2, [None] * 2
    bias_sums = [None] * 2
    for at, rows in enumerate(windows):
        dq_t, extras, dk, dv = [], [], None, None
        for head in range(2):
            mine = first if head == 0 else ~first
            query = jnp.where(mine, q_ref[rows, :], zero)
            grad = jnp.where(mine, do_ref[rows, :], zero)
            tile = dt_ref[head].astype(F32)
            place = 2 * at + head
            for block in range(WIN // 128):
                span = slice(block * 128, block * 128 + 128)
                scores = with_near(lane_blocks(s_scr[place, span, :]), tile, block)
                probs = [jnp.exp(piece) for piece in scores]
                dprobs = lane_blocks(dp_scr[place, span, :])
                dscores = [a * b for a, b in zip(probs, dprobs)]
                p_scr[place, span, :] = jnp.concatenate([a.astype(BF) for a in probs], axis=1)
                ds_scr[place, span, :] = jnp.concatenate([a.astype(BF) for a in dscores], axis=1)
                diag[head] = plus(diag[head], dscores[block])
                if block > 0:
                    low[head] = plus(low[head], dscores[block - 1][:16])
                if block < 3:
                    high[head] = plus(high[head], dscores[block + 1][112:])
            dv = plus(dv, dot(p_scr[place], grad))
            dk = plus(dk, dot(ds_scr[place], query))
            left = jnp.concatenate(
                [keys_t[at][head * HD : head * HD + HD], own_ref[:96, rows]], axis=0
            )
            both = dot(left, ds_scr[place])
            dq_t.append(both[:HD] * SCALE)
            extras.append(both[HD:].astype(BF))
        far_left.append(jnp.concatenate(extras, axis=0))
        dq = jnp.concatenate(dq_t, axis=0).astype(BF).T
        dv = dv.astype(BF)
        dq_ref[rows, :] = dq
        dk_ref[rows, :] = dk.astype(BF)
        dv_ref[rows, :] = dv
        for which, array in enumerate((dq, dv)):
            total = jnp.sum(array.astype(F32), axis=0, keepdims=True)
            bias_sums[which] = plus(bias_sums[which], total)
    grads = jnp.concatenate([dq_ref[...], dk_ref[...], dv_ref[...]], axis=1)
    products[...] = dot(x_t[...], grads)
    place_rows(index, products, keep_ref, send_ref)
    bias_ref[...] = jnp.zeros_like(bias_ref)
    for which in range(2):
        bias_ref[which : which + 1, :] = bias_sums[which]
    far = dot(jnp.concatenate(far_left, axis=1), oh_ref[...])
    for head in range(2):
        sums = diagonal_rows(far[head * 96 : head * 96 + 96])
        far_ref[head] = jnp.concatenate(sums + [jnp.zeros((5, 128), F32)], axis=0)
        corners = jnp.concatenate([low[head], jnp.zeros((96, 128), F32), high[head]], axis=0)
        tile = jnp.concatenate([diag[head], corners], axis=1)
        near_ref[head] = jnp.broadcast_to(near_rows(tile), (8, 256))


def attend_back(
    group, room, index, qkv, w, own, ke, oh, near_t, dmixed, mixed, lse, x, old=()
):
    start, pairs = group
    kernel = attend_back_kernel
    if old:
        kernel = lambda *refs: attend_back_kernel(*refs[:13], *refs[15:])
    tokens, width = x.shape
    scores = 2 * (tokens // WIN)
    out = struct((pairs, tokens, 128), BF)
    weight_rows = struct((2, width // 4, room), BF)
    weight_block = pl.BlockSpec(
        (2, width // 4, 384), lambda p: (0, 0, p + (start if old else 0))
    )
    return pl.pallas_call(
        kernel,
        grid=(pairs,),
        in_specs=[
            SMEM,
            pair_block(tokens, start),
            pair_block(tokens, start + PAIRS),
            pair_block(tokens, start + 2 * PAIRS),
            pl.BlockSpec((2, 128, 128), lambda p: (p + start, 0, 0)),
            whole(own),
            whole(ke),
            whole(oh),
            pl.BlockSpec((2, 128, 256), lambda p: (p + start, 0, 0)),
            pair_block(tokens, start),
            pair_block(tokens, start),
            pl.BlockSpec((None, 8, tokens), lambda p: (p + start, 0, 0)),
            whole(x),
        ]
        + [ANY] * len(old),
        out_specs=[
            pair_block(tokens, 0),
            pair_block(tokens, 0),
            pair_block(tokens, 0),
            pl.BlockSpec((None, 8, 128), lambda p: (p, 0, 0)),
            pl.BlockSpec((2, 8, 128), lambda p: (p, 0, 0)),
            pl.BlockSpec((2, 8, 256), lambda p: (p, 0, 0)),
            weight_block,
            weight_block,
        ],
        out_shape=[
            out,
            out,
            out,
            struct((pairs, 8, 128), F32),
            struct((2 * pairs, 8, 128), F32),
            struct((2 * pairs, 8, 256), F32),
            weight_rows,
            weight_rows,
        ],
        input_output_aliases={13: 6, 14: 7} if old else {},
        scratch_shapes=[
            pltpu.VMEM((scores, WIN, WIN), F32),
            pltpu.VMEM((scores, WIN, WIN), F32),
            pltpu.VMEM((scores, WIN, WIN), BF),
            pltpu.VMEM((scores, WIN, WIN), BF),
            pltpu.VMEM((width, tokens), BF),
            pltpu.VMEM((width, 384), F32),
        ],
        compiler_params=params(),
        cost_estimate=cost(
            tokens * WIN * pairs * 2 * 2048, 12e6, tokens * WIN * pairs * 2
        ),
        name="attend_back",
    )(index, qkv, qkv, qkv, w, own, ke, oh, near_t, dmixed, mixed, lse, x, *old)


def norm_parts(values):
    centre = values - jnp.mean(values, axis=-1, keepdims=True)
    spread = jnp.mean(centre * centre, axis=-1, keepdims=True)
    scale = lax.rsqrt(spread + EPS)
    return centre * scale, scale


def norm_back(grad, hat, scale):
    mean = jnp.mean(grad, axis=-1, keepdims=True)
    along = jnp.mean(grad * hat, axis=-1, keepdims=True)
    return scale * (grad - mean - hat * along)


def add_rows(ref, rows):
    for at, values in enumerate(rows):
        ref[at : at + 1, :] += jnp.sum(values.astype(F32), axis=0, keepdims=True)


def gelu_and_slope(values):
    upto = 0.5 + 0.5 * lax.erf(values * math.sqrt(0.5))
    density = jnp.exp(values * values * -0.5) * (1.0 / math.sqrt(2.0 * math.pi))
    return values * upto, upto + values * density


def store_rows(index, total, keep, send, stage, sems):
    me, shard = index[0], keep.shape[1]
    copies = []
    for at, (which, ref) in enumerate(((1, send), (3, send), (2, keep), (0, keep))):
        rows = pl.ds(pl.multiple_of((me ^ which) * shard, 16), shard)
        stage[at] = total[rows, :].astype(BF)
        copies.append(pltpu.make_async_copy(stage.at[at], ref.at[which // 2], sems.at[at]))
        copies[-1].start()
    return copies


def forward_kernel(index, *refs):
    up_parts, down_parts = refs[:BIG_PARTS], refs[BIG_PARTS : 2 * BIG_PARTS]
    (
        mixed_ref, x_ref, cot_ref, small_ref, up_bias_ref,
        out_ref, dfinal_ref, resid_ref, slope_ref, sums_ref, keep_ref, send_ref,
        w_up, w_down, total, active_scr, stage, sems, out_sems,
    ) = refs[2 * BIG_PARTS :]
    step = pl.program_id(0)
    up_copies = fetch_copies(index, up_parts, w_up, sems.at[0])
    down_copies = fetch_copies(index, down_parts, w_down, sems.at[1], QUARTERS)

    @pl.when(step == 0)
    def _():
        start_copies(up_copies)
        start_copies(down_copies)
        for ref in (sums_ref, total):
            ref[...] = jnp.zeros_like(ref)
        wait_copies(up_copies)

    width, hidden = w_down.shape[1], w_down.shape[0]
    small = lambda at: small_ref[at + 2 : at + 3, :]
    resid = x_ref[...].astype(F32) + (dot(join(mixed_ref), w_up[:, :width]) + small(0))
    resid_ref[...] = resid
    hat, _ = norm_parts(resid)
    normed = hat * small(1) + small(2)
    low = normed.astype(BF)
    for at in range(0, hidden, width):
        span = slice(at, at + width)
        values = dot(low, w_up[:, at + width : at + 2 * width]) + up_bias_ref[:, span]
        active, slope = gelu_and_slope(values)
        active_scr[:, span] = active.astype(BF)
        slope_ref[:, span] = slope.astype(BF)

    @pl.when(step == 0)
    def _():
        wait_copies(down_copies)

    final = normed + dot(active_scr[...], w_down[...]) + small(3)
    hat, scale = norm_parts(final)
    out_ref[...] = (hat * small(4) + small(5)).astype(BF)
    cot = cot_ref[...].astype(F32)
    dfinal = norm_back(cot * small(4), hat, scale)
    dfinal_ref[...] = dfinal
    dbranch = dfinal.astype(BF)
    for at in range(0, hidden, width):
        total[at : at + width, :] += tdot(active_scr[:, at : at + width], dbranch)
    add_rows(sums_ref, (cot * hat, cot, dbranch))

    @pl.when(step == pl.num_programs(0) - 1)
    def _():
        wait_copies(store_rows(index, total, keep_ref, send_ref, stage, out_sems))


def forward(index, up_parts, down_parts, mixed, tokens, cotangent, smalls, up_bias, block=256):
    rows, width = tokens.shape
    hidden = up_bias.shape[1]
    spec = lambda columns: pl.BlockSpec((block, columns), lambda i: (i, 0))
    pairs = pl.BlockSpec((PAIRS, block, 128), lambda i: (0, i, 0))
    sums = struct((8, width), F32)
    down_rows = struct((2, hidden // 4, width), BF)
    return pl.pallas_call(
        forward_kernel,
        grid=(rows // block,),
        in_specs=[SMEM]
        + [ANY] * (2 * BIG_PARTS)
        + [pairs, spec(width), spec(width), whole(smalls), whole(up_bias)],
        out_specs=[spec(width), spec(width), spec(width), spec(hidden), whole(sums), ANY, ANY],
        out_shape=[
            struct((rows, width), BF),
            struct((rows, width), F32),
            struct((rows, width), F32),
            struct((rows, hidden), BF),
            sums,
            down_rows,
            down_rows,
        ],
        scratch_shapes=[
            pltpu.VMEM((width, width + hidden), BF),
            pltpu.VMEM((hidden, width), BF),
            pltpu.VMEM((hidden, width), F32),
            pltpu.VMEM((block, hidden), BF),
            pltpu.VMEM((4, hidden // 4, width), BF),
            pltpu.SemaphoreType.DMA((2, BIG_PARTS)),
            pltpu.SemaphoreType.DMA((4,)),
        ],
        compiler_params=params(),
        cost_estimate=cost(2 * rows * width * (width + 3 * hidden), 40e6),
        name="forward",
    )(index, *up_parts, *down_parts, mixed, tokens, cotangent, smalls, up_bias)


def backward_kernel(index, *refs):
    up_parts, down_parts = refs[:BIG_PARTS], refs[BIG_PARTS : 2 * BIG_PARTS]
    (
        dfinal_ref, resid_ref, slope_ref, mixed_ref, small_ref,
        dresid_ref, dmixed_ref, sums_ref, up_sums_ref, *row_refs,
        w_up, w_down, total, stage, sems, out_sems,
    ) = refs[2 * BIG_PARTS :]
    step = pl.program_id(0)

    @pl.when(step == 0)
    def _():
        copies = fetch_copies(index, down_parts, w_down, sems.at[0], QUARTERS)
        copies += fetch_copies(index, up_parts, w_up, sems.at[1])
        start_copies(copies)
        for ref in (sums_ref, up_sums_ref, total):
            ref[...] = jnp.zeros_like(ref)
        wait_copies(copies)

    width, hidden = w_down.shape[1], w_down.shape[0]
    small = lambda at: small_ref[at + 2 : at + 3, :]
    hat, scale = norm_parts(resid_ref[...])
    low_t = (hat * small(1) + small(2)).astype(BF).T
    dnormed = dfinal_ref[...]
    dbranch = dnormed.astype(BF)
    for at in range(0, hidden, width):
        span = slice(at, at + width)
        up_span = slice(at + width, at + 2 * width)
        dactive = dot_t(dbranch, w_down[span, :])
        dhidden = (dactive * slope_ref[:, span].astype(F32)).astype(BF)
        up_sums_ref[:, span] += jnp.sum(dhidden.astype(F32), axis=0, keepdims=True)
        total[:, up_span] += dot(low_t, dhidden)
        dnormed = dnormed + dot_t(dhidden, w_up[:, up_span])
    dresid = norm_back(dnormed * small(1), hat, scale)
    dresid_ref[...] = dresid
    dattn = dresid.astype(BF)
    dmixed = dot_t(dattn, w_up[:, :width]).astype(BF)
    for pair in range(PAIRS):
        dmixed_ref[pair] = dmixed[:, pair * 128 : pair * 128 + 128]
    total[:, :width] += tdot(join(mixed_ref), dattn)
    add_rows(sums_ref, (dnormed * hat, dnormed, dattn))

    @pl.when(step == pl.num_programs(0) - 1)
    def _():
        half = (width + hidden) // 2
        for at in range(2):
            columns = slice(at * half, at * half + half)
            wait_copies(
                store_rows(
                    index,
                    total.at[:, columns],
                    *row_refs[2 * at : 2 * at + 2],
                    stage.at[:, :, columns],
                    out_sems,
                )
            )


def backward(index, up_parts, down_parts, dfinal, resid, slope, mixed, smalls, block=256):
    rows, width = resid.shape
    hidden = slope.shape[1]
    spec = lambda columns: pl.BlockSpec((block, columns), lambda i: (i, 0))
    pairs = pl.BlockSpec((PAIRS, block, 128), lambda i: (0, i, 0))
    sums = [struct((8, width), F32), struct((1, hidden), F32)]
    up_rows = struct((2, width // 4, (width + hidden) // 2), BF)
    return pl.pallas_call(
        backward_kernel,
        grid=(rows // block,),
        in_specs=[SMEM]
        + [ANY] * (2 * BIG_PARTS)
        + [spec(width), spec(width), spec(hidden), pairs, whole(smalls)],
        out_specs=[spec(width), pairs] + [whole(shape) for shape in sums] + [ANY] * 4,
        out_shape=[struct((rows, width), F32), struct((PAIRS, rows, 128), BF)]
        + sums
        + [up_rows] * 4,
        scratch_shapes=[
            pltpu.VMEM((width, width + hidden), BF),
            pltpu.VMEM((hidden, width), BF),
            pltpu.VMEM((width, width + hidden), F32),
            pltpu.VMEM((4, width // 4, width + hidden), BF),
            pltpu.SemaphoreType.DMA((2, BIG_PARTS)),
            pltpu.SemaphoreType.DMA((4,)),
        ],
        compiler_params=params(),
        cost_estimate=cost(4 * rows * width * (width + 2 * hidden), 40e6),
        name="backward",
    )(index, *up_parts, *down_parts, dfinal, resid, slope, mixed, smalls)


def place_rows(index, total, keep_ref, send_ref):
    me, shard = index[0], keep_ref.shape[1]
    for at, ref in ((0, keep_ref), (2, keep_ref), (1, send_ref), (3, send_ref)):
        rows = pl.ds(pl.multiple_of((me ^ at) * shard, 16), shard)
        ref[at // 2] = total[rows, :].astype(BF)


def small_rows(refs, places, sums_one, sums_two, up_sums, rows, sums):
    width = rows.shape[1]
    shard = width // 4
    rows[...] = jnp.zeros_like(rows)
    sums[...] = jnp.zeros_like(sums)
    pair, head = 0, 0
    for bias, far, near in refs:
        for at in range(bias.shape[0]):
            rows[0:2, pair * 128 : pair * 128 + 128] = bias[at, 0:2, :]
            pair += 1
        for at in range(far.shape[0]):
            parts = [far[at, row : row + 1, :] for row in range(3)] + [near[at, 0:1, :]]
            sums[head : head + 1, :] = jnp.concatenate(parts, axis=1)
            head += 1
    for row, source in enumerate((2, 0, 1)):
        rows[row + 2 : row + 3, :] = sums_one[source : source + 1, :]
        rows[row + 5 : row + 6, :] = sums_two[source : source + 1, :]
    lane = iota((1, width), 1)
    for at in range(4):
        values = up_sums[:, at * width : at * width + width]
        inside = (lane >= at * shard) & (lane < (at + 1) * shard)
        for part in range(4):
            rolled = pltpu.roll(values, (at - part) % 4 * shard, 1)
            rows[8 + part : 9 + part, :] += jnp.where(inside, rolled, 0.0)
    pick = as_bf(places[...] == iota((LANES, 128), 1))
    table = sum(dot(part, pick) for part in split3(sums[...]))
    table = jnp.concatenate([table, jnp.zeros((table.shape[0], width - 128), F32)], axis=1)
    for at in range(HEADS):
        within = at % 3
        shift = at // 3 * shard + within % 2 * 96
        rolled = pltpu.roll(table[at : at + 1], shift, 1)
        rows[12 + within // 2 : 13 + within // 2, :] += rolled


def small_kernel(count, index, *refs):
    groups, refs = refs[: 3 * count], refs[3 * count :]
    (
        places, sums_one, sums_two, up_sums, keep_in, send_in, keep_ref, send_ref, total, rows, sums
    ) = refs
    del keep_in, send_in
    groups = [groups[at : at + 3] for at in range(0, 3 * count, 3)]
    small_rows(groups, places, sums_one, sums_two, up_sums, rows, sums)
    total[...] = rows[...].T
    place_rows(index, total, keep_ref, send_ref)


def small_gradients(index, groups, sums_one, sums_two, up_sums, keep, send):
    width = sums_one.shape[1]
    block = keep.shape[2] // 128 - 1
    arrays = [array for group in groups for array in group]
    arrays += [jnp.asarray(diagonal_places()), sums_one, sums_two, up_sums]
    out = pl.BlockSpec((2, width // 4, 128), lambda i: (0, 0, block))
    return pl.pallas_call(
        functools.partial(small_kernel, len(groups)),
        grid=(1,),
        in_specs=[SMEM] + [whole(array) for array in arrays] + [ANY, ANY],
        out_specs=[out, out],
        out_shape=[struct(keep.shape, BF)] * 2,
        input_output_aliases={len(arrays) + 1: 0, len(arrays) + 2: 1},
        scratch_shapes=[
            pltpu.VMEM((width, 128), F32),
            pltpu.VMEM((128, width), F32),
            pltpu.VMEM((16, LANES), F32),
        ],
        compiler_params=params(),
        cost_estimate=cost(1e7, 1e6),
        name="small_gradients",
    )(index, *arrays, keep, send)


def unpack_kernel(factor, index, *refs):
    halves, (query_ref, key_ref, value_ref) = refs[:4], refs[4:7]
    *vector_refs, up_bias_ref, table_ref, small_scr = refs[7:]
    half = halves[0].shape[0]
    for at in range(2):
        rows = pl.ds(pl.multiple_of((index[1] ^ at) * half, 16), half)
        first = 0
        for ref in (halves[at], halves[2 + at]):
            for column in range(0, ref.shape[1] // 384 * 384, 384):
                for which, out in enumerate((query_ref, key_ref, value_ref)):
                    place = column + which * 128
                    values = ref[:, place : place + 128].astype(F32) * factor
                    out[rows, first : first + 128] = values
                first += 128
        values = halves[2 + at][:, halves[2].shape[1] - 128 :]
        small_scr[rows, :] = values.astype(F32) * factor
    rows = small_scr[...].T
    for at, ref in enumerate(vector_refs):
        ref[...] = rows[at]
    up_bias_ref[...] = jnp.concatenate([rows[8 + at] for at in range(4)])
    table = jnp.concatenate([rows[12:13, :96], rows[12:13, 96:192], rows[13:14, :96]], axis=0)
    table_ref[...] = table


def unpack(index, early, late, factor):
    half, width = early[0].shape[0], PAIRS * 128
    arrays = [*early, *late]
    outs = [struct((2 * half, width), F32)] * 3 + [struct((2 * half,), F32)] * 8
    outs += [struct((8 * half,), F32), struct((HEADS // 4, 3 * BUCKETS), F32)]
    return pl.pallas_call(
        functools.partial(unpack_kernel, factor),
        grid=(1,),
        in_specs=[SMEM] + [whole(array) for array in arrays],
        out_specs=[whole(shape) for shape in outs],
        out_shape=outs,
        scratch_shapes=[pltpu.VMEM((2 * half, 128), F32)],
        compiler_params=params(),
        cost_estimate=cost(1e6, 3e6),
        name="unpack",
    )(index, *arrays)


def on_device(
    tokens,
    layout_cells,
    pad_mask,
    query_weight,
    key_weight,
    value_weight,
    out_weight,
    query_bias,
    value_bias,
    out_bias,
    bias_table,
    first_gain,
    first_shift,
    up_weight,
    up_bias,
    down_weight,
    down_bias,
    second_gain,
    second_shift,
    cotangent,
):
    rows, width = tokens.shape
    hidden = down_weight.shape[0] * 4
    shard = width // 4
    me = lax.axis_index("fsdp")
    parity = lax.axis_index("dp") & 1
    beside = (lax.axis_index("dp") >> 1) & 1
    index = jnp.stack([me, parity, beside]).astype(jnp.int32)
    factor = 1.0 / math.sqrt(rows * lax.axis_size("dp") * lax.axis_size("fsdp"))

    vectors = (
        query_bias, value_bias, out_bias, first_gain, first_shift, down_bias, second_gain,
        second_shift,
    )
    pack = pack_vectors(vectors, up_bias, bias_table)
    chain = lambda *args: Chain(send_once(*args))

    side = jnp.concatenate
    packs = [chain(pack, "fsdp", bit) for bit in (1, 2, 3)]
    third, piece = shard // 3, shard // 4
    qkv_shard, *qkv_thirds = side_by_side(
        index, (query_weight, key_weight, value_weight), third, ((0, third), (2 * third, 0))
    )

    def cores_of(chains):
        return [chain(part, "fsdp", 1) for far in chains for part in far.result]

    def parts_of(shard, core, chains, cores):
        parts = [shard, core.result]
        for at, far in enumerate(chains):
            parts += [*far.result, *(c.result for c in cores[2 * at : 2 * at + 2])]
        return parts

    out_weight, up_weight, qkv_thirds = together(out_weight, up_weight, qkv_thirds)
    qkv_far = Chain(gather_far(qkv_thirds[0], 1))
    qkv_direct = chain(qkv_thirds[1], "fsdp", 2)
    up_shard, *up_pieces = side_by_side(
        index, (out_weight, up_weight), piece, ((0, 2 * piece), (piece, 2 * piece))
    )
    up_far = [Chain(gather_far(half, 1)) for half in up_pieces]
    down_far = Chain(gather_far(half_of(half_of(down_weight, beside), parity), 1))
    qkv_core, up_core, down_core = (
        chain(shard, "fsdp", 1) for shard in (qkv_shard, up_shard, down_weight)
    )
    run(None, (), [qkv_far, *packs, qkv_direct, qkv_core], [qkv_far, *packs])
    w, own, ke, oh, near_t, smalls, full_up_bias = run(
        lambda *a: prepare(index, *a),
        ((pack, *(p.result for p in packs)), layout_cells, pad_mask),
        [qkv_far, down_far],
        [qkv_far, qkv_direct, qkv_core],
    )
    thirds = [*qkv_far.result, qkv_direct.result]
    qkv_cores = [chain(part, "fsdp", 1) for part in thirds]
    run(None, (), qkv_cores, [*qkv_cores, down_far])
    qkv_parts = [qkv_shard, qkv_core.result, *thirds, *(c.result for c in qkv_cores)]
    qkv = run(
        lambda *a: project(index, *a),
        (qkv_parts, tokens, smalls),
        [up_far[0], down_far, up_core, down_core],
    )
    quarters = list(down_far.result)
    line = [chain(quarter, "dp", 2) for quarter in quarters]
    cores = [chain(quarter, "fsdp", 1) for quarter in quarters]
    old = run(
        lambda *a: attend(FORWARD_GROUPS[0], *a),
        (qkv, w, own, ke, near_t),
        [up_far[1], up_far[0], line[0], *cores],
    )
    up_cores = cores_of(up_far[:1])
    cores.append(chain(line[0].result, "fsdp", 1))
    mixed, lse = run(
        lambda *a: attend(FORWARD_GROUPS[1], *a),
        (qkv, w, own, ke, near_t, old),
        [up_far[1], line[1], *up_cores, cores[2]],
    )
    up_cores += cores_of(up_far[1:])
    cores.append(chain(line[1].result, "fsdp", 1))
    run(None, (), [*up_cores[2:], cores[3]])
    up_parts = parts_of(up_shard, up_core, up_far, up_cores)
    quarters += [c.result for c in line]
    down_parts = [down_weight, down_core.result, *quarters, *(c.result for c in cores)]
    result, dfinal, resid, slope, sums_two, *down_rows = run(
        lambda *a: forward(index, up_parts, down_parts, *a),
        (mixed, tokens, cotangent, smalls, full_up_bias),
    )

    down_sum = Chain(reduce_steps(*down_rows))
    run(None, (), [down_sum])
    dresid, dmixed, sums_one, up_sums, *up_rows = run(
        lambda *a: backward(index, up_parts, down_parts, *a),
        (dfinal, resid, slope, mixed, smalls),
        [down_sum],
    )
    first_sum = Chain(reduce_steps(*up_rows[:2]))
    second_sum = Chain(reduce_steps(*up_rows[2:], line_first=True))
    run(None, (), [first_sum, second_sum])

    def back(at, room, begin, finish, old=()):
        return run(
            lambda *a: attend_back(GROUPS[at], room, index, *a),
            (qkv, w, own, ke, oh, near_t, dmixed, mixed, lse, tokens, old),
            begin,
            finish,
        )

    columns = 384 * (GROUPS[0][1] + GROUPS[1][1])
    three = [first_sum, second_sum, down_sum]
    backs = [back(0, columns, three, three)]
    backs.append(back(1, columns, three, three, tuple(backs[0][6:])))
    early_sum = Chain(reduce_steps(*backs[1][6:]))
    run(None, (), [early_sum])
    room = 3 * width + 128 - columns
    backs.append(back(2, room, [early_sum, *three], [early_sum, *three]))
    late_rows = run(
        lambda *a: small_gradients(index, *a),
        ([group[3:6] for group in backs], sums_one, sums_two, up_sums, *backs[2][6:]),
    )
    late_sum = Chain(reduce_steps(*late_rows))
    run(None, (), [late_sum])
    input_grad = run(
        lambda *a: input_gradient(index, qkv_parts, *a),
        ([array for group in backs for array in group[:3]], dresid),
        [late_sum, early_sum, second_sum, down_sum, first_sum],
        [late_sum, early_sum, second_sum, down_sum],
    )
    run(None, (), [late_sum, early_sum], [])
    run(None, (), [], [first_sum])
    run(None, (), [], [late_sum, early_sum])
    chains = [late_sum, early_sum, second_sum, first_sum, down_sum]
    while any(c.move is not None for c in chains):
        left = [c for c in chains if c.move is not None]
        for c in left:
            run(None, (), [c], [])
        for c in left:
            run(None, (), [], [c])
    halves = [c.result for c in (down_sum, first_sum, second_sum)]
    ordered = [in_order(*pair).astype(F32) * factor for pair in halves]
    grad_up = side([ordered[1][:, width:], ordered[2]], axis=1)
    *grad_qkv, tail_up, tail_table = unpack(index, early_sum.result[:2], late_sum.result[:2], factor)
    grad_qkv, tail = grad_qkv[:3], grad_qkv[3:]
    return (
        result,
        input_grad,
        *grad_qkv,
        ordered[1][:, :width],
        tail[0],
        tail[1],
        tail[2],
        tail_table,
        tail[3],
        tail[4],
        grad_up,
        tail_up,
        ordered[0],
        tail[5],
        tail[6],
        tail[7],
    )


def solution(mesh):
    rows = P(("dp", "fsdp"), None)
    matrix, vector = P("fsdp", None), P("fsdp")
    return jax.shard_map(
        on_device,
        mesh=mesh,
        in_specs=(
            rows, P(None, ("dp", "fsdp")), P(("dp", "fsdp")),
            matrix, matrix, matrix, matrix,
            vector, vector, vector, matrix, vector, vector,
            matrix, vector, matrix, vector, vector, vector,
            rows,
        ),
        out_specs=(
            rows, rows,
            matrix, matrix, matrix, matrix,
            vector, vector, vector, matrix, vector, vector,
            matrix, vector, matrix, vector, vector, vector,
        ),
        check_vma=False,
    )
```

```python
import functools
import math

import jax
import jax.numpy as jnp
import numpy as np
from jax import lax
from jax.experimental import pallas as pl
from jax.experimental.pallas import tpu as pltpu
from jax.sharding import PartitionSpec as P

HEADS = 12
HD = 64
WIN = 512
BUCKETS = 32
PAIRS = HEADS // 2
SCALE = HD ** (-0.5)
EPS = 1e-05
BF = jnp.bfloat16
F32 = jnp.float32
VMEM_LIMIT = 60 * 1024 * 1024
GROUPS = ((0, 2), (2, 2), (4, 2))
FORWARD_GROUPS = ((0, 3), (3, 3))


def params():
    return pltpu.CompilerParams(vmem_limit_bytes=VMEM_LIMIT)


def cost(flops, nbytes, transcendentals=0):
    return pl.CostEstimate(
        flops=int(flops / 100),
        bytes_accessed=int(nbytes / 100),
        transcendentals=int(transcendentals / 100),
    )


def struct(shape, dtype):
    return jax.ShapeDtypeStruct(shape, dtype)


def whole(array):
    return pl.BlockSpec(array.shape, lambda *at: (0,) * len(array.shape))


def dot(left, right):
    return lax.dot_general(left, right, (((1,), (0,)), ((), ())), preferred_element_type=F32)


def dot_t(left, right):
    return lax.dot_general(left, right, (((1,), (1,)), ((), ())), preferred_element_type=F32)


def tdot(left, right):
    return lax.dot_general(left, right, (((0,), (0,)), ((), ())), preferred_element_type=F32)


def split3(values):
    high = values.astype(BF)
    rest = values - high.astype(F32)
    middle = rest.astype(BF)
    return high, middle, (rest - middle.astype(F32)).astype(BF)


def swap(array, axis, bit):
    return lax.ppermute(array, axis, [(i, i ^ bit) for i in range(lax.axis_size(axis))])


def together(*groups):
    flat, tree = jax.tree.flatten(groups)
    return jax.tree.unflatten(tree, lax.optimization_barrier(tuple(flat)))


def half_of(array, which, axis=0):
    rows = array.shape[axis] // 2
    return lax.dynamic_slice_in_dim(array, which * rows, rows, axis)


class Chain:
    def __init__(self, steps):
        self.steps = steps
        self.result = None
        self.move = next(steps)

    def advance(self, arrived):
        try:
            self.move = self.steps.send(arrived)
        except StopIteration as stop:
            self.move, self.result = None, stop.value


def run(call, arrays, begin=(), finish=None):
    finish = begin if finish is None else finish
    arrays, sent = together(arrays, [chain.move[0] for chain in begin])
    for chain, array in zip(begin, sent):
        chain.flight = swap(array, chain.move[1], chain.move[2])
    out = call(*arrays) if call is not None else ()
    out, arrived = together(out, [chain.flight for chain in finish])
    for chain, array in zip(finish, arrived):
        chain.advance(array)
    return out


def gather_far(piece, bit):
    far = yield piece, "fsdp", 2
    beside = yield far, "dp", bit
    return far, beside


def send_once(array, axis, bit):
    arrived = yield array, axis, bit
    return arrived


def part_rows(index, rows, count):
    me, near, beside = index[0], index[1], index[2]
    places = [(me * rows, rows), ((me ^ 1) * rows, rows)]
    if count == QUARTERS:
        quarter = rows // 4
        firsts = [
            (2 * line + side) * quarter
            for line in (beside, 1 - beside)
            for side in (near, 1 - near)
        ]
        return places + [
            ((me ^ other) * rows + first, quarter) for other in (2, 3) for first in firsts
        ]
    if count == PARTS:
        third = rows // 3
        firsts = (near * third, (1 - near) * third, 2 * third)
        return places + [((me ^ other) * rows + first, third) for other in (2, 3) for first in firsts]
    half, pieces = rows // 2, (count - 2) // 4
    size = half // pieces
    for piece in range(pieces):
        for other in (2, 3):
            for side in (near, 1 - near):
                places.append(((me ^ other) * rows + side * half + piece * size, size))
    return places


PARTS, BIG_PARTS, QUARTERS = 8, 10, 11


def fetch_copies(index, parts, whole, sems, count=None):
    places = part_rows(index, whole.shape[0] // 4, count or len(parts))
    return [
        pltpu.make_async_copy(part, whole.at[pl.ds(pl.multiple_of(first, 16), size)], sems.at[at])
        for at, (part, (first, size)) in enumerate(zip(parts, places))
    ]


def start_copies(copies):
    for copy in copies:
        copy.start()


def wait_copies(copies):
    for copy in copies:
        copy.wait()


ANY = pl.BlockSpec(memory_space=pl.ANY)
SMEM = pl.BlockSpec(memory_space=pltpu.SMEM)


def reduce_steps(keep, send, line_first=False, own=None):
    place = lax.axis_index("dp")

    def add(*arrays):
        return functools.reduce(jnp.add, [array.astype(F32) for array in arrays]).astype(BF)

    got = yield send, "fsdp", 1
    bits = [1, 2]
    if line_first:
        bits = [2, 1]
        total = add(keep, got)
        which = (place // 2) & 1
        got = yield half_of(total, 1 - which, 1), "dp", 2
        total = add(half_of(total, which, 1), got)
        far = yield total[1], "fsdp", 2
        total = add(total[0], far)
    else:
        far = yield add(keep[1], got[1] if own is None else got), "fsdp", 2
        total = add(keep[0], got[0] if own is None else own.result, far)
    for bit in bits[1:] if line_first else bits:
        which = (place // bit) & 1
        got = yield half_of(total, 1 - which), "dp", bit
        total = add(half_of(total, which), got)
    bit = 4
    while bit < lax.axis_size("dp"):
        got = yield total, "dp", bit
        total = add(total, got)
        bit *= 2
    got = yield total, "dp", bits[1]
    total = in_order(total, got, (place // bits[1]) & 1)
    got = yield total, "dp", bits[0]
    return total, got, (place // bits[0]) & 1


def in_order(mine, other, which):
    return jnp.where(
        which == 0, jnp.concatenate([mine, other]), jnp.concatenate([other, mine])
    )


def table_places():
    step = np.arange(128)
    step = np.where(step < 64, -step, 128 - step)
    near = np.clip(step, -16, 15) + 16
    far = np.where(step <= -2, 0, np.where(step >= 2, 31, -1))
    wide = np.arange(256)
    wide = np.where(wide < 128, -wide, 256 - wide)
    places = np.concatenate([near + 32, near + 64, far, np.clip(wide, -16, 15) + 16])
    return places.astype(np.int32)[None, :]


def diagonal_places():
    lane = np.arange(128)
    x_place = np.where(lane < 63, np.clip(lane - 31, -16, 15) + 48, -1)
    y_place = np.where((lane >= 32) & (lane < 95), np.clip(lane - 63, -16, 15) + 80, -1)
    step = lane - 95
    block_place = np.where(
        (lane >= 64) & (step <= -2), 0, np.where((lane < 127) & (step >= 2), 31, -1)
    )
    step = (127 - np.arange(256) + 128) % 256 - 128
    places = np.concatenate([x_place, y_place, block_place, np.clip(step, -16, 15) + 16])
    return places.astype(np.int32)[:, None]


LANES = 640


def iota(shape, axis):
    return lax.broadcasted_iota(jnp.int32, shape, axis)


def as_bf(mask):
    return jnp.where(mask, 1.0, 0.0).astype(BF)


def near_mask():
    r, c = iota((128, 256), 0), iota((128, 256), 1)
    gap = (r >> 4) - (c >> 4)
    inside = (c < 128) & (gap <= 1) & (gap >= -1)
    return inside | ((r >= 112) & (c >= 128) & (c < 144)) | ((r < 16) & (c >= 240))


def hot_places(x, y, shape, axis):
    column = iota(shape, axis)
    block = (iota(shape, 1 - axis) & (WIN - 1)) >> 4
    third = column >> 5
    hot = jnp.where(third == 0, x, jnp.where(third == 1, y + 32, block + 64)) == column
    return column, hot & (column < 96)


PACK_ROWS, UP_ROW, TABLE_ROW = 16, 8, 10


def pack_vectors(vectors, up_bias, table):
    width, shard = up_bias.shape[0], vectors[0].shape[0]
    row = lax.broadcasted_iota(jnp.int32, (PACK_ROWS, shard), 0)
    pack = jnp.zeros((PACK_ROWS, shard), BF)
    for at, vector in enumerate(vectors):
        pack = jnp.where(row == at, vector[None, :], pack)
    pack = jnp.pad(pack, ((0, 0), (0, width - shard)))
    row = lax.broadcasted_iota(jnp.int32, (PACK_ROWS, width), 0)
    pack = jnp.where(row == UP_ROW, up_bias[None, :], pack)
    below = PACK_ROWS - TABLE_ROW - table.shape[0]
    return pack + jnp.pad(table, ((TABLE_ROW, below), (0, width - table.shape[1])))


def prep_kernel(
    index, p0, p1, p2, p3, cells_ref, mask_ref, places_ref,
    w_ref, own_ref, ke_ref, oh_ref, dt_ref, vectors_ref, up_bias_ref, packs,
):
    tokens = cells_ref.shape[1]
    me = index[0]
    for at, ref in enumerate((p0, p1, p2, p3)):
        packs[at] = ref[...]
    vectors = 0.0
    width = vectors_ref.shape[1]
    for at in range(4):
        rows = packs[me ^ at].astype(F32)
        vectors = vectors + pltpu.roll(rows[:8], at * (width // 4), 1)
        up_bias_ref[:, at * width : at * width + width] = rows[UP_ROW : UP_ROW + 1]
    vectors_ref[...] = vectors
    x, y, valid = cells_ref[0:1, :], cells_ref[1:2, :], mask_ref[...]
    column, hot = hot_places(x, y, (128, tokens), 0)
    own_ref[...] = as_bf(hot | (column == 96))
    sub = iota((8, tokens), 0)
    columns = jnp.where(sub == 0, x, jnp.where(sub == 1, y, valid)).astype(F32)
    columns = columns.T.astype(jnp.int32)
    x, y, valid = columns[:, 0:1], columns[:, 1:2], columns[:, 2:3]
    column, hot = hot_places(x, y, (tokens, 128), 1)
    masked = jnp.where((column == 99) & (valid <= 0), -1e30, 0.0)
    ones = hot | ((column >= 96) & (column < 99))
    ke_ref[...] = jnp.where(ones, 1.0, masked).astype(BF)
    block = (iota((tokens, 128), 0) & (WIN - 1)) >> 4
    third = column >> 5
    back = jnp.where(third == 0, 31 - x, jnp.where(third == 1, 63 - y, 95 - block)) == column
    oh_ref[...] = as_bf(back & (column < 96))

    pick = as_bf(iota((128, LANES), 0) == places_ref[...])
    lane = iota((32, 128), 1)
    mask = near_mask()
    for part in range(4):
        table = dot(packs[me ^ part][:, :128], pick)
        for head in range(HEADS // 4):
            row = table[TABLE_ROW + head : TABLE_ROW + head + 1]
            blocks = []
            for at in range(3):
                spread = jnp.broadcast_to(row[:, at * 128 : at * 128 + 128], (32, 128))
                spread = pltpu.roll(spread, at * 32, 1, stride=1, stride_axis=0)
                blocks.append(jnp.where(lane >> 5 == at, spread, 0.0))
            blocks.append(jnp.where((iota((32, 128), 0) == 3) & (lane == 96), 1.0, 0.0))
            place = part * (HEADS // 4) + head
            w_ref[place] = jnp.concatenate(blocks, axis=0).astype(BF)
            wide = jnp.broadcast_to(row[:, 384:640], (128, 256))
            rolled = pltpu.roll(wide, 0, 1, stride=1, stride_axis=0)
            dt_ref[place] = jnp.where(mask, rolled, 0.0).astype(BF)


def prepare(index, packs, layout_cells, pad_mask):
    tokens = pad_mask.shape[0]
    width = packs[0].shape[1]
    shapes = [
        struct((HEADS, 128, 128), BF),
        struct((128, tokens), BF),
        struct((tokens, 128), BF),
        struct((tokens, 128), BF),
        struct((HEADS, 128, 256), BF),
        struct((8, width), F32),
        struct((1, 4 * width), F32),
    ]
    arrays = [*packs, layout_cells, pad_mask.reshape(1, tokens), jnp.asarray(table_places())]
    return pl.pallas_call(
        prep_kernel,
        grid=(1,),
        in_specs=[SMEM] + [whole(array) for array in arrays],
        out_specs=[whole(shape) for shape in shapes],
        out_shape=shapes,
        scratch_shapes=[pltpu.VMEM((4, PACK_ROWS, width), BF)],
        compiler_params=params(),
        cost_estimate=cost(1e7, 3e6),
        name="prepare",
    )(index, *arrays)


def side_kernel(pieces, index, *refs):
    shards, outs = refs[: -1 - len(pieces)], refs[-1 - len(pieces) :]
    first = 0
    for ref in shards:
        columns = slice(first, first + ref.shape[1])
        first += ref.shape[1]
        outs[0][:, columns] = ref[...]
        for out, (start, step) in zip(outs[1:], pieces):
            row = pl.multiple_of(start + index[1] * step, 16)
            out[:, columns] = ref[pl.ds(row, out.shape[0]), :]


def side_by_side(index, shards, rows, pieces):
    columns = sum(shard.shape[1] for shard in shards)
    outs = [struct((shards[0].shape[0], columns), BF)] + [struct((rows, columns), BF)] * len(pieces)
    return pl.pallas_call(
        functools.partial(side_kernel, pieces),
        grid=(1,),
        in_specs=[SMEM] + [whole(shard) for shard in shards],
        out_specs=[whole(shape) for shape in outs],
        out_shape=outs,
        compiler_params=params(),
        cost_estimate=cost(0, 3e6),
        name="side_by_side",
    )(index, *shards)


def project_kernel(index, *refs):
    parts, (x_ref, bias_ref, out_ref, turned_ref, weight, sems) = refs[:PARTS], refs[PARTS:]

    @pl.when(pl.program_id(0) == 0)
    def _():
        copies = fetch_copies(index, parts, weight, sems)
        start_copies(copies)
        wait_copies(copies)

    width = x_ref.shape[1]
    turned_ref[...] = x_ref[...].T
    for at in range(3):
        values = dot(x_ref[...], weight[:, at * width : (at + 1) * width])
        if at == 0:
            values = (values + bias_ref[0:1, :]).astype(BF) * SCALE
        if at == 2:
            values = values + bias_ref[1:2, :]
        values = values.astype(BF)
        for pair in range(PAIRS):
            out_ref[at * PAIRS + pair] = values[:, pair * 128 : pair * 128 + 128]


def project(index, parts, tokens, biases, block=512):
    rows, width = tokens.shape
    return pl.pallas_call(
        project_kernel,
        grid=(rows // block,),
        in_specs=[SMEM]
        + [ANY] * PARTS
        + [
            pl.BlockSpec((block, width), lambda i: (i, 0)),
            pl.BlockSpec((8, width), lambda i: (0, 0)),
        ],
        out_specs=[
            pl.BlockSpec((3 * PAIRS, block, 128), lambda i: (0, i, 0)),
            pl.BlockSpec((width, block), lambda i: (0, i)),
        ],
        out_shape=[struct((3 * PAIRS, rows, 128), BF), struct((width, rows), BF)],
        scratch_shapes=[pltpu.VMEM((width, 3 * width), BF), pltpu.SemaphoreType.DMA((PARTS,))],
        compiler_params=params(),
        cost_estimate=cost(6 * rows * width * width, 10e6),
        name="project",
    )(index, *parts, tokens, biases)


def join(ref):
    return jnp.concatenate([ref[at] for at in range(ref.shape[0])], axis=1)


def input_kernel(index, *refs):
    count = len(GROUPS) * 3
    parts, grads = refs[:PARTS], refs[PARTS : PARTS + count]
    dresid_ref, out_ref, weight, sems = refs[PARTS + count :]

    @pl.when(pl.program_id(0) == 0)
    def _():
        copies = fetch_copies(index, parts, weight, sems)
        start_copies(copies)
        wait_copies(copies)

    joined = [join(grads[3 * group + at]) for at in range(3) for group in range(len(GROUPS))]
    total = dot_t(jnp.concatenate(joined, axis=1), weight[...])
    out_ref[...] = (dresid_ref[...] + total).astype(BF)


def input_gradient(index, parts, grads, dresid, block=256):
    rows, width = dresid.shape
    spec = pl.BlockSpec((block, width), lambda i: (i, 0))
    pairs = [pl.BlockSpec((a.shape[0], block, 128), lambda i: (0, i, 0)) for a in grads]
    return pl.pallas_call(
        input_kernel,
        grid=(rows // block,),
        in_specs=[SMEM] + [ANY] * PARTS + pairs + [spec],
        out_specs=spec,
        out_shape=struct((rows, width), BF),
        scratch_shapes=[pltpu.VMEM((width, 3 * width), BF), pltpu.SemaphoreType.DMA((PARTS,))],
        compiler_params=params(),
        cost_estimate=cost(6 * rows * width * width, 13e6),
        name="input_gradient",
    )(index, *parts, *grads, dresid)


def with_near(pieces, tile, at):
    pieces = list(pieces)
    pieces[at] = pieces[at] + tile[:, :128]
    if at > 0:
        left = pieces[at - 1]
        pieces[at - 1] = jnp.concatenate([left[:16] + tile[:16, 128:], left[16:]], axis=0)
    if at < 3:
        right = pieces[at + 1]
        pieces[at + 1] = jnp.concatenate([right[:112], right[112:] + tile[112:, 128:]], axis=0)
    return pieces


def lane_blocks(values):
    return [values[:, c * 128 : c * 128 + 128] for c in range(WIN // 128)]


def attend_kernel(
    q_ref, k_ref, v_ref, w_ref, own_ref, ke_ref, dt_ref, out_ref, lse_ref, s_scr, p_scr
):
    first = iota((128, WIN), 0) < HD
    windows = [slice(at, at + WIN) for at in range(0, q_ref.shape[0], WIN)]
    extras = dot(w_ref[...].reshape(256, 128), own_ref[...]).astype(BF)
    values = []
    for at, rows in enumerate(windows):
        keys = jnp.concatenate([k_ref[rows, :], ke_ref[rows, :]], axis=1)
        query_t = q_ref[rows, :].T
        values.append(v_ref[rows, :].T)
        for head in range(2):
            mine = first if head == 0 else ~first
            query = jnp.where(mine, query_t, jnp.zeros((), BF))
            extra = extras[head * 128 : head * 128 + 128, rows]
            s_scr[2 * at + head] = dot(keys, jnp.concatenate([query, extra], axis=0))
    for at, rows in enumerate(windows):
        mixed = []
        for head in range(2):
            place = 2 * at + head
            tile = dt_ref[head].astype(F32)
            scores = [
                with_near(lane_blocks(s_scr[place, row : row + 128, :]), tile, row // 128)
                for row in range(0, WIN, 128)
            ]
            tops, totals = [], []
            for column in range(WIN // 128):
                pieces = [row[column] for row in scores]
                top = jnp.maximum(
                    jnp.maximum(pieces[0], pieces[1]), jnp.maximum(pieces[2], pieces[3])
                )
                top = jnp.max(top, axis=0, keepdims=True)
                pieces = [jnp.exp(piece - top) for piece in pieces]
                total = (pieces[0] + pieces[1]) + (pieces[2] + pieces[3])
                totals.append(jnp.sum(total, axis=0, keepdims=True))
                tops.append(top)
                span = slice(column * 128, column * 128 + 128)
                for row, piece in enumerate(pieces):
                    p_scr[place, row * 128 : row * 128 + 128, span] = piece.astype(BF)
            total = jnp.concatenate(totals, axis=1)
            mixed.append(dot(values[at][head * HD : head * HD + HD], p_scr[place]) / total)
            lse_ref[head : head + 1, rows] = jnp.concatenate(tops, axis=1) + jnp.log(total)
        out_ref[rows, :] = jnp.concatenate(mixed, axis=0).astype(BF).T


def pair_block(tokens, shift):
    return pl.BlockSpec((None, tokens, 128), lambda p: (p + shift, 0, 0))


def attend(group, qkv, w, own, ke, near_t, old=()):
    start, pairs = group
    tokens = qkv.shape[1]
    scores = 2 * (tokens // WIN)
    kernel = attend_kernel
    if old:
        kernel = lambda *refs: attend_kernel(*refs[:7], *refs[9:])
    return pl.pallas_call(
        kernel,
        grid=(pairs,),
        in_specs=[
            pair_block(tokens, start),
            pair_block(tokens, start + PAIRS),
            pair_block(tokens, start + 2 * PAIRS),
            pl.BlockSpec((2, 128, 128), lambda p: (p + start, 0, 0)),
            whole(own),
            whole(ke),
            pl.BlockSpec((2, 128, 256), lambda p: (p + start, 0, 0)),
        ]
        + [ANY] * len(old),
        out_specs=[
            pair_block(tokens, start),
            pl.BlockSpec((None, 8, tokens), lambda p: (p + start, 0, 0)),
        ],
        out_shape=[struct((PAIRS, tokens, 128), BF), struct((PAIRS, 8, tokens), F32)],
        input_output_aliases={7: 0, 8: 1} if old else {},
        scratch_shapes=[pltpu.VMEM((scores, WIN, WIN), F32), pltpu.VMEM((scores, WIN, WIN), BF)],
        compiler_params=params(),
        cost_estimate=cost(tokens * WIN * pairs * 1536, 4e6 * pairs / 2, tokens * WIN * 2 * pairs),
        name="attend",
    )(qkv, qkv, qkv, w, own, ke, near_t, *old)


def diagonal_rows(sums):
    lane = iota((32, 128), 1)
    rows = []
    for at in range(3):
        block = jnp.where(lane >> 5 == at, sums[at * 32 : at * 32 + 32], 0.0)
        rolled = pltpu.roll(block, 0, 1, stride=1, stride_axis=0)
        rows.append(jnp.sum(rolled, axis=0, keepdims=True))
    return rows


def near_rows(tile):
    tile = jnp.where(near_mask(), tile, 0.0)
    turn = as_bf(iota((128, 128), 0) + iota((128, 128), 1) == 127)
    high, middle, low = split3(tile)
    turned = dot(turn, high) + dot(turn, middle) + dot(turn, low)
    rolled = pltpu.roll(turned, 0, 1, stride=1, stride_axis=0)
    return jnp.sum(rolled, axis=0, keepdims=True)


def attend_back_kernel(
    index, q_ref, k_ref, v_ref, w_ref, own_ref, ke_ref, oh_ref, dt_ref, do_ref, o_ref, lse_ref,
    x_ref, dq_ref, dk_ref, dv_ref, bias_ref, far_ref, near_ref, keep_ref, send_ref,
    s_scr, dp_scr, p_scr, ds_scr, products,
):
    zero = jnp.zeros((), BF)
    first = iota((WIN, 128), 1) < HD
    first_t = iota((128, WIN), 0) < HD
    place = iota((128, WIN), 0)
    windows = [slice(at, at + WIN) for at in range(0, q_ref.shape[0], WIN)]
    extra_columns = dot(w_ref[...].reshape(256, 128), own_ref[...]).astype(BF)
    keys_t = []
    for at, rows in enumerate(windows):
        keys = jnp.concatenate([k_ref[rows, :], ke_ref[rows, :]], axis=1)
        values = jnp.concatenate([v_ref[rows, :], ke_ref[rows, :]], axis=1)
        keys_t.append(k_ref[rows, :].T)
        query_t, grad_t = q_ref[rows, :].T, do_ref[rows, :].T
        product = grad_t.astype(F32) * o_ref[rows, :].T.astype(F32)
        for head in range(2):
            mine = first_t if head == 0 else ~first_t
            delta = -jnp.sum(product[head * HD : head * HD + HD], axis=0, keepdims=True)
            minus = jnp.zeros((128, WIN), BF)
            extra = extra_columns[head * 128 : head * 128 + 128, rows]
            parts = split3(-lse_ref[head : head + 1, rows])
            for part, (less, less_delta) in enumerate(zip(parts, split3(delta))):
                extra = jnp.where(place == 96 + part, less, extra)
                minus = jnp.where(place == 96 + part, less_delta, minus)
            query = jnp.where(mine, query_t, zero)
            grad = jnp.where(mine, grad_t, zero)
            s_scr[2 * at + head] = dot(keys, jnp.concatenate([query, extra], axis=0))
            dp_scr[2 * at + head] = dot(values, jnp.concatenate([grad, minus], axis=0))
    plus = lambda total, term: term if total is None else total + term
    far_left, diag, low, high = [], [None] * 2, [None] * 2, [None] * 2
    bias_sums = [None] * 2
    for at, rows in enumerate(windows):
        dq_t, extras, dk, dv = [], [], None, None
        for head in range(2):
            mine = first if head == 0 else ~first
            query = jnp.where(mine, q_ref[rows, :], zero)
            grad = jnp.where(mine, do_ref[rows, :], zero)
            tile = dt_ref[head].astype(F32)
            place = 2 * at + head
            for block in range(WIN // 128):
                span = slice(block * 128, block * 128 + 128)
                scores = with_near(lane_blocks(s_scr[place, span, :]), tile, block)
                probs = [jnp.exp(piece) for piece in scores]
                dprobs = lane_blocks(dp_scr[place, span, :])
                dscores = [a * b for a, b in zip(probs, dprobs)]
                p_scr[place, span, :] = jnp.concatenate([a.astype(BF) for a in probs], axis=1)
                ds_scr[place, span, :] = jnp.concatenate([a.astype(BF) for a in dscores], axis=1)
                diag[head] = plus(diag[head], dscores[block])
                if block > 0:
                    low[head] = plus(low[head], dscores[block - 1][:16])
                if block < 3:
                    high[head] = plus(high[head], dscores[block + 1][112:])
            dv = plus(dv, dot(p_scr[place], grad))
            dk = plus(dk, dot(ds_scr[place], query))
            left = jnp.concatenate(
                [keys_t[at][head * HD : head * HD + HD], own_ref[:96, rows]], axis=0
            )
            both = dot(left, ds_scr[place])
            dq_t.append(both[:HD] * SCALE)
            extras.append(both[HD:].astype(BF))
        far_left.append(jnp.concatenate(extras, axis=0))
        dq = jnp.concatenate(dq_t, axis=0).astype(BF).T
        dv = dv.astype(BF)
        dq_ref[rows, :] = dq
        dk_ref[rows, :] = dk.astype(BF)
        dv_ref[rows, :] = dv
        for which, array in enumerate((dq, dv)):
            total = jnp.sum(array.astype(F32), axis=0, keepdims=True)
            bias_sums[which] = plus(bias_sums[which], total)
    grads = jnp.concatenate([dq_ref[...], dk_ref[...], dv_ref[...]], axis=1)
    products[...] = dot(x_ref[...], grads)
    place_rows(index, products, keep_ref, send_ref)
    bias_ref[...] = jnp.zeros_like(bias_ref)
    for which in range(2):
        bias_ref[which : which + 1, :] = bias_sums[which]
    far = dot(jnp.concatenate(far_left, axis=1), oh_ref[...])
    for head in range(2):
        sums = diagonal_rows(far[head * 96 : head * 96 + 96])
        far_ref[head] = jnp.concatenate(sums + [jnp.zeros((5, 128), F32)], axis=0)
        corners = jnp.concatenate([low[head], jnp.zeros((96, 128), F32), high[head]], axis=0)
        tile = jnp.concatenate([diag[head], corners], axis=1)
        near_ref[head] = jnp.broadcast_to(near_rows(tile), (8, 256))


def attend_back(
    group, room, index, qkv, w, own, ke, oh, near_t, dmixed, mixed, lse, x, old=()
):
    start, pairs = group
    kernel = attend_back_kernel
    if old:
        kernel = lambda *refs: attend_back_kernel(*refs[:13], *refs[15:])
    width, tokens = x.shape
    scores = 2 * (tokens // WIN)
    out = struct((pairs, tokens, 128), BF)
    weight_rows = struct((2, width // 4, room), BF)
    weight_block = pl.BlockSpec(
        (2, width // 4, 384), lambda p: (0, 0, p + (start if old else 0))
    )
    return pl.pallas_call(
        kernel,
        grid=(pairs,),
        in_specs=[
            SMEM,
            pair_block(tokens, start),
            pair_block(tokens, start + PAIRS),
            pair_block(tokens, start + 2 * PAIRS),
            pl.BlockSpec((2, 128, 128), lambda p: (p + start, 0, 0)),
            whole(own),
            whole(ke),
            whole(oh),
            pl.BlockSpec((2, 128, 256), lambda p: (p + start, 0, 0)),
            pair_block(tokens, start),
            pair_block(tokens, start),
            pl.BlockSpec((None, 8, tokens), lambda p: (p + start, 0, 0)),
            whole(x),
        ]
        + [ANY] * len(old),
        out_specs=[
            pair_block(tokens, 0),
            pair_block(tokens, 0),
            pair_block(tokens, 0),
            pl.BlockSpec((None, 8, 128), lambda p: (p, 0, 0)),
            pl.BlockSpec((2, 8, 128), lambda p: (p, 0, 0)),
            pl.BlockSpec((2, 8, 256), lambda p: (p, 0, 0)),
            weight_block,
            weight_block,
        ],
        out_shape=[
            out,
            out,
            out,
            struct((pairs, 8, 128), F32),
            struct((2 * pairs, 8, 128), F32),
            struct((2 * pairs, 8, 256), F32),
            weight_rows,
            weight_rows,
        ],
        input_output_aliases={13: 6, 14: 7} if old else {},
        scratch_shapes=[
            pltpu.VMEM((scores, WIN, WIN), F32),
            pltpu.VMEM((scores, WIN, WIN), F32),
            pltpu.VMEM((scores, WIN, WIN), BF),
            pltpu.VMEM((scores, WIN, WIN), BF),
            pltpu.VMEM((width, 384), F32),
        ],
        compiler_params=params(),
        cost_estimate=cost(
            tokens * WIN * pairs * 2 * 2048, 12e6, tokens * WIN * pairs * 2
        ),
        name="attend_back",
    )(index, qkv, qkv, qkv, w, own, ke, oh, near_t, dmixed, mixed, lse, x, *old)


def norm_parts(values):
    centre = values - jnp.mean(values, axis=-1, keepdims=True)
    spread = jnp.mean(centre * centre, axis=-1, keepdims=True)
    scale = lax.rsqrt(spread + EPS)
    return centre * scale, scale


def norm_back(grad, hat, scale):
    mean = jnp.mean(grad, axis=-1, keepdims=True)
    along = jnp.mean(grad * hat, axis=-1, keepdims=True)
    return scale * (grad - mean - hat * along)


def add_rows(ref, rows):
    for at, values in enumerate(rows):
        ref[at : at + 1, :] += jnp.sum(values.astype(F32), axis=0, keepdims=True)


def gelu_and_slope(values):
    upto = 0.5 + 0.5 * lax.erf(values * math.sqrt(0.5))
    density = jnp.exp(values * values * -0.5) * (1.0 / math.sqrt(2.0 * math.pi))
    return values * upto, upto + values * density


def store_rows(index, total, places, stage, sems):
    copies = []
    for at, (which, place) in enumerate(places):
        shard = place.shape[0]
        rows = pl.ds(pl.multiple_of((index[0] ^ which) * shard, 16), shard)
        stage[at] = total[rows, :].astype(BF)
        copies.append(pltpu.make_async_copy(stage.at[at], place, sems.at[at]))
        copies[-1].start()
    return copies


def forward_kernel(index, *refs):
    up_parts, down_parts = refs[:BIG_PARTS], refs[BIG_PARTS : 2 * BIG_PARTS]
    (
        mixed_ref, x_ref, cot_ref, small_ref, up_bias_ref,
        out_ref, dfinal_ref, resid_ref, slope_ref, sums_ref, keep_ref, send_ref, send_far_ref,
        w_up, w_down, total, active_scr, stage, sems, out_sems,
    ) = refs[2 * BIG_PARTS :]
    step = pl.program_id(0)
    up_copies = fetch_copies(index, up_parts, w_up, sems.at[0])
    down_copies = fetch_copies(index, down_parts, w_down, sems.at[1], QUARTERS)

    @pl.when(step == 0)
    def _():
        start_copies(up_copies)
        start_copies(down_copies)
        for ref in (sums_ref, total):
            ref[...] = jnp.zeros_like(ref)
        wait_copies(up_copies)

    width, hidden = w_down.shape[1], w_down.shape[0]
    small = lambda at: small_ref[at + 2 : at + 3, :]
    resid = x_ref[...].astype(F32) + (dot(join(mixed_ref), w_up[:, :width]) + small(0))
    resid_ref[...] = resid
    hat, _ = norm_parts(resid)
    normed = hat * small(1) + small(2)
    low = normed.astype(BF)
    for at in range(0, hidden, width):
        span = slice(at, at + width)
        values = dot(low, w_up[:, at + width : at + 2 * width]) + up_bias_ref[:, span]
        active, slope = gelu_and_slope(values)
        active_scr[:, span] = active.astype(BF)
        slope_ref[:, span] = slope.astype(BF)

    @pl.when(step == 0)
    def _():
        wait_copies(down_copies)

    final = normed + dot(active_scr[...], w_down[...]) + small(3)
    hat, scale = norm_parts(final)
    out_ref[...] = (hat * small(4) + small(5)).astype(BF)
    cot = cot_ref[...].astype(F32)
    dfinal = norm_back(cot * small(4), hat, scale)
    dfinal_ref[...] = dfinal
    dbranch = dfinal.astype(BF)
    for at in range(0, hidden, width):
        total[at : at + width, :] += tdot(active_scr[:, at : at + width], dbranch)
    add_rows(sums_ref, (cot * hat, cot, dbranch))

    @pl.when(step == pl.num_programs(0) - 1)
    def _():
        places = ((1, send_ref), (3, send_far_ref), (2, keep_ref.at[1]), (0, keep_ref.at[0]))
        wait_copies(store_rows(index, total, places, stage, out_sems))


def forward(index, up_parts, down_parts, mixed, tokens, cotangent, smalls, up_bias, block=256):
    rows, width = tokens.shape
    hidden = up_bias.shape[1]
    spec = lambda columns: pl.BlockSpec((block, columns), lambda i: (i, 0))
    pairs = pl.BlockSpec((PAIRS, block, 128), lambda i: (0, i, 0))
    sums = struct((8, width), F32)
    down_rows = [struct((2, hidden // 4, width), BF)] + [struct((hidden // 4, width), BF)] * 2
    return pl.pallas_call(
        forward_kernel,
        grid=(rows // block,),
        in_specs=[SMEM]
        + [ANY] * (2 * BIG_PARTS)
        + [pairs, spec(width), spec(width), whole(smalls), whole(up_bias)],
        out_specs=[spec(width), spec(width), spec(width), spec(hidden), whole(sums)] + [ANY] * 3,
        out_shape=[
            struct((rows, width), BF),
            struct((rows, width), F32),
            struct((rows, width), F32),
            struct((rows, hidden), BF),
            sums,
        ]
        + down_rows,
        scratch_shapes=[
            pltpu.VMEM((width, width + hidden), BF),
            pltpu.VMEM((hidden, width), BF),
            pltpu.VMEM((hidden, width), F32),
            pltpu.VMEM((block, hidden), BF),
            pltpu.VMEM((4, hidden // 4, width), BF),
            pltpu.SemaphoreType.DMA((2, BIG_PARTS)),
            pltpu.SemaphoreType.DMA((4,)),
        ],
        compiler_params=params(),
        cost_estimate=cost(2 * rows * width * (width + 3 * hidden), 40e6),
        name="forward",
    )(index, *up_parts, *down_parts, mixed, tokens, cotangent, smalls, up_bias)


def backward_kernel(index, *refs):
    up_parts, down_parts = refs[:BIG_PARTS], refs[BIG_PARTS : 2 * BIG_PARTS]
    (
        dfinal_ref, resid_ref, slope_ref, mixed_ref, small_ref,
        dresid_ref, dmixed_ref, sums_ref, up_sums_ref, *row_refs,
        w_up, w_down, total, stage, sems, out_sems,
    ) = refs[2 * BIG_PARTS :]
    step = pl.program_id(0)

    @pl.when(step == 0)
    def _():
        copies = fetch_copies(index, down_parts, w_down, sems.at[0], QUARTERS)
        copies += fetch_copies(index, up_parts, w_up, sems.at[1])
        start_copies(copies)
        for ref in (sums_ref, up_sums_ref, total):
            ref[...] = jnp.zeros_like(ref)
        wait_copies(copies)

    width, hidden = w_down.shape[1], w_down.shape[0]
    small = lambda at: small_ref[at + 2 : at + 3, :]
    hat, scale = norm_parts(resid_ref[...])
    low_t = (hat * small(1) + small(2)).astype(BF).T
    dnormed = dfinal_ref[...]
    dbranch = dnormed.astype(BF)
    for at in range(0, hidden, width):
        span = slice(at, at + width)
        up_span = slice(at + width, at + 2 * width)
        dactive = dot_t(dbranch, w_down[span, :])
        dhidden = (dactive * slope_ref[:, span].astype(F32)).astype(BF)
        up_sums_ref[:, span] += jnp.sum(dhidden.astype(F32), axis=0, keepdims=True)
        total[:, up_span] += dot(low_t, dhidden)
        dnormed = dnormed + dot_t(dhidden, w_up[:, up_span])
    dresid = norm_back(dnormed * small(1), hat, scale)
    dresid_ref[...] = dresid
    dattn = dresid.astype(BF)
    dmixed = dot_t(dattn, w_up[:, :width]).astype(BF)
    for pair in range(PAIRS):
        dmixed_ref[pair] = dmixed[:, pair * 128 : pair * 128 + 128]
    total[:, :width] += tdot(join(mixed_ref), dattn)
    add_rows(sums_ref, (dnormed * hat, dnormed, dattn))

    @pl.when(step == pl.num_programs(0) - 1)
    def _():
        half = (width + hidden) // 2
        for at in range(2):
            columns = slice(at * half, at * half + half)
            keep, send = row_refs[2 * at : 2 * at + 2]
            places = ((1, send.at[0]), (3, send.at[1]), (2, keep.at[1]), (0, keep.at[0]))
            staged = stage.at[:, :, columns]
            wait_copies(store_rows(index, total.at[:, columns], places, staged, out_sems))


def backward(index, up_parts, down_parts, dfinal, resid, slope, mixed, smalls, block=256):
    rows, width = resid.shape
    hidden = slope.shape[1]
    spec = lambda columns: pl.BlockSpec((block, columns), lambda i: (i, 0))
    pairs = pl.BlockSpec((PAIRS, block, 128), lambda i: (0, i, 0))
    sums = [struct((8, width), F32), struct((1, hidden), F32)]
    up_rows = struct((2, width // 4, (width + hidden) // 2), BF)
    return pl.pallas_call(
        backward_kernel,
        grid=(rows // block,),
        in_specs=[SMEM]
        + [ANY] * (2 * BIG_PARTS)
        + [spec(width), spec(width), spec(hidden), pairs, whole(smalls)],
        out_specs=[spec(width), pairs] + [whole(shape) for shape in sums] + [ANY] * 4,
        out_shape=[struct((rows, width), F32), struct((PAIRS, rows, 128), BF)]
        + sums
        + [up_rows] * 4,
        scratch_shapes=[
            pltpu.VMEM((width, width + hidden), BF),
            pltpu.VMEM((hidden, width), BF),
            pltpu.VMEM((width, width + hidden), F32),
            pltpu.VMEM((4, width // 4, width + hidden), BF),
            pltpu.SemaphoreType.DMA((2, BIG_PARTS)),
            pltpu.SemaphoreType.DMA((4,)),
        ],
        compiler_params=params(),
        cost_estimate=cost(4 * rows * width * (width + 2 * hidden), 40e6),
        name="backward",
    )(index, *up_parts, *down_parts, dfinal, resid, slope, mixed, smalls)


def place_rows(index, total, keep_ref, send_ref):
    me, shard = index[0], keep_ref.shape[1]
    for at, ref in ((0, keep_ref), (2, keep_ref), (1, send_ref), (3, send_ref)):
        rows = pl.ds(pl.multiple_of((me ^ at) * shard, 16), shard)
        ref[at // 2] = total[rows, :].astype(BF)


def small_rows(refs, places, sums_one, sums_two, up_sums, rows, sums):
    width = rows.shape[1]
    shard = width // 4
    rows[...] = jnp.zeros_like(rows)
    sums[...] = jnp.zeros_like(sums)
    pair, head = 0, 0
    for bias, far, near in refs:
        for at in range(bias.shape[0]):
            rows[0:2, pair * 128 : pair * 128 + 128] = bias[at, 0:2, :]
            pair += 1
        for at in range(far.shape[0]):
            parts = [far[at, row : row + 1, :] for row in range(3)] + [near[at, 0:1, :]]
            sums[head : head + 1, :] = jnp.concatenate(parts, axis=1)
            head += 1
    for row, source in enumerate((2, 0, 1)):
        rows[row + 2 : row + 3, :] = sums_one[source : source + 1, :]
        rows[row + 5 : row + 6, :] = sums_two[source : source + 1, :]
    lane = iota((1, width), 1)
    for at in range(4):
        values = up_sums[:, at * width : at * width + width]
        inside = (lane >= at * shard) & (lane < (at + 1) * shard)
        for part in range(4):
            rolled = pltpu.roll(values, (at - part) % 4 * shard, 1)
            rows[8 + part : 9 + part, :] += jnp.where(inside, rolled, 0.0)
    pick = as_bf(places[...] == iota((LANES, 128), 1))
    table = sum(dot(part, pick) for part in split3(sums[...]))
    table = jnp.concatenate([table, jnp.zeros((table.shape[0], width - 128), F32)], axis=1)
    for at in range(HEADS):
        within = at % 3
        shift = at // 3 * shard + within % 2 * 96
        rolled = pltpu.roll(table[at : at + 1], shift, 1)
        rows[12 + within // 2 : 13 + within // 2, :] += rolled


def small_kernel(count, index, *refs):
    groups, refs = refs[: 3 * count], refs[3 * count :]
    (
        places, sums_one, sums_two, up_sums, keep_in, send_in, keep_ref, send_ref, total, rows, sums
    ) = refs
    del keep_in, send_in
    groups = [groups[at : at + 3] for at in range(0, 3 * count, 3)]
    small_rows(groups, places, sums_one, sums_two, up_sums, rows, sums)
    total[...] = rows[...].T
    place_rows(index, total, keep_ref, send_ref)


def small_gradients(index, groups, sums_one, sums_two, up_sums, keep, send):
    width = sums_one.shape[1]
    block = keep.shape[2] // 128 - 1
    arrays = [array for group in groups for array in group]
    arrays += [jnp.asarray(diagonal_places()), sums_one, sums_two, up_sums]
    out = pl.BlockSpec((2, width // 4, 128), lambda i: (0, 0, block))
    return pl.pallas_call(
        functools.partial(small_kernel, len(groups)),
        grid=(1,),
        in_specs=[SMEM] + [whole(array) for array in arrays] + [ANY, ANY],
        out_specs=[out, out],
        out_shape=[struct(keep.shape, BF)] * 2,
        input_output_aliases={len(arrays) + 1: 0, len(arrays) + 2: 1},
        scratch_shapes=[
            pltpu.VMEM((width, 128), F32),
            pltpu.VMEM((128, width), F32),
            pltpu.VMEM((16, LANES), F32),
        ],
        compiler_params=params(),
        cost_estimate=cost(1e7, 1e6),
        name="small_gradients",
    )(index, *arrays, keep, send)


def unpack_kernel(factor, index, *refs):
    halves, (query_ref, key_ref, value_ref) = refs[:4], refs[4:7]
    *vector_refs, up_bias_ref, table_ref, small_scr = refs[7:]
    half = halves[0].shape[0]
    for at in range(2):
        rows = pl.ds(pl.multiple_of((index[1] ^ at) * half, 16), half)
        first = 0
        for ref in (halves[at], halves[2 + at]):
            for column in range(0, ref.shape[1] // 384 * 384, 384):
                for which, out in enumerate((query_ref, key_ref, value_ref)):
                    place = column + which * 128
                    values = ref[:, place : place + 128].astype(F32) * factor
                    out[rows, first : first + 128] = values
                first += 128
        values = halves[2 + at][:, halves[2].shape[1] - 128 :]
        small_scr[rows, :] = values.astype(F32) * factor
    rows = small_scr[...].T
    for at, ref in enumerate(vector_refs):
        ref[...] = rows[at]
    up_bias_ref[...] = jnp.concatenate([rows[8 + at] for at in range(4)])
    table = jnp.concatenate([rows[12:13, :96], rows[12:13, 96:192], rows[13:14, :96]], axis=0)
    table_ref[...] = table


def unpack(index, early, late, factor):
    half, width = early[0].shape[0], PAIRS * 128
    arrays = [*early, *late]
    outs = [struct((2 * half, width), F32)] * 3 + [struct((2 * half,), F32)] * 8
    outs += [struct((8 * half,), F32), struct((HEADS // 4, 3 * BUCKETS), F32)]
    return pl.pallas_call(
        functools.partial(unpack_kernel, factor),
        grid=(1,),
        in_specs=[SMEM] + [whole(array) for array in arrays],
        out_specs=[whole(shape) for shape in outs],
        out_shape=outs,
        scratch_shapes=[pltpu.VMEM((2 * half, 128), F32)],
        compiler_params=params(),
        cost_estimate=cost(1e6, 3e6),
        name="unpack",
    )(index, *arrays)


def on_device(
    tokens,
    layout_cells,
    pad_mask,
    query_weight,
    key_weight,
    value_weight,
    out_weight,
    query_bias,
    value_bias,
    out_bias,
    bias_table,
    first_gain,
    first_shift,
    up_weight,
    up_bias,
    down_weight,
    down_bias,
    second_gain,
    second_shift,
    cotangent,
):
    rows, width = tokens.shape
    hidden = down_weight.shape[0] * 4
    shard = width // 4
    me = lax.axis_index("fsdp")
    parity = lax.axis_index("dp") & 1
    beside = (lax.axis_index("dp") >> 1) & 1
    index = jnp.stack([me, parity, beside]).astype(jnp.int32)
    factor = 1.0 / math.sqrt(rows * lax.axis_size("dp") * lax.axis_size("fsdp"))

    vectors = (
        query_bias, value_bias, out_bias, first_gain, first_shift, down_bias, second_gain,
        second_shift,
    )
    pack = pack_vectors(vectors, up_bias, bias_table)
    chain = lambda *args: Chain(send_once(*args))

    side = jnp.concatenate
    packs = [chain(pack, "fsdp", bit) for bit in (1, 2, 3)]
    third, piece = shard // 3, shard // 4
    qkv_shard, *qkv_thirds = side_by_side(
        index, (query_weight, key_weight, value_weight), third, ((0, third), (2 * third, 0))
    )

    def cores_of(chains):
        return [chain(part, "fsdp", 1) for far in chains for part in far.result]

    def parts_of(shard, core, chains, cores):
        parts = [shard, core.result]
        for at, far in enumerate(chains):
            parts += [*far.result, *(c.result for c in cores[2 * at : 2 * at + 2])]
        return parts

    out_weight, up_weight, qkv_thirds = together(out_weight, up_weight, qkv_thirds)
    qkv_far = Chain(gather_far(qkv_thirds[0], 1))
    qkv_direct = chain(qkv_thirds[1], "fsdp", 2)
    up_shard, *up_pieces = side_by_side(
        index, (out_weight, up_weight), piece, ((0, 2 * piece), (piece, 2 * piece))
    )
    up_far = [Chain(gather_far(half, 1)) for half in up_pieces]
    down_far = Chain(gather_far(half_of(half_of(down_weight, beside), parity), 1))
    qkv_core, up_core, down_core = (
        chain(shard, "fsdp", 1) for shard in (qkv_shard, up_shard, down_weight)
    )
    run(None, (), [qkv_far, *packs, qkv_direct, qkv_core], [qkv_far, *packs])
    w, own, ke, oh, near_t, smalls, full_up_bias = run(
        lambda *a: prepare(index, *a),
        ((pack, *(p.result for p in packs)), layout_cells, pad_mask),
        [qkv_far, down_far],
        [qkv_far, qkv_direct, qkv_core],
    )
    thirds = [*qkv_far.result, qkv_direct.result]
    qkv_cores = [chain(part, "fsdp", 1) for part in thirds]
    run(None, (), qkv_cores, [*qkv_cores, down_far])
    qkv_parts = [qkv_shard, qkv_core.result, *thirds, *(c.result for c in qkv_cores)]
    qkv, tokens_t = run(
        lambda *a: project(index, *a),
        (qkv_parts, tokens, smalls),
        [up_far[0], down_far, up_core, down_core],
    )
    quarters = list(down_far.result)
    line = [chain(quarter, "dp", 2) for quarter in quarters]
    cores = [chain(quarter, "fsdp", 1) for quarter in quarters]
    old = run(
        lambda *a: attend(FORWARD_GROUPS[0], *a),
        (qkv, w, own, ke, near_t),
        [up_far[1], up_far[0], line[0], *cores],
    )
    up_cores = cores_of(up_far[:1])
    cores.append(chain(line[0].result, "fsdp", 1))
    mixed, lse = run(
        lambda *a: attend(FORWARD_GROUPS[1], *a),
        (qkv, w, own, ke, near_t, old),
        [up_far[1], line[1], *up_cores, cores[2]],
    )
    up_cores += cores_of(up_far[1:])
    cores.append(chain(line[1].result, "fsdp", 1))
    run(None, (), [*up_cores[2:], cores[3]])
    up_parts = parts_of(up_shard, up_core, up_far, up_cores)
    quarters += [c.result for c in line]
    down_parts = [down_weight, down_core.result, *quarters, *(c.result for c in cores)]
    result, dfinal, resid, slope, sums_two, *down_rows = run(
        lambda *a: forward(index, up_parts, down_parts, *a),
        (mixed, tokens, cotangent, smalls, full_up_bias),
    )

    down_keep, down_own, down_far = down_rows
    own_core = chain(down_own, "fsdp", 1)
    down_sum = Chain(reduce_steps(down_keep, down_far, own=own_core))
    run(None, (), [down_sum])
    dresid, dmixed, sums_one, up_sums, *up_rows = run(
        lambda *a: backward(index, up_parts, down_parts, *a),
        (dfinal, resid, slope, mixed, smalls),
        [own_core, down_sum],
    )
    first_sum = Chain(reduce_steps(*up_rows[:2]))
    second_sum = Chain(reduce_steps(*up_rows[2:], line_first=True))
    run(None, (), [first_sum, second_sum])

    def back(at, room, begin, finish, old=()):
        return run(
            lambda *a: attend_back(GROUPS[at], room, index, *a),
            (qkv, w, own, ke, oh, near_t, dmixed, mixed, lse, tokens_t, old),
            begin,
            finish,
        )

    columns = 384 * (GROUPS[0][1] + GROUPS[1][1])
    three = [first_sum, second_sum, down_sum]
    backs = [back(0, columns, three, three)]
    backs.append(back(1, columns, three, three, tuple(backs[0][6:])))
    early_sum = Chain(reduce_steps(*backs[1][6:]))
    run(None, (), [early_sum])
    room = 3 * width + 128 - columns
    backs.append(back(2, room, [early_sum, *three], [early_sum, *three]))
    late_rows = run(
        lambda *a: small_gradients(index, *a),
        ([group[3:6] for group in backs], sums_one, sums_two, up_sums, *backs[2][6:]),
    )
    late_sum = Chain(reduce_steps(*late_rows))
    run(None, (), [late_sum])
    input_grad = run(
        lambda *a: input_gradient(index, qkv_parts, *a),
        ([array for group in backs for array in group[:3]], dresid),
        [late_sum, early_sum, second_sum, down_sum, first_sum],
        [late_sum, early_sum, second_sum, down_sum],
    )
    run(None, (), [late_sum, early_sum], [])
    run(None, (), [], [first_sum])
    run(None, (), [], [late_sum, early_sum])
    chains = [late_sum, early_sum, second_sum, first_sum, down_sum]
    rest = chains[2:]
    while any(c.move is not None for c in rest):
        left = [c for c in chains if c.move is not None]
        for c in left:
            run(None, (), [c], [])
            if c is second_sum and down_sum.move is not None:
                moved, _ = together([down_sum.move[0]], [second_sum.flight])
                down_sum.move = (moved[0], *down_sum.move[1:])
        for c in left:
            run(None, (), [], [c])
    ordered = [in_order(*c.result).astype(F32) * factor for c in (down_sum, first_sum, second_sum)]
    grad_down, grad_out = ordered[0], ordered[1][:, :width]
    grad_up = side([ordered[1][:, width:], ordered[2]], axis=1)
    ready = (grad_down,)
    while any(c.move is not None for c in chains[:2]):
        left = [c for c in chains[:2] if c.move is not None]
        for c in left:
            run(None, (), [c], [])
        for c in left:
            ready, (arrived,) = together(ready, [c.flight])
            c.advance(arrived)
    (grad_down,) = ready
    *grad_qkv, tail_up, tail_table = unpack(index, early_sum.result[:2], late_sum.result[:2], factor)
    grad_qkv, tail = grad_qkv[:3], grad_qkv[3:]
    return (
        result,
        input_grad,
        *grad_qkv,
        grad_out,
        tail[0],
        tail[1],
        tail[2],
        tail_table,
        tail[3],
        tail[4],
        grad_up,
        tail_up,
        grad_down,
        tail[5],
        tail[6],
        tail[7],
    )


def solution(mesh):
    rows = P(("dp", "fsdp"), None)
    matrix, vector = P("fsdp", None), P("fsdp")
    return jax.shard_map(
        on_device,
        mesh=mesh,
        in_specs=(
            rows, P(None, ("dp", "fsdp")), P(("dp", "fsdp")),
            matrix, matrix, matrix, matrix,
            vector, vector, vector, matrix, vector, vector,
            matrix, vector, matrix, vector, vector, vector,
            rows,
        ),
        out_specs=(
            rows, rows,
            matrix, matrix, matrix, matrix,
            vector, vector, vector, matrix, vector, vector,
            matrix, vector, matrix, vector, vector, vector,
        ),
        check_vma=False,
    )
```

```python
import functools
import math

import jax
import jax.numpy as jnp
import numpy as np
from jax import lax
from jax.experimental import pallas as pl
from jax.experimental.pallas import tpu as pltpu
from jax.sharding import PartitionSpec as P

HEADS = 12
HD = 64
WIN = 512
BUCKETS = 32
PAIRS = HEADS // 2
SCALE = HD ** (-0.5)
EPS = 1e-05
BF = jnp.bfloat16
F32 = jnp.float32
VMEM_LIMIT = 60 * 1024 * 1024
GROUPS = ((0, 2), (2, 2), (4, 2))
FORWARD_GROUPS = ((0, 3), (3, 3))


def params():
    return pltpu.CompilerParams(vmem_limit_bytes=VMEM_LIMIT)


def cost(flops, nbytes, transcendentals=0):
    return pl.CostEstimate(
        flops=int(flops / 100),
        bytes_accessed=int(nbytes / 100),
        transcendentals=int(transcendentals / 100),
    )


def struct(shape, dtype):
    return jax.ShapeDtypeStruct(shape, dtype)


def whole(array):
    return pl.BlockSpec(array.shape, lambda *at: (0,) * len(array.shape))


def dot(left, right):
    return lax.dot_general(left, right, (((1,), (0,)), ((), ())), preferred_element_type=F32)


def dot_t(left, right):
    return lax.dot_general(left, right, (((1,), (1,)), ((), ())), preferred_element_type=F32)


def tdot(left, right):
    return lax.dot_general(left, right, (((0,), (0,)), ((), ())), preferred_element_type=F32)


def split3(values):
    high = values.astype(BF)
    rest = values - high.astype(F32)
    middle = rest.astype(BF)
    return high, middle, (rest - middle.astype(F32)).astype(BF)


def swap(array, axis, bit):
    return lax.ppermute(array, axis, [(i, i ^ bit) for i in range(lax.axis_size(axis))])


def together(*groups):
    flat, tree = jax.tree.flatten(groups)
    return jax.tree.unflatten(tree, lax.optimization_barrier(tuple(flat)))


def half_of(array, which, axis=0):
    rows = array.shape[axis] // 2
    return lax.dynamic_slice_in_dim(array, which * rows, rows, axis)


class Chain:
    def __init__(self, steps):
        self.steps = steps
        self.result = None
        self.move = next(steps)

    def advance(self, arrived):
        try:
            self.move = self.steps.send(arrived)
        except StopIteration as stop:
            self.move, self.result = None, stop.value


def run(call, arrays, begin=(), finish=None):
    finish = begin if finish is None else finish
    arrays, sent = together(arrays, [chain.move[0] for chain in begin])
    for chain, array in zip(begin, sent):
        chain.flight = swap(array, chain.move[1], chain.move[2])
    out = call(*arrays) if call is not None else ()
    out, arrived = together(out, [chain.flight for chain in finish])
    for chain, array in zip(finish, arrived):
        chain.advance(array)
    return out


def gather_far(piece, bit):
    far = yield piece, "fsdp", 2
    beside = yield far, "dp", bit
    return far, beside


def send_once(array, axis, bit):
    arrived = yield array, axis, bit
    return arrived


def part_rows(index, rows, count):
    me, near, beside = index[0], index[1], index[2]
    places = [(me * rows, rows), ((me ^ 1) * rows, rows)]
    if count == QUARTERS:
        quarter = rows // 4
        firsts = [
            (2 * line + side) * quarter
            for line in (beside, 1 - beside)
            for side in (near, 1 - near)
        ]
        return places + [
            ((me ^ other) * rows + first, quarter) for other in (2, 3) for first in firsts
        ]
    if count == PARTS:
        third = rows // 3
        firsts = (near * third, (1 - near) * third, 2 * third)
        return places + [((me ^ other) * rows + first, third) for other in (2, 3) for first in firsts]
    half, pieces = rows // 2, (count - 2) // 4
    size = half // pieces
    for piece in range(pieces):
        for other in (2, 3):
            for side in (near, 1 - near):
                places.append(((me ^ other) * rows + side * half + piece * size, size))
    return places


PARTS, BIG_PARTS, QUARTERS = 8, 10, 11


def fetch_copies(index, parts, whole, sems, count=None):
    places = part_rows(index, whole.shape[0] // 4, count or len(parts))
    return [
        pltpu.make_async_copy(part, whole.at[pl.ds(pl.multiple_of(first, 16), size)], sems.at[at])
        for at, (part, (first, size)) in enumerate(zip(parts, places))
    ]


def start_copies(copies):
    for copy in copies:
        copy.start()


def wait_copies(copies):
    for copy in copies:
        copy.wait()


ANY = pl.BlockSpec(memory_space=pl.ANY)
SMEM = pl.BlockSpec(memory_space=pltpu.SMEM)


def reduce_steps(keep, send, line_first=False, own=None):
    place = lax.axis_index("dp")

    def add(*arrays):
        return functools.reduce(jnp.add, [array.astype(F32) for array in arrays]).astype(BF)

    got = yield send, "fsdp", 1
    bits = [1, 2]
    if line_first:
        bits = [2, 1]
        total = add(keep, got)
        which = (place // 2) & 1
        got = yield half_of(total, 1 - which, 1), "dp", 2
        total = add(half_of(total, which, 1), got)
        far = yield total[1], "fsdp", 2
        total = add(total[0], far)
    else:
        far = yield add(keep[1], got[1] if own is None else got), "fsdp", 2
        total = add(keep[0], got[0] if own is None else own.result, far)
    for bit in bits[1:] if line_first else bits:
        which = (place // bit) & 1
        got = yield half_of(total, 1 - which), "dp", bit
        total = add(half_of(total, which), got)
    bit = 4
    while bit < lax.axis_size("dp"):
        got = yield total, "dp", bit
        total = add(total, got)
        bit *= 2
    got = yield total, "dp", bits[1]
    total = in_order(total, got, (place // bits[1]) & 1)
    got = yield total, "dp", bits[0]
    return total, got, (place // bits[0]) & 1


def in_order(mine, other, which):
    return jnp.where(
        which == 0, jnp.concatenate([mine, other]), jnp.concatenate([other, mine])
    )


def table_places():
    step = np.arange(128)
    step = np.where(step < 64, -step, 128 - step)
    near = np.clip(step, -16, 15) + 16
    far = np.where(step <= -2, 0, np.where(step >= 2, 31, -1))
    wide = np.arange(256)
    wide = np.where(wide < 128, -wide, 256 - wide)
    places = np.concatenate([near + 32, near + 64, far, np.clip(wide, -16, 15) + 16])
    return places.astype(np.int32)[None, :]


def diagonal_places():
    lane = np.arange(128)
    x_place = np.where(lane < 63, np.clip(lane - 31, -16, 15) + 48, -1)
    y_place = np.where((lane >= 32) & (lane < 95), np.clip(lane - 63, -16, 15) + 80, -1)
    step = lane - 95
    block_place = np.where(
        (lane >= 64) & (step <= -2), 0, np.where((lane < 127) & (step >= 2), 31, -1)
    )
    step = (127 - np.arange(256) + 128) % 256 - 128
    places = np.concatenate([x_place, y_place, block_place, np.clip(step, -16, 15) + 16])
    return places.astype(np.int32)[:, None]


LANES = 640


def iota(shape, axis):
    return lax.broadcasted_iota(jnp.int32, shape, axis)


def as_bf(mask):
    return jnp.where(mask, 1.0, 0.0).astype(BF)


def near_mask():
    r, c = iota((128, 256), 0), iota((128, 256), 1)
    gap = (r >> 4) - (c >> 4)
    inside = (c < 128) & (gap <= 1) & (gap >= -1)
    return inside | ((r >= 112) & (c >= 128) & (c < 144)) | ((r < 16) & (c >= 240))


def hot_places(x, y, shape, axis):
    column = iota(shape, axis)
    block = (iota(shape, 1 - axis) & (WIN - 1)) >> 4
    third = column >> 5
    hot = jnp.where(third == 0, x, jnp.where(third == 1, y + 32, block + 64)) == column
    return column, hot & (column < 96)


PACK_ROWS, UP_ROW, TABLE_ROW = 16, 8, 10


def pack_vectors(vectors, up_bias, table):
    width, shard = up_bias.shape[0], vectors[0].shape[0]
    row = lax.broadcasted_iota(jnp.int32, (PACK_ROWS, shard), 0)
    pack = jnp.zeros((PACK_ROWS, shard), BF)
    for at, vector in enumerate(vectors):
        pack = jnp.where(row == at, vector[None, :], pack)
    pack = jnp.pad(pack, ((0, 0), (0, width - shard)))
    row = lax.broadcasted_iota(jnp.int32, (PACK_ROWS, width), 0)
    pack = jnp.where(row == UP_ROW, up_bias[None, :], pack)
    below = PACK_ROWS - TABLE_ROW - table.shape[0]
    return pack + jnp.pad(table, ((TABLE_ROW, below), (0, width - table.shape[1])))


def prep_kernel(
    index, p0, p1, p2, p3, cells_ref, mask_ref, places_ref,
    w_ref, own_ref, ke_ref, oh_ref, dt_ref, vectors_ref, up_bias_ref, packs,
):
    tokens = cells_ref.shape[1]
    me = index[0]
    for at, ref in enumerate((p0, p1, p2, p3)):
        packs[at] = ref[...]
    vectors = 0.0
    width = vectors_ref.shape[1]
    for at in range(4):
        rows = packs[me ^ at].astype(F32)
        vectors = vectors + pltpu.roll(rows[:8], at * (width // 4), 1)
        up_bias_ref[:, at * width : at * width + width] = rows[UP_ROW : UP_ROW + 1]
    vectors_ref[...] = vectors
    x, y, valid = cells_ref[0:1, :], cells_ref[1:2, :], mask_ref[...]
    column, hot = hot_places(x, y, (128, tokens), 0)
    own_ref[...] = as_bf(hot | (column == 96))
    sub = iota((8, tokens), 0)
    columns = jnp.where(sub == 0, x, jnp.where(sub == 1, y, valid)).astype(F32)
    columns = columns.T.astype(jnp.int32)
    x, y, valid = columns[:, 0:1], columns[:, 1:2], columns[:, 2:3]
    column, hot = hot_places(x, y, (tokens, 128), 1)
    masked = jnp.where((column == 99) & (valid <= 0), -1e30, 0.0)
    ones = hot | ((column >= 96) & (column < 99))
    ke_ref[...] = jnp.where(ones, 1.0, masked).astype(BF)
    block = (iota((tokens, 128), 0) & (WIN - 1)) >> 4
    third = column >> 5
    back = jnp.where(third == 0, 31 - x, jnp.where(third == 1, 63 - y, 95 - block)) == column
    oh_ref[...] = as_bf(back & (column < 96))

    pick = as_bf(iota((128, LANES), 0) == places_ref[...])
    lane = iota((32, 128), 1)
    mask = near_mask()
    for part in range(4):
        table = dot(packs[me ^ part][:, :128], pick)
        for head in range(HEADS // 4):
            row = table[TABLE_ROW + head : TABLE_ROW + head + 1]
            blocks = []
            for at in range(3):
                spread = jnp.broadcast_to(row[:, at * 128 : at * 128 + 128], (32, 128))
                spread = pltpu.roll(spread, at * 32, 1, stride=1, stride_axis=0)
                blocks.append(jnp.where(lane >> 5 == at, spread, 0.0))
            blocks.append(jnp.where((iota((32, 128), 0) == 3) & (lane == 96), 1.0, 0.0))
            place = part * (HEADS // 4) + head
            w_ref[place] = jnp.concatenate(blocks, axis=0).astype(BF)
            wide = jnp.broadcast_to(row[:, 384:640], (128, 256))
            rolled = pltpu.roll(wide, 0, 1, stride=1, stride_axis=0)
            dt_ref[place] = jnp.where(mask, rolled, 0.0).astype(BF)


def prepare(index, packs, layout_cells, pad_mask):
    tokens = pad_mask.shape[0]
    width = packs[0].shape[1]
    shapes = [
        struct((HEADS, 128, 128), BF),
        struct((128, tokens), BF),
        struct((tokens, 128), BF),
        struct((tokens, 128), BF),
        struct((HEADS, 128, 256), BF),
        struct((8, width), F32),
        struct((1, 4 * width), F32),
    ]
    arrays = [*packs, layout_cells, pad_mask.reshape(1, tokens), jnp.asarray(table_places())]
    return pl.pallas_call(
        prep_kernel,
        grid=(1,),
        in_specs=[SMEM] + [whole(array) for array in arrays],
        out_specs=[whole(shape) for shape in shapes],
        out_shape=shapes,
        scratch_shapes=[pltpu.VMEM((4, PACK_ROWS, width), BF)],
        compiler_params=params(),
        cost_estimate=cost(1e7, 3e6),
        name="prepare",
    )(index, *arrays)


def side_kernel(pieces, index, *refs):
    shards, outs = refs[: -1 - len(pieces)], refs[-1 - len(pieces) :]
    first = 0
    for ref in shards:
        columns = slice(first, first + ref.shape[1])
        first += ref.shape[1]
        outs[0][:, columns] = ref[...]
        for out, (start, step) in zip(outs[1:], pieces):
            row = pl.multiple_of(start + index[1] * step, 16)
            out[:, columns] = ref[pl.ds(row, out.shape[0]), :]


def side_by_side(index, shards, rows, pieces):
    columns = sum(shard.shape[1] for shard in shards)
    outs = [struct((shards[0].shape[0], columns), BF)] + [struct((rows, columns), BF)] * len(pieces)
    return pl.pallas_call(
        functools.partial(side_kernel, pieces),
        grid=(1,),
        in_specs=[SMEM] + [whole(shard) for shard in shards],
        out_specs=[whole(shape) for shape in outs],
        out_shape=outs,
        compiler_params=params(),
        cost_estimate=cost(0, 3e6),
        name="side_by_side",
    )(index, *shards)


def project_kernel(index, *refs):
    parts, (x_ref, bias_ref, out_ref, turned_ref, weight, sems) = refs[:PARTS], refs[PARTS:]

    @pl.when(pl.program_id(0) == 0)
    def _():
        copies = fetch_copies(index, parts, weight, sems)
        start_copies(copies)
        wait_copies(copies)

    width = x_ref.shape[1]
    turned_ref[...] = x_ref[...].T
    for at in range(3):
        values = dot(x_ref[...], weight[:, at * width : (at + 1) * width])
        if at == 0:
            values = (values + bias_ref[0:1, :]).astype(BF) * SCALE
        if at == 2:
            values = values + bias_ref[1:2, :]
        values = values.astype(BF)
        for pair in range(PAIRS):
            out_ref[at * PAIRS + pair] = values[:, pair * 128 : pair * 128 + 128]


def project(index, parts, tokens, biases, block=512):
    rows, width = tokens.shape
    return pl.pallas_call(
        project_kernel,
        grid=(rows // block,),
        in_specs=[SMEM]
        + [ANY] * PARTS
        + [
            pl.BlockSpec((block, width), lambda i: (i, 0)),
            pl.BlockSpec((8, width), lambda i: (0, 0)),
        ],
        out_specs=[
            pl.BlockSpec((3 * PAIRS, block, 128), lambda i: (0, i, 0)),
            pl.BlockSpec((width, block), lambda i: (0, i)),
        ],
        out_shape=[struct((3 * PAIRS, rows, 128), BF), struct((width, rows), BF)],
        scratch_shapes=[pltpu.VMEM((width, 3 * width), BF), pltpu.SemaphoreType.DMA((PARTS,))],
        compiler_params=params(),
        cost_estimate=cost(6 * rows * width * width, 10e6),
        name="project",
    )(index, *parts, tokens, biases)


def join(ref):
    return jnp.concatenate([ref[at] for at in range(ref.shape[0])], axis=1)


def input_kernel(index, *refs):
    count = len(GROUPS) * 3
    parts, grads = refs[:PARTS], refs[PARTS : PARTS + count]
    dresid_ref, out_ref, weight, sems = refs[PARTS + count :]

    @pl.when(pl.program_id(0) == 0)
    def _():
        copies = fetch_copies(index, parts, weight, sems)
        start_copies(copies)
        wait_copies(copies)

    joined = [join(grads[3 * group + at]) for at in range(3) for group in range(len(GROUPS))]
    total = dot_t(jnp.concatenate(joined, axis=1), weight[...])
    out_ref[...] = (dresid_ref[...] + total).astype(BF)


def input_gradient(index, parts, grads, dresid, block=256):
    rows, width = dresid.shape
    spec = pl.BlockSpec((block, width), lambda i: (i, 0))
    pairs = [pl.BlockSpec((a.shape[0], block, 128), lambda i: (0, i, 0)) for a in grads]
    return pl.pallas_call(
        input_kernel,
        grid=(rows // block,),
        in_specs=[SMEM] + [ANY] * PARTS + pairs + [spec],
        out_specs=spec,
        out_shape=struct((rows, width), BF),
        scratch_shapes=[pltpu.VMEM((width, 3 * width), BF), pltpu.SemaphoreType.DMA((PARTS,))],
        compiler_params=params(),
        cost_estimate=cost(6 * rows * width * width, 13e6),
        name="input_gradient",
    )(index, *parts, *grads, dresid)


def with_near(pieces, tile, at):
    pieces = list(pieces)
    pieces[at] = pieces[at] + tile[:, :128]
    if at > 0:
        left = pieces[at - 1]
        pieces[at - 1] = jnp.concatenate([left[:16] + tile[:16, 128:], left[16:]], axis=0)
    if at < 3:
        right = pieces[at + 1]
        pieces[at + 1] = jnp.concatenate([right[:112], right[112:] + tile[112:, 128:]], axis=0)
    return pieces


def lane_blocks(values):
    return [values[:, c * 128 : c * 128 + 128] for c in range(WIN // 128)]


def attend_kernel(
    q_ref, k_ref, v_ref, w_ref, own_ref, ke_ref, dt_ref, out_ref, lse_ref, s_scr, p_scr
):
    first = iota((128, WIN), 0) < HD
    windows = [slice(at, at + WIN) for at in range(0, q_ref.shape[0], WIN)]
    extras = dot(w_ref[...].reshape(256, 128), own_ref[...]).astype(BF)
    values = []
    for at, rows in enumerate(windows):
        keys = jnp.concatenate([k_ref[rows, :], ke_ref[rows, :]], axis=1)
        query_t = q_ref[rows, :].T
        values.append(v_ref[rows, :].T)
        for head in range(2):
            mine = first if head == 0 else ~first
            query = jnp.where(mine, query_t, jnp.zeros((), BF))
            extra = extras[head * 128 : head * 128 + 128, rows]
            s_scr[2 * at + head] = dot(keys, jnp.concatenate([query, extra], axis=0))
    for at, rows in enumerate(windows):
        mixed = []
        for head in range(2):
            place = 2 * at + head
            tile = dt_ref[head].astype(F32)
            scores = [
                with_near(lane_blocks(s_scr[place, row : row + 128, :]), tile, row // 128)
                for row in range(0, WIN, 128)
            ]
            tops, totals = [], []
            for column in range(WIN // 128):
                pieces = [row[column] for row in scores]
                top = jnp.maximum(
                    jnp.maximum(pieces[0], pieces[1]), jnp.maximum(pieces[2], pieces[3])
                )
                top = jnp.max(top, axis=0, keepdims=True)
                pieces = [jnp.exp(piece - top) for piece in pieces]
                total = (pieces[0] + pieces[1]) + (pieces[2] + pieces[3])
                totals.append(jnp.sum(total, axis=0, keepdims=True))
                tops.append(top)
                span = slice(column * 128, column * 128 + 128)
                for row, piece in enumerate(pieces):
                    p_scr[place, row * 128 : row * 128 + 128, span] = piece.astype(BF)
            total = jnp.concatenate(totals, axis=1)
            mixed.append(dot(values[at][head * HD : head * HD + HD], p_scr[place]) / total)
            lse_ref[head : head + 1, rows] = jnp.concatenate(tops, axis=1) + jnp.log(total)
        out_ref[rows, :] = jnp.concatenate(mixed, axis=0).astype(BF).T


def pair_block(tokens, shift):
    return pl.BlockSpec((None, tokens, 128), lambda p: (p + shift, 0, 0))


def attend(group, qkv, w, own, ke, near_t, old=()):
    start, pairs = group
    tokens = qkv.shape[1]
    scores = 2 * (tokens // WIN)
    kernel = attend_kernel
    if old:
        kernel = lambda *refs: attend_kernel(*refs[:7], *refs[9:])
    return pl.pallas_call(
        kernel,
        grid=(pairs,),
        in_specs=[
            pair_block(tokens, start),
            pair_block(tokens, start + PAIRS),
            pair_block(tokens, start + 2 * PAIRS),
            pl.BlockSpec((2, 128, 128), lambda p: (p + start, 0, 0)),
            whole(own),
            whole(ke),
            pl.BlockSpec((2, 128, 256), lambda p: (p + start, 0, 0)),
        ]
        + [ANY] * len(old),
        out_specs=[
            pair_block(tokens, start),
            pl.BlockSpec((None, 8, tokens), lambda p: (p + start, 0, 0)),
        ],
        out_shape=[struct((PAIRS, tokens, 128), BF), struct((PAIRS, 8, tokens), F32)],
        input_output_aliases={7: 0, 8: 1} if old else {},
        scratch_shapes=[pltpu.VMEM((scores, WIN, WIN), F32), pltpu.VMEM((scores, WIN, WIN), BF)],
        compiler_params=params(),
        cost_estimate=cost(tokens * WIN * pairs * 1536, 4e6 * pairs / 2, tokens * WIN * 2 * pairs),
        name="attend",
    )(qkv, qkv, qkv, w, own, ke, near_t, *old)


def diagonal_rows(sums):
    lane = iota((32, 128), 1)
    rows = []
    for at in range(3):
        block = jnp.where(lane >> 5 == at, sums[at * 32 : at * 32 + 32], 0.0)
        rolled = pltpu.roll(block, 0, 1, stride=1, stride_axis=0)
        rows.append(jnp.sum(rolled, axis=0, keepdims=True))
    return rows


def near_rows(tile):
    tile = jnp.where(near_mask(), tile, 0.0)
    turn = as_bf(iota((128, 128), 0) + iota((128, 128), 1) == 127)
    high, middle, low = split3(tile)
    turned = dot(turn, high) + dot(turn, middle) + dot(turn, low)
    rolled = pltpu.roll(turned, 0, 1, stride=1, stride_axis=0)
    return jnp.sum(rolled, axis=0, keepdims=True)


def attend_back_kernel(
    index, q_ref, k_ref, v_ref, w_ref, own_ref, ke_ref, oh_ref, dt_ref, do_ref, o_ref, lse_ref,
    x_ref, dq_ref, dk_ref, dv_ref, bias_ref, far_ref, near_ref, keep_ref, send_ref,
    s_scr, dp_scr, p_scr, ds_scr, products,
):
    zero = jnp.zeros((), BF)
    first = iota((WIN, 128), 1) < HD
    first_t = iota((128, WIN), 0) < HD
    place = iota((128, WIN), 0)
    windows = [slice(at, at + WIN) for at in range(0, q_ref.shape[0], WIN)]
    extra_columns = dot(w_ref[...].reshape(256, 128), own_ref[...]).astype(BF)
    keys_t = []
    for at, rows in enumerate(windows):
        keys = jnp.concatenate([k_ref[rows, :], ke_ref[rows, :]], axis=1)
        values = jnp.concatenate([v_ref[rows, :], ke_ref[rows, :]], axis=1)
        keys_t.append(k_ref[rows, :].T)
        query_t, grad_t = q_ref[rows, :].T, do_ref[rows, :].T
        product = grad_t.astype(F32) * o_ref[rows, :].T.astype(F32)
        for head in range(2):
            mine = first_t if head == 0 else ~first_t
            delta = -jnp.sum(product[head * HD : head * HD + HD], axis=0, keepdims=True)
            minus = jnp.zeros((128, WIN), BF)
            extra = extra_columns[head * 128 : head * 128 + 128, rows]
            parts = split3(-lse_ref[head : head + 1, rows])
            for part, (less, less_delta) in enumerate(zip(parts, split3(delta))):
                extra = jnp.where(place == 96 + part, less, extra)
                minus = jnp.where(place == 96 + part, less_delta, minus)
            query = jnp.where(mine, query_t, zero)
            grad = jnp.where(mine, grad_t, zero)
            s_scr[2 * at + head] = dot(keys, jnp.concatenate([query, extra], axis=0))
            dp_scr[2 * at + head] = dot(values, jnp.concatenate([grad, minus], axis=0))
    plus = lambda total, term: term if total is None else total + term
    far_left, diag, low, high = [], [None] * 2, [None] * 2, [None] * 2
    bias_sums = [None] * 2
    for at, rows in enumerate(windows):
        dq_t, extras, dk, dv = [], [], None, None
        for head in range(2):
            mine = first if head == 0 else ~first
            query = jnp.where(mine, q_ref[rows, :], zero)
            grad = jnp.where(mine, do_ref[rows, :], zero)
            tile = dt_ref[head].astype(F32)
            place = 2 * at + head
            for block in range(WIN // 128):
                span = slice(block * 128, block * 128 + 128)
                scores = with_near(lane_blocks(s_scr[place, span, :]), tile, block)
                probs = [jnp.exp(piece) for piece in scores]
                dprobs = lane_blocks(dp_scr[place, span, :])
                dscores = [a * b for a, b in zip(probs, dprobs)]
                p_scr[place, span, :] = jnp.concatenate([a.astype(BF) for a in probs], axis=1)
                ds_scr[place, span, :] = jnp.concatenate([a.astype(BF) for a in dscores], axis=1)
                diag[head] = plus(diag[head], dscores[block])
                if block > 0:
                    low[head] = plus(low[head], dscores[block - 1][:16])
                if block < 3:
                    high[head] = plus(high[head], dscores[block + 1][112:])
            dv = plus(dv, dot(p_scr[place], grad))
            dk = plus(dk, dot(ds_scr[place], query))
            left = jnp.concatenate(
                [keys_t[at][head * HD : head * HD + HD], own_ref[:96, rows]], axis=0
            )
            both = dot(left, ds_scr[place])
            dq_t.append(both[:HD] * SCALE)
            extras.append(both[HD:].astype(BF))
        far_left.append(jnp.concatenate(extras, axis=0))
        dq = jnp.concatenate(dq_t, axis=0).astype(BF).T
        dv = dv.astype(BF)
        dq_ref[rows, :] = dq
        dk_ref[rows, :] = dk.astype(BF)
        dv_ref[rows, :] = dv
        for which, array in enumerate((dq, dv)):
            total = jnp.sum(array.astype(F32), axis=0, keepdims=True)
            bias_sums[which] = plus(bias_sums[which], total)
    grads = jnp.concatenate([dq_ref[...], dk_ref[...], dv_ref[...]], axis=1)
    products[...] = dot(x_ref[...], grads)
    place_rows(index, products, keep_ref, send_ref)
    bias_ref[...] = jnp.zeros_like(bias_ref)
    for which in range(2):
        bias_ref[which : which + 1, :] = bias_sums[which]
    far = dot(jnp.concatenate(far_left, axis=1), oh_ref[...])
    for head in range(2):
        sums = diagonal_rows(far[head * 96 : head * 96 + 96])
        far_ref[head] = jnp.concatenate(sums + [jnp.zeros((5, 128), F32)], axis=0)
        corners = jnp.concatenate([low[head], jnp.zeros((96, 128), F32), high[head]], axis=0)
        tile = jnp.concatenate([diag[head], corners], axis=1)
        near_ref[head] = jnp.broadcast_to(near_rows(tile), (8, 256))


def attend_back(
    group, room, index, qkv, w, own, ke, oh, near_t, dmixed, mixed, lse, x, old=()
):
    start, pairs = group
    kernel = attend_back_kernel
    if old:
        kernel = lambda *refs: attend_back_kernel(*refs[:13], *refs[15:])
    width, tokens = x.shape
    scores = 2 * (tokens // WIN)
    out = struct((pairs, tokens, 128), BF)
    weight_rows = struct((2, width // 4, room), BF)
    weight_block = pl.BlockSpec(
        (2, width // 4, 384), lambda p: (0, 0, p + (start if old else 0))
    )
    return pl.pallas_call(
        kernel,
        grid=(pairs,),
        in_specs=[
            SMEM,
            pair_block(tokens, start),
            pair_block(tokens, start + PAIRS),
            pair_block(tokens, start + 2 * PAIRS),
            pl.BlockSpec((2, 128, 128), lambda p: (p + start, 0, 0)),
            whole(own),
            whole(ke),
            whole(oh),
            pl.BlockSpec((2, 128, 256), lambda p: (p + start, 0, 0)),
            pair_block(tokens, start),
            pair_block(tokens, start),
            pl.BlockSpec((None, 8, tokens), lambda p: (p + start, 0, 0)),
            whole(x),
        ]
        + [ANY] * len(old),
        out_specs=[
            pair_block(tokens, 0),
            pair_block(tokens, 0),
            pair_block(tokens, 0),
            pl.BlockSpec((None, 8, 128), lambda p: (p, 0, 0)),
            pl.BlockSpec((2, 8, 128), lambda p: (p, 0, 0)),
            pl.BlockSpec((2, 8, 256), lambda p: (p, 0, 0)),
            weight_block,
            weight_block,
        ],
        out_shape=[
            out,
            out,
            out,
            struct((pairs, 8, 128), F32),
            struct((2 * pairs, 8, 128), F32),
            struct((2 * pairs, 8, 256), F32),
            weight_rows,
            weight_rows,
        ],
        input_output_aliases={13: 6, 14: 7} if old else {},
        scratch_shapes=[
            pltpu.VMEM((scores, WIN, WIN), F32),
            pltpu.VMEM((scores, WIN, WIN), F32),
            pltpu.VMEM((scores, WIN, WIN), BF),
            pltpu.VMEM((scores, WIN, WIN), BF),
            pltpu.VMEM((width, 384), F32),
        ],
        compiler_params=params(),
        cost_estimate=cost(
            tokens * WIN * pairs * 2 * 2048, 12e6, tokens * WIN * pairs * 2
        ),
        name="attend_back",
    )(index, qkv, qkv, qkv, w, own, ke, oh, near_t, dmixed, mixed, lse, x, *old)


def norm_parts(values):
    centre = values - jnp.mean(values, axis=-1, keepdims=True)
    spread = jnp.mean(centre * centre, axis=-1, keepdims=True)
    scale = lax.rsqrt(spread + EPS)
    return centre * scale, scale


def norm_back(grad, hat, scale):
    mean = jnp.mean(grad, axis=-1, keepdims=True)
    along = jnp.mean(grad * hat, axis=-1, keepdims=True)
    return scale * (grad - mean - hat * along)


def add_rows(ref, rows):
    for at, values in enumerate(rows):
        ref[at : at + 1, :] += jnp.sum(values.astype(F32), axis=0, keepdims=True)


def gelu_and_slope(values):
    upto = 0.5 + 0.5 * lax.erf(values * math.sqrt(0.5))
    density = jnp.exp(values * values * -0.5) * (1.0 / math.sqrt(2.0 * math.pi))
    return values * upto, upto + values * density


def store_rows(index, total, places, stage, sems):
    copies = []
    for at, (which, place) in enumerate(places):
        shard = place.shape[0]
        rows = pl.ds(pl.multiple_of((index[0] ^ which) * shard, 16), shard)
        stage[at] = total[rows, :].astype(BF)
        copies.append(pltpu.make_async_copy(stage.at[at], place, sems.at[at]))
        copies[-1].start()
    return copies


def forward_kernel(index, *refs):
    up_parts, down_parts = refs[:BIG_PARTS], refs[BIG_PARTS : 2 * BIG_PARTS]
    (
        mixed_ref, x_ref, cot_ref, small_ref, up_bias_ref,
        out_ref, dfinal_ref, resid_ref, slope_ref, sums_ref, keep_ref, send_ref, send_far_ref,
        w_up, w_down, total, active_scr, stage, sems, out_sems,
    ) = refs[2 * BIG_PARTS :]
    step = pl.program_id(0)
    up_copies = fetch_copies(index, up_parts, w_up, sems.at[0])
    down_copies = fetch_copies(index, down_parts, w_down, sems.at[1], QUARTERS)

    @pl.when(step == 0)
    def _():
        start_copies(up_copies)
        start_copies(down_copies)
        for ref in (sums_ref, total):
            ref[...] = jnp.zeros_like(ref)
        wait_copies(up_copies)

    width, hidden = w_down.shape[1], w_down.shape[0]
    small = lambda at: small_ref[at + 2 : at + 3, :]
    resid = x_ref[...].astype(F32) + (dot(join(mixed_ref), w_up[:, :width]) + small(0))
    resid_ref[...] = resid
    hat, _ = norm_parts(resid)
    normed = hat * small(1) + small(2)
    low = normed.astype(BF)
    for at in range(0, hidden, width):
        span = slice(at, at + width)
        values = dot(low, w_up[:, at + width : at + 2 * width]) + up_bias_ref[:, span]
        active, slope = gelu_and_slope(values)
        active_scr[:, span] = active.astype(BF)
        slope_ref[:, span] = slope.astype(BF)

    @pl.when(step == 0)
    def _():
        wait_copies(down_copies)

    final = normed + dot(active_scr[...], w_down[...]) + small(3)
    hat, scale = norm_parts(final)
    out_ref[...] = (hat * small(4) + small(5)).astype(BF)
    cot = cot_ref[...].astype(F32)
    dfinal = norm_back(cot * small(4), hat, scale)
    dfinal_ref[...] = dfinal
    dbranch = dfinal.astype(BF)
    for at in range(0, hidden, width):
        total[at : at + width, :] += tdot(active_scr[:, at : at + width], dbranch)
    add_rows(sums_ref, (cot * hat, cot, dbranch))

    @pl.when(step == pl.num_programs(0) - 1)
    def _():
        places = ((1, send_ref), (3, send_far_ref), (2, keep_ref.at[1]), (0, keep_ref.at[0]))
        wait_copies(store_rows(index, total, places, stage, out_sems))


def forward(index, up_parts, down_parts, mixed, tokens, cotangent, smalls, up_bias, block=256):
    rows, width = tokens.shape
    hidden = up_bias.shape[1]
    spec = lambda columns: pl.BlockSpec((block, columns), lambda i: (i, 0))
    pairs = pl.BlockSpec((PAIRS, block, 128), lambda i: (0, i, 0))
    sums = struct((8, width), F32)
    down_rows = [struct((2, hidden // 4, width), BF)] + [struct((hidden // 4, width), BF)] * 2
    return pl.pallas_call(
        forward_kernel,
        grid=(rows // block,),
        in_specs=[SMEM]
        + [ANY] * (2 * BIG_PARTS)
        + [pairs, spec(width), spec(width), whole(smalls), whole(up_bias)],
        out_specs=[spec(width), spec(width), spec(width), spec(hidden), whole(sums)] + [ANY] * 3,
        out_shape=[
            struct((rows, width), BF),
            struct((rows, width), F32),
            struct((rows, width), F32),
            struct((rows, hidden), BF),
            sums,
        ]
        + down_rows,
        scratch_shapes=[
            pltpu.VMEM((width, width + hidden), BF),
            pltpu.VMEM((hidden, width), BF),
            pltpu.VMEM((hidden, width), F32),
            pltpu.VMEM((block, hidden), BF),
            pltpu.VMEM((4, hidden // 4, width), BF),
            pltpu.SemaphoreType.DMA((2, BIG_PARTS)),
            pltpu.SemaphoreType.DMA((4,)),
        ],
        compiler_params=params(),
        cost_estimate=cost(2 * rows * width * (width + 3 * hidden), 40e6),
        name="forward",
    )(index, *up_parts, *down_parts, mixed, tokens, cotangent, smalls, up_bias)


def backward_kernel(index, *refs):
    up_parts, down_parts = refs[:BIG_PARTS], refs[BIG_PARTS : 2 * BIG_PARTS]
    (
        dfinal_ref, resid_ref, slope_ref, mixed_ref, small_ref,
        dresid_ref, dmixed_ref, sums_ref, up_sums_ref, *row_refs,
        w_up, w_down, total, stage, sems, out_sems,
    ) = refs[2 * BIG_PARTS :]
    step = pl.program_id(0)

    down_copies = fetch_copies(index, down_parts, w_down, sems.at[0], QUARTERS)
    up_copies = fetch_copies(index, up_parts, w_up, sems.at[1])

    @pl.when(step == 0)
    def _():
        start_copies(down_copies)
        start_copies(up_copies)
        for ref in (sums_ref, up_sums_ref, total):
            ref[...] = jnp.zeros_like(ref)
        wait_copies(down_copies)

    width, hidden = w_down.shape[1], w_down.shape[0]
    small = lambda at: small_ref[at + 2 : at + 3, :]
    hat, scale = norm_parts(resid_ref[...])
    low_t = (hat * small(1) + small(2)).astype(BF).T
    dnormed = dfinal_ref[...]
    dbranch = dnormed.astype(BF)
    for at in range(0, hidden, width):
        span = slice(at, at + width)
        up_span = slice(at + width, at + 2 * width)
        dactive = dot_t(dbranch, w_down[span, :])
        dhidden = (dactive * slope_ref[:, span].astype(F32)).astype(BF)
        up_sums_ref[:, span] += jnp.sum(dhidden.astype(F32), axis=0, keepdims=True)
        total[:, up_span] += dot(low_t, dhidden)
        if at == 0:

            @pl.when(step == 0)
            def _():
                wait_copies(up_copies)

        dnormed = dnormed + dot_t(dhidden, w_up[:, up_span])
    dresid = norm_back(dnormed * small(1), hat, scale)
    dresid_ref[...] = dresid
    dattn = dresid.astype(BF)
    dmixed = dot_t(dattn, w_up[:, :width]).astype(BF)
    for pair in range(PAIRS):
        dmixed_ref[pair] = dmixed[:, pair * 128 : pair * 128 + 128]
    total[:, :width] += tdot(join(mixed_ref), dattn)
    add_rows(sums_ref, (dnormed * hat, dnormed, dattn))

    @pl.when(step == pl.num_programs(0) - 1)
    def _():
        half = (width + hidden) // 2
        for at in range(2):
            columns = slice(at * half, at * half + half)
            keep, send = row_refs[2 * at : 2 * at + 2]
            places = ((1, send.at[0]), (3, send.at[1]), (2, keep.at[1]), (0, keep.at[0]))
            staged = stage.at[:, :, columns]
            wait_copies(store_rows(index, total.at[:, columns], places, staged, out_sems))


def backward(index, up_parts, down_parts, dfinal, resid, slope, mixed, smalls, block=256):
    rows, width = resid.shape
    hidden = slope.shape[1]
    spec = lambda columns: pl.BlockSpec((block, columns), lambda i: (i, 0))
    pairs = pl.BlockSpec((PAIRS, block, 128), lambda i: (0, i, 0))
    sums = [struct((8, width), F32), struct((1, hidden), F32)]
    up_rows = struct((2, width // 4, (width + hidden) // 2), BF)
    return pl.pallas_call(
        backward_kernel,
        grid=(rows // block,),
        in_specs=[SMEM]
        + [ANY] * (2 * BIG_PARTS)
        + [spec(width), spec(width), spec(hidden), pairs, whole(smalls)],
        out_specs=[spec(width), pairs] + [whole(shape) for shape in sums] + [ANY] * 4,
        out_shape=[struct((rows, width), F32), struct((PAIRS, rows, 128), BF)]
        + sums
        + [up_rows] * 4,
        scratch_shapes=[
            pltpu.VMEM((width, width + hidden), BF),
            pltpu.VMEM((hidden, width), BF),
            pltpu.VMEM((width, width + hidden), F32),
            pltpu.VMEM((4, width // 4, width + hidden), BF),
            pltpu.SemaphoreType.DMA((2, BIG_PARTS)),
            pltpu.SemaphoreType.DMA((4,)),
        ],
        compiler_params=params(),
        cost_estimate=cost(4 * rows * width * (width + 2 * hidden), 40e6),
        name="backward",
    )(index, *up_parts, *down_parts, dfinal, resid, slope, mixed, smalls)


def place_rows(index, total, keep_ref, send_ref):
    me, shard = index[0], keep_ref.shape[1]
    for at, ref in ((0, keep_ref), (2, keep_ref), (1, send_ref), (3, send_ref)):
        rows = pl.ds(pl.multiple_of((me ^ at) * shard, 16), shard)
        ref[at // 2] = total[rows, :].astype(BF)


def small_rows(refs, places, sums_one, sums_two, up_sums, rows, sums):
    width = rows.shape[1]
    shard = width // 4
    rows[...] = jnp.zeros_like(rows)
    sums[...] = jnp.zeros_like(sums)
    pair, head = 0, 0
    for bias, far, near in refs:
        for at in range(bias.shape[0]):
            rows[0:2, pair * 128 : pair * 128 + 128] = bias[at, 0:2, :]
            pair += 1
        for at in range(far.shape[0]):
            parts = [far[at, row : row + 1, :] for row in range(3)] + [near[at, 0:1, :]]
            sums[head : head + 1, :] = jnp.concatenate(parts, axis=1)
            head += 1
    for row, source in enumerate((2, 0, 1)):
        rows[row + 2 : row + 3, :] = sums_one[source : source + 1, :]
        rows[row + 5 : row + 6, :] = sums_two[source : source + 1, :]
    lane = iota((1, width), 1)
    for at in range(4):
        values = up_sums[:, at * width : at * width + width]
        inside = (lane >= at * shard) & (lane < (at + 1) * shard)
        for part in range(4):
            rolled = pltpu.roll(values, (at - part) % 4 * shard, 1)
            rows[8 + part : 9 + part, :] += jnp.where(inside, rolled, 0.0)
    pick = as_bf(places[...] == iota((LANES, 128), 1))
    table = sum(dot(part, pick) for part in split3(sums[...]))
    table = jnp.concatenate([table, jnp.zeros((table.shape[0], width - 128), F32)], axis=1)
    for at in range(HEADS):
        within = at % 3
        shift = at // 3 * shard + within % 2 * 96
        rolled = pltpu.roll(table[at : at + 1], shift, 1)
        rows[12 + within // 2 : 13 + within // 2, :] += rolled


def small_kernel(count, index, *refs):
    groups, refs = refs[: 3 * count], refs[3 * count :]
    (
        places, sums_one, sums_two, up_sums, keep_in, send_in, keep_ref, send_ref, total, rows, sums
    ) = refs
    del keep_in, send_in
    groups = [groups[at : at + 3] for at in range(0, 3 * count, 3)]
    small_rows(groups, places, sums_one, sums_two, up_sums, rows, sums)
    total[...] = rows[...].T
    place_rows(index, total, keep_ref, send_ref)


def small_gradients(index, groups, sums_one, sums_two, up_sums, keep, send):
    width = sums_one.shape[1]
    block = keep.shape[2] // 128 - 1
    arrays = [array for group in groups for array in group]
    arrays += [jnp.asarray(diagonal_places()), sums_one, sums_two, up_sums]
    out = pl.BlockSpec((2, width // 4, 128), lambda i: (0, 0, block))
    return pl.pallas_call(
        functools.partial(small_kernel, len(groups)),
        grid=(1,),
        in_specs=[SMEM] + [whole(array) for array in arrays] + [ANY, ANY],
        out_specs=[out, out],
        out_shape=[struct(keep.shape, BF)] * 2,
        input_output_aliases={len(arrays) + 1: 0, len(arrays) + 2: 1},
        scratch_shapes=[
            pltpu.VMEM((width, 128), F32),
            pltpu.VMEM((128, width), F32),
            pltpu.VMEM((16, LANES), F32),
        ],
        compiler_params=params(),
        cost_estimate=cost(1e7, 1e6),
        name="small_gradients",
    )(index, *arrays, keep, send)


def unpack_kernel(factor, index, *refs):
    halves, (query_ref, key_ref, value_ref) = refs[:4], refs[4:7]
    *vector_refs, up_bias_ref, table_ref, small_scr = refs[7:]
    half = halves[0].shape[0]
    for at in range(2):
        rows = pl.ds(pl.multiple_of((index[1] ^ at) * half, 16), half)
        first = 0
        for ref in (halves[at], halves[2 + at]):
            for column in range(0, ref.shape[1] // 384 * 384, 384):
                for which, out in enumerate((query_ref, key_ref, value_ref)):
                    place = column + which * 128
                    values = ref[:, place : place + 128].astype(F32) * factor
                    out[rows, first : first + 128] = values
                first += 128
        values = halves[2 + at][:, halves[2].shape[1] - 128 :]
        small_scr[rows, :] = values.astype(F32) * factor
    rows = small_scr[...].T
    for at, ref in enumerate(vector_refs):
        ref[...] = rows[at]
    up_bias_ref[...] = jnp.concatenate([rows[8 + at] for at in range(4)])
    table = jnp.concatenate([rows[12:13, :96], rows[12:13, 96:192], rows[13:14, :96]], axis=0)
    table_ref[...] = table


def unpack(index, early, late, factor):
    half, width = early[0].shape[0], PAIRS * 128
    arrays = [*early, *late]
    outs = [struct((2 * half, width), F32)] * 3 + [struct((2 * half,), F32)] * 8
    outs += [struct((8 * half,), F32), struct((HEADS // 4, 3 * BUCKETS), F32)]
    return pl.pallas_call(
        functools.partial(unpack_kernel, factor),
        grid=(1,),
        in_specs=[SMEM] + [whole(array) for array in arrays],
        out_specs=[whole(shape) for shape in outs],
        out_shape=outs,
        scratch_shapes=[pltpu.VMEM((2 * half, 128), F32)],
        compiler_params=params(),
        cost_estimate=cost(1e6, 3e6),
        name="unpack",
    )(index, *arrays)


def on_device(
    tokens,
    layout_cells,
    pad_mask,
    query_weight,
    key_weight,
    value_weight,
    out_weight,
    query_bias,
    value_bias,
    out_bias,
    bias_table,
    first_gain,
    first_shift,
    up_weight,
    up_bias,
    down_weight,
    down_bias,
    second_gain,
    second_shift,
    cotangent,
):
    rows, width = tokens.shape
    hidden = down_weight.shape[0] * 4
    shard = width // 4
    me = lax.axis_index("fsdp")
    parity = lax.axis_index("dp") & 1
    beside = (lax.axis_index("dp") >> 1) & 1
    index = jnp.stack([me, parity, beside]).astype(jnp.int32)
    factor = 1.0 / math.sqrt(rows * lax.axis_size("dp") * lax.axis_size("fsdp"))

    vectors = (
        query_bias, value_bias, out_bias, first_gain, first_shift, down_bias, second_gain,
        second_shift,
    )
    pack = pack_vectors(vectors, up_bias, bias_table)
    chain = lambda *args: Chain(send_once(*args))

    side = jnp.concatenate
    packs = [chain(pack, "fsdp", bit) for bit in (1, 2, 3)]
    third, piece = shard // 3, shard // 4
    qkv_shard, *qkv_thirds = side_by_side(
        index, (query_weight, key_weight, value_weight), third, ((0, third), (2 * third, 0))
    )

    def cores_of(chains):
        return [chain(part, "fsdp", 1) for far in chains for part in far.result]

    def parts_of(shard, core, chains, cores):
        parts = [shard, core.result]
        for at, far in enumerate(chains):
            parts += [*far.result, *(c.result for c in cores[2 * at : 2 * at + 2])]
        return parts

    out_weight, up_weight, qkv_thirds = together(out_weight, up_weight, qkv_thirds)
    qkv_far = Chain(gather_far(qkv_thirds[0], 1))
    qkv_direct = chain(qkv_thirds[1], "fsdp", 2)
    up_shard, *up_pieces = side_by_side(
        index, (out_weight, up_weight), piece, ((0, 2 * piece), (piece, 2 * piece))
    )
    up_far = [Chain(gather_far(half, 1)) for half in up_pieces]
    down_far = Chain(gather_far(half_of(half_of(down_weight, beside), parity), 1))
    qkv_core, up_core, down_core = (
        chain(shard, "fsdp", 1) for shard in (qkv_shard, up_shard, down_weight)
    )
    run(None, (), [qkv_far, *packs, qkv_direct, qkv_core], [qkv_far, *packs])
    w, own, ke, oh, near_t, smalls, full_up_bias = run(
        lambda *a: prepare(index, *a),
        ((pack, *(p.result for p in packs)), layout_cells, pad_mask),
        [qkv_far, down_far],
        [qkv_far, qkv_direct, qkv_core],
    )
    thirds = [*qkv_far.result, qkv_direct.result]
    qkv_cores = [chain(part, "fsdp", 1) for part in thirds]
    run(None, (), qkv_cores, [*qkv_cores, down_far])
    qkv_parts = [qkv_shard, qkv_core.result, *thirds, *(c.result for c in qkv_cores)]
    qkv, tokens_t = run(
        lambda *a: project(index, *a),
        (qkv_parts, tokens, smalls),
        [up_far[0], down_far, up_core, down_core],
    )
    quarters = list(down_far.result)
    line = [chain(quarter, "dp", 2) for quarter in quarters]
    cores = [chain(quarter, "fsdp", 1) for quarter in quarters]
    old = run(
        lambda *a: attend(FORWARD_GROUPS[0], *a),
        (qkv, w, own, ke, near_t),
        [up_far[1], up_far[0], line[0], *cores],
    )
    up_cores = cores_of(up_far[:1])
    cores.append(chain(line[0].result, "fsdp", 1))
    mixed, lse = run(
        lambda *a: attend(FORWARD_GROUPS[1], *a),
        (qkv, w, own, ke, near_t, old),
        [up_far[1], line[1], *up_cores, cores[2]],
    )
    up_cores += cores_of(up_far[1:])
    cores.append(chain(line[1].result, "fsdp", 1))
    run(None, (), [*up_cores[2:], cores[3]])
    up_parts = parts_of(up_shard, up_core, up_far, up_cores)
    quarters += [c.result for c in line]
    down_parts = [down_weight, down_core.result, *quarters, *(c.result for c in cores)]
    result, dfinal, resid, slope, sums_two, *down_rows = run(
        lambda *a: forward(index, up_parts, down_parts, *a),
        (mixed, tokens, cotangent, smalls, full_up_bias),
    )

    down_keep, down_own, down_far = down_rows
    own_core = chain(down_own, "fsdp", 1)
    down_sum = Chain(reduce_steps(down_keep, down_far, own=own_core))
    run(None, (), [down_sum])
    dresid, dmixed, sums_one, up_sums, *up_rows = run(
        lambda *a: backward(index, up_parts, down_parts, *a),
        (dfinal, resid, slope, mixed, smalls),
        [own_core, down_sum],
    )
    first_sum = Chain(reduce_steps(*up_rows[:2]))
    second_sum = Chain(reduce_steps(*up_rows[2:], line_first=True))
    run(None, (), [first_sum, second_sum])

    def back(at, room, begin, finish, old=()):
        return run(
            lambda *a: attend_back(GROUPS[at], room, index, *a),
            (qkv, w, own, ke, oh, near_t, dmixed, mixed, lse, tokens_t, old),
            begin,
            finish,
        )

    columns = 384 * (GROUPS[0][1] + GROUPS[1][1])
    three = [first_sum, second_sum, down_sum]
    backs = [back(0, columns, three, three)]
    backs.append(back(1, columns, three, three, tuple(backs[0][6:])))
    early_sum = Chain(reduce_steps(*backs[1][6:]))
    run(None, (), [early_sum])
    room = 3 * width + 128 - columns
    backs.append(back(2, room, [early_sum, *three], [early_sum, *three]))
    late_rows = run(
        lambda *a: small_gradients(index, *a),
        ([group[3:6] for group in backs], sums_one, sums_two, up_sums, *backs[2][6:]),
    )
    late_sum = Chain(reduce_steps(*late_rows))
    run(None, (), [late_sum])
    input_grad = run(
        lambda *a: input_gradient(index, qkv_parts, *a),
        ([array for group in backs for array in group[:3]], dresid),
        [late_sum, early_sum, second_sum, down_sum, first_sum],
        [late_sum, early_sum, second_sum, down_sum],
    )
    run(None, (), [late_sum, early_sum], [])
    run(None, (), [], [first_sum])
    run(None, (), [], [late_sum, early_sum])
    chains = [late_sum, early_sum, second_sum, first_sum, down_sum]
    rest = chains[2:]
    while any(c.move is not None for c in rest):
        left = [c for c in chains if c.move is not None]
        for c in left:
            run(None, (), [c], [])
            if c is second_sum and down_sum.move is not None:
                moved, _ = together([down_sum.move[0]], [second_sum.flight])
                down_sum.move = (moved[0], *down_sum.move[1:])
        for c in left:
            run(None, (), [], [c])
    ordered = [in_order(*c.result).astype(F32) * factor for c in (down_sum, first_sum, second_sum)]
    grad_down, grad_out = ordered[0], ordered[1][:, :width]
    grad_up = side([ordered[1][:, width:], ordered[2]], axis=1)
    ready = (grad_down,)
    while any(c.move is not None for c in chains[:2]):
        left = [c for c in chains[:2] if c.move is not None]
        for c in left:
            run(None, (), [c], [])
        for c in left:
            ready, (arrived,) = together(ready, [c.flight])
            c.advance(arrived)
    (grad_down,) = ready
    *grad_qkv, tail_up, tail_table = unpack(index, early_sum.result[:2], late_sum.result[:2], factor)
    grad_qkv, tail = grad_qkv[:3], grad_qkv[3:]
    return (
        result,
        input_grad,
        *grad_qkv,
        grad_out,
        tail[0],
        tail[1],
        tail[2],
        tail_table,
        tail[3],
        tail[4],
        grad_up,
        tail_up,
        grad_down,
        tail[5],
        tail[6],
        tail[7],
    )


def solution(mesh):
    rows = P(("dp", "fsdp"), None)
    matrix, vector = P("fsdp", None), P("fsdp")
    return jax.shard_map(
        on_device,
        mesh=mesh,
        in_specs=(
            rows, P(None, ("dp", "fsdp")), P(("dp", "fsdp")),
            matrix, matrix, matrix, matrix,
            vector, vector, vector, matrix, vector, vector,
            matrix, vector, matrix, vector, vector, vector,
            rows,
        ),
        out_specs=(
            rows, rows,
            matrix, matrix, matrix, matrix,
            vector, vector, vector, matrix, vector, vector,
            matrix, vector, matrix, vector, vector, vector,
        ),
        check_vma=False,
    )
```
